32 devices in a mesh: rep: 2 (over y), dp: 4 (over z), ctx: 4 (over x, core).
Axes of the slice: x: 2, y: 2, z: 4, core: 2. Of those that a mesh axis runs over, the one named last changes fastest.
Arguments:
- tokens: bfloat16 [2, 8, 1024, 2560], P(None, ('rep', 'dp'), 'ctx'), may hold values from -6 to 6
- cotangent: bfloat16 [2, 8, 1024, 2560], P(None, ('rep', 'dp'), 'ctx'), may hold values from -6 to 6
- segments: int32 [2, 8, 1024], P(None, ('rep', 'dp')), may hold values from 0 to 8, as said below
- attn_gain: bfloat16 [2560], P(('dp', 'ctx')), may hold values from 0.099609375 to 1.8984375
- w_query: bfloat16 [2560, 2560], P(('dp', 'ctx')), may hold values from -0.125 to 0.125
- w_key: bfloat16 [2560, 640], P(('dp', 'ctx')), may hold values from -0.125 to 0.125
- w_value: bfloat16 [2560, 640], P(('dp', 'ctx')), may hold values from -0.125 to 0.125
- w_out: bfloat16 [2560, 2560], P(('dp', 'ctx')), may hold values from -0.5 to 0.5
- mlp_gain: bfloat16 [2560], P(('dp', 'ctx')), may hold values from 0.099609375 to 1.8984375
- w_gate: bfloat16 [2560, 6912], P(('dp', 'ctx')), may hold values from -0.125 to 0.125
- w_up: bfloat16 [2560, 6912], P(('dp', 'ctx')), may hold values from -0.125 to 0.125
- w_down: bfloat16 [2560, 6912], P(('dp', 'ctx')), may hold values from -0.078125 to 0.078125
Outputs:
- output: bfloat16 [2, 8, 1024, 2560], P(None, ('rep', 'dp'), 'ctx')
- input_grad: float32 [2, 8, 1024, 2560], P(None, ('rep', 'dp'), 'ctx')
- attn_gain_grad: float32 [2560], P(('dp', 'ctx'))
- query_grad: float32 [2560, 2560], P(('dp', 'ctx'))
- key_grad: float32 [2560, 640], P(('dp', 'ctx'))
- value_grad: float32 [2560, 640], P(('dp', 'ctx'))
- out_grad: float32 [2560, 2560], P(('dp', 'ctx'))
- mlp_gain_grad: float32 [2560], P(('dp', 'ctx'))
- gate_grad: float32 [2560, 6912], P(('dp', 'ctx'))
- up_grad: float32 [2560, 6912], P(('dp', 'ctx'))
- down_grad: float32 [2560, 6912], P(('dp', 'ctx'))
The draws below stay inside these ranges and needn't reach their ends.
Inputs may be any that keep to these rules, and one draw needn't show every extreme that they name: `segments`: within a sequence the ids never fall along pos; document 0 starts at pos 0 and covers more than half of the positions; every sequence has ids 0 to 8.
All inputs are finite; a program needn't handle non-finite values.
Results may differ from the reference program's by a relative error of at most 0.018.
Values may be sent and summed in bfloat16 or wider, within the bound.
A program may use at most 640 MiB of HBM per device.

```python
import math
import jax
import jax.numpy as jnp
from jax import lax

D = 2560
FF = 6912
HEADS = 32
KV_HEADS = 8
HEAD_DIM = 80
MB = 2
LENGTH = 1024
BATCH = 8
N_CTX = 4


def draw_segments(key, part):
    key = jax.random.fold_in(key, 7)
    seq_length = LENGTH
    span_rows = seq_length // N_CTX
    half_rows = span_rows // 2
    stored_index = jnp.arange(seq_length, dtype=jnp.int32)
    device_of = stored_index // span_rows
    within_rows = stored_index % span_rows
    block_of = jnp.where(within_rows < half_rows, device_of, 2 * N_CTX - 1 - device_of)
    true_places = block_of * half_rows + within_rows % half_rows
    seq_count = MB * BATCH
    first_key, gap_key = jax.random.split(key)
    first_end = seq_length // 2 + 1 + jax.random.randint(first_key, (seq_count, 1), 0, seq_length // 8)
    gap_range = 3 * seq_length // 64 - 1
    uniform_ints = jax.random.randint(gap_key, (seq_count, 7), 0, gap_range)
    gap_sizes = 1 + uniform_ints * uniform_ints * uniform_ints // (gap_range * gap_range)
    doc_bounds = jnp.concatenate([first_end, first_end + jnp.cumsum(gap_sizes, axis=1)], axis=1)
    segment_ids = jnp.sum((true_places[None, :, None] >= doc_bounds[:, None, :]).astype(jnp.int32), axis=2)
    return segment_ids.reshape(MB, BATCH, seq_length).astype(jnp.int32)


def steps_of(own_key, extent, cuts, smallest, largest):
    factor_of = 1.0
    for dim, shards_of in cuts:
        draws = jax.random.uniform(jax.random.fold_in(jax.random.fold_in(own_key, 6), dim), (shards_of,), jnp.float32, smallest / len(cuts), largest / len(cuts))
        factor_of = factor_of * jnp.repeat(jnp.exp(draws), extent[dim] // shards_of).reshape((-1,) + (1,) * (len(extent) - 1 - dim))
    return factor_of


def normal_values(rng, dims, width, bound, cuts=(), held_as=jnp.bfloat16):
    entries = width * jax.random.normal(rng, dims, jnp.float32)
    if cuts:
        entries = entries * steps_of(rng, dims, cuts, -0.22, 0.18)
    return jnp.clip(entries, -bound, bound).astype(held_as)


def setup_inputs(seed: int = 0) -> dict:
    splits = jax.random.split(jax.random.key(seed), 13)
    tokens = normal_values(splits[0], (MB, BATCH, LENGTH, D), 1.0, 6.0, ((1, 8), (2, 4)))
    cotangent = normal_values(splits[1], (MB, BATCH, LENGTH, D), 1.0, 6.0, ((1, 8), (2, 4)))
    segments = draw_segments(jax.random.fold_in(splits[12], 71), 0)
    attn_gain = jnp.clip(1.0 + 0.18 * jax.random.normal(splits[3], (D,), jnp.float32), 0.099609375, 1.8984375).astype(jnp.bfloat16)
    w_query = normal_values(splits[4], (D, HEADS * HEAD_DIM), D ** -0.5, 0.125, ((0, 16),))
    w_key = normal_values(splits[5], (D, KV_HEADS * HEAD_DIM), D ** -0.5, 0.125, ((0, 16),))
    w_value = normal_values(splits[6], (D, KV_HEADS * HEAD_DIM), D ** -0.5, 0.125, ((0, 16),))
    w_out = normal_values(splits[7], (D, HEADS * HEAD_DIM), (HEADS * HEAD_DIM // 16) ** -0.5, 0.5, ((0, 16),))
    mlp_gain = jnp.clip(1.0 + 0.18 * jax.random.normal(splits[8], (D,), jnp.float32), 0.099609375, 1.8984375).astype(jnp.bfloat16)
    w_gate = normal_values(splits[9], (D, FF), D ** -0.5, 0.125, ((0, 16),))
    w_up = normal_values(splits[10], (D, FF), D ** -0.5, 0.125, ((0, 16),))
    w_down = normal_values(splits[11], (D, FF), FF ** -0.5, 0.078125, ((0, 16),))
    return {"tokens": tokens, "cotangent": cotangent, "segments": segments, "attn_gain": attn_gain, "w_query": w_query, "w_key": w_key, "w_value": w_value, "w_out": w_out, "mlp_gain": mlp_gain, "w_gate": w_gate, "w_up": w_up, "w_down": w_down}


@jax.custom_vjp
def low(v):
    return lax.optimization_barrier(v.astype(jnp.bfloat16)).astype(jnp.float32)

@jax.custom_vjp
def low_back(v):
    return v

def low_keep(v):
    return (low(v), None)

def low_pass(kept, grad):
    return (grad,)

def back_keep(v):
    return (v, None)

def back_low(kept, grad):
    return (low(grad),)
low.defvjp(low_keep, low_pass)
low_back.defvjp(back_keep, back_low)
rope_base = 10000.0
norm_epsilon = 1e-05
highest_precision = lax.Precision.HIGHEST

def true_positions(seq_length, ctx_parts):
    span_rows = seq_length // ctx_parts
    half_rows = span_rows // 2
    stored_index = jnp.arange(seq_length, dtype=jnp.int32)
    device_of = stored_index // span_rows
    within_rows = stored_index % span_rows
    block_of = jnp.where(within_rows < half_rows, device_of, 2 * ctx_parts - 1 - device_of)
    return (block_of * half_rows + within_rows % half_rows).astype(jnp.int32)

def rotate(values, places, direction):
    half_width = values.shape[-1] // 2
    frequency = rope_base ** (-2.0 * jnp.arange(half_width, dtype=jnp.float32) / values.shape[-1])
    angles = places.astype(jnp.float32)[:, None] * frequency[None, :]
    cosine = jnp.cos(angles)[:, None, :]
    sine = direction * jnp.sin(angles)[:, None, :]
    first_half = values[..., :half_width]
    second_half = values[..., half_width:]
    return jnp.concatenate([first_half * cosine - second_half * sine, second_half * cosine + first_half * sine], axis=-1)

def rms_scale(values):
    return lax.rsqrt(lax.optimization_barrier(jnp.mean(values * values, axis=-1, keepdims=True)) + norm_epsilon)

def matmul(left_side, right_side):
    return jnp.dot(left_side, right_side, precision=highest_precision, preferred_element_type=jnp.float32)

def layer(hidden_in, segment_ids, places, attn_gain, w_query, w_key, w_value, w_out, mlp_gain, w_gate, w_up, w_down):
    seq_length = hidden_in.shape[0]
    group_size = HEADS // KV_HEADS
    normed = low(hidden_in * rms_scale(hidden_in) * attn_gain)
    queries = low(rotate(low_back(matmul(normed, w_query)).reshape(seq_length, HEADS, HEAD_DIM), places, 1.0))
    key_rot = low(rotate(low_back(matmul(normed, w_key)).reshape(seq_length, KV_HEADS, HEAD_DIM), places, 1.0))
    value_heads = low(low_back(matmul(normed, w_value))).reshape(seq_length, KV_HEADS, HEAD_DIM)
    query_groups = queries.reshape(seq_length, KV_HEADS, group_size, HEAD_DIM)
    scores = low_back(jnp.einsum('rkgd,lkd->kgrl', query_groups, key_rot, precision=highest_precision) / math.sqrt(HEAD_DIM))
    visible = (segment_ids[:, None] == segment_ids[None, :]) & (places[None, :] <= places[:, None])
    masked = jnp.where(visible, scores, -1e+30)
    top_score = lax.optimization_barrier(jnp.max(masked, axis=-1, keepdims=True))
    weights_exp = jnp.exp(masked - top_score)
    probabilities = weights_exp / lax.optimization_barrier(jnp.sum(weights_exp, axis=-1, keepdims=True))
    mixed_heads = jnp.einsum('kgrl,lkd->rkgd', low(probabilities), value_heads, precision=highest_precision)
    attended = low(low_back(mixed_heads.reshape(seq_length, HEADS * HEAD_DIM)))
    residual = hidden_in + low_back(matmul(attended, w_out.T))
    normed_mlp = low(residual * rms_scale(residual) * mlp_gain)
    gate_pre = low_back(matmul(normed_mlp, w_gate))
    up_pre = low_back(matmul(normed_mlp, w_up))
    activated = low(jax.nn.silu(gate_pre) * up_pre)
    return residual + low_back(matmul(activated, w_down.T))

def reference(tokens, cotangent, segments, attn_gain, w_query, w_key, w_value, w_out, mlp_gain, w_gate, w_up, w_down):
    seq_length = tokens.shape[2]
    model_width = tokens.shape[3]
    places = true_positions(seq_length, N_CTX)
    flat_inputs = tokens.reshape(-1, seq_length, model_width).astype(jnp.float32)
    flat_cotangent = cotangent.reshape(-1, seq_length, model_width).astype(jnp.float32)
    flat_segments = segments.reshape(-1, seq_length)
    weight_list = tuple((weight_item.astype(jnp.float32) for weight_item in (attn_gain, w_query, w_key, w_value, w_out, mlp_gain, w_gate, w_up, w_down)))

    def one_sequence(totals, items):
        inputs_seq, cotangent_seq, segment_seq = items

        def forward(inputs_arg, *weight_args):
            return layer(inputs_arg, segment_seq, places, *weight_args)
        outputs_seq, pullback = jax.vjp(forward, inputs_seq, *weight_list)
        gradients = pullback(cotangent_seq)
        new_totals = tuple((total_item + grad_item for total_item, grad_item in zip(totals, gradients[1:])))
        return (new_totals, (outputs_seq.astype(jnp.bfloat16), gradients[0]))
    zero_totals = tuple((jnp.zeros(weight_item.shape, jnp.float32) for weight_item in weight_list))
    totals, (outputs_all, input_grads) = lax.scan(one_sequence, zero_totals, (flat_inputs, flat_cotangent, flat_segments))
    return (outputs_all.reshape(tokens.shape), input_grads.reshape(tokens.shape), totals[0], totals[1], totals[2], totals[3], totals[4], totals[5], totals[6], totals[7], totals[8])
```

```python
import functools

import jax
import jax.numpy as jnp
from jax import lax
from jax.experimental import pallas as pl
from jax.experimental.pallas import tpu as pltpu
from jax.sharding import PartitionSpec as P

D = 2560
HEADS = 32
KV_HEADS = 8
HEAD_DIM = 80
GROUP = HEADS // KV_HEADS
HALF = HEAD_DIM // 2
LANES = 128
SHARE = 8
INNER = 4

rope_base = 10000.0
norm_epsilon = 1e-05
log2_e = 1.4426950408889634
bf16 = jnp.bfloat16
f32 = jnp.float32


def round_up(value, unit):
    return -(-value // unit) * unit


def true_positions(seq_length, ctx_parts):
    span_rows = seq_length // ctx_parts
    half_rows = span_rows // 2
    stored_index = jnp.arange(seq_length, dtype=jnp.int32)
    device_of = stored_index // span_rows
    within_rows = stored_index % span_rows
    block_of = jnp.where(within_rows < half_rows, device_of, 2 * ctx_parts - 1 - device_of)
    return block_of * half_rows + within_rows % half_rows


def dot_nn(left, right, out=f32):
    return lax.dot_general(left, right, (((1,), (0,)), ((), ())), preferred_element_type=out)


def dot_nt(left, right, out=f32):
    return lax.dot_general(left, right, (((1,), (1,)), ((), ())), preferred_element_type=out)


def dot_tn(left, right, out=f32):
    return lax.dot_general(left, right, (((0,), (0,)), ((), ())), preferred_element_type=out)


def stack_heads(block):
    return jnp.concatenate(
        [block[:, g * LANES : (g + 1) * LANES] for g in range(GROUP)], axis=0
    )


def bias_of(seg_k, seg_q, first, base):
    rows, cols = seg_k.shape[0], seg_q.shape[1]
    key_pos = first + lax.broadcasted_iota(jnp.int32, (rows, cols), 0)
    query_pos = base + lax.broadcasted_iota(jnp.int32, (rows, cols), 1)
    bias = jnp.where((seg_k == seg_q) & (key_pos <= query_pos), 0.0, -1e30).astype(f32)
    return jnp.concatenate([bias] * GROUP, axis=1)


def forward_kernel(
    chunk, base_ref, q_ref, k_ref, vt_ref, segq_ref, segk_ref, o_ref, lse_ref, s_ref
):
    half_rows = q_ref.shape[2]
    length = k_ref.shape[1]
    base = base_ref[pl.program_id(1)]
    count = (base + half_rows - 1) // chunk + 1
    scale = HEAD_DIM**-0.5 * log2_e

    def run(chunks):
        queries = stack_heads(q_ref[0, 0])
        seg_q = segq_ref[0, 0]
        top = None
        for c in range(chunks):
            at = pl.ds(c * chunk, chunk)
            s = dot_nt(k_ref[0, at], queries) * scale
            s = s + bias_of(segk_ref[0, at], seg_q, c * chunk, base)
            s_ref[at] = s
            now = jnp.max(s, axis=0, keepdims=True)
            top = now if top is None else jnp.maximum(top, now)
        total = None
        mixed = None
        for c in range(chunks):
            at = pl.ds(c * chunk, chunk)
            p = jnp.exp2(s_ref[at] - top)
            now = jnp.sum(p, axis=0, keepdims=True)
            total = now if total is None else total + now
            part = dot_nn(vt_ref[0, :, at], p.astype(bf16))
            mixed = part if mixed is None else mixed + part
        out = (mixed / total).T.astype(bf16)
        for g in range(GROUP):
            o_ref[0, 0, :, g * LANES : (g + 1) * LANES] = out[g * half_rows : (g + 1) * half_rows]
        lse_ref[0, 0] = top + jnp.log2(total)

    for chunks in range(1, length // chunk + 1):
        pl.when(count == chunks)(functools.partial(run, chunks))


def backward_kernel(
    chunk,
    base_ref,
    q_ref,
    k_ref,
    kt_ref,
    v_ref,
    segq_ref,
    segk_ref,
    do_ref,
    lse_ref,
    cos_ref,
    sin_ref,
    dq_ref,
    dk_ref,
    dv_ref,
    p_ref,
    dp_ref,
):
    half_rows = q_ref.shape[2]
    length = k_ref.shape[1]
    base = base_ref[pl.program_id(1)]
    count = (base + half_rows - 1) // chunk + 1
    scale = HEAD_DIM**-0.5

    @pl.when(pl.program_id(1) == 0)
    def _():
        dk_ref[...] = jnp.zeros_like(dk_ref)
        dv_ref[...] = jnp.zeros_like(dv_ref)

    def run(chunks):
        queries = stack_heads(q_ref[0, 0])
        grads = stack_heads(do_ref[0, 0])
        seg_q = segq_ref[0, 0]
        log_total = lse_ref[0, 0]
        inner = None
        for c in range(chunks):
            at = pl.ds(c * chunk, chunk)
            s = dot_nt(k_ref[0, at], queries) * (scale * log2_e)
            s = s + bias_of(segk_ref[0, at], seg_q, c * chunk, base)
            p = jnp.exp2(s - log_total)
            dp = dot_nt(v_ref[0, at], grads)
            dv_ref[0, at] += dot_nn(p.astype(bf16), grads)
            now = jnp.sum(p * dp, axis=0, keepdims=True)
            inner = now if inner is None else inner + now
            p_ref[at] = p
            dp_ref[at] = dp
        dq = None
        for c in range(chunks):
            at = pl.ds(c * chunk, chunk)
            ds = (p_ref[at] * (dp_ref[at] - inner)).astype(bf16)
            dk_ref[0, at] += dot_nn(ds, queries) * scale
            part = dot_nn(kt_ref[0, :, at], ds)
            dq = part if dq is None else dq + part
        dq = (dq * scale).T
        cosine, sine = cos_ref[0], sin_ref[0]
        for g in range(GROUP):
            one = dq[g * half_rows : (g + 1) * half_rows]
            turned = one * cosine - pltpu.roll(one, LANES // 2, 1) * sine
            dq_ref[0, 0, :, g * LANES : (g + 1) * LANES] = turned.astype(bf16)

    for chunks in range(1, length // chunk + 1):
        pl.when(count == chunks)(functools.partial(run, chunks))


def attention_specs(half_rows, length):
    wide = GROUP * LANES
    query = pl.BlockSpec((1, 1, half_rows, wide), lambda s, j, *_: (s, j, 0, 0))
    keys = pl.BlockSpec((1, length, LANES), lambda s, j, *_: (s, 0, 0))
    keys_t = pl.BlockSpec((1, LANES, length), lambda s, j, *_: (s, 0, 0))
    seg_q = pl.BlockSpec((1, 1, 1, half_rows), lambda s, j, *_: (s, j, 0, 0))
    seg_k = pl.BlockSpec((1, length, 1), lambda s, j, *_: (s, 0, 0))
    lse = pl.BlockSpec((1, 1, 1, GROUP * half_rows), lambda s, j, *_: (s, j, 0, 0))
    table = pl.BlockSpec((1, half_rows, LANES), lambda s, j, *_: (j, 0, 0))
    return query, keys, keys_t, seg_q, seg_k, lse, table


def attention_cost(seqs, subs, half_rows, length, products):
    pairs = seqs * subs * half_rows * length * GROUP
    return pl.CostEstimate(
        flops=pairs * LANES * 2 * products * 5 // 8,
        transcendentals=pairs * 5 // 8,
        bytes_accessed=seqs * (subs * half_rows * GROUP + length) * LANES * 2 * products,
    )


def attend(bases, queries, k, vt, seg_q, seg_k):
    seqs, subs, half_rows, _ = queries.shape
    length = k.shape[1]
    chunk = 256
    query, keys, keys_t, sq, sk, lse, _ = attention_specs(half_rows, length)
    return pl.pallas_call(
        functools.partial(forward_kernel, chunk),
        grid_spec=pltpu.PrefetchScalarGridSpec(
            num_scalar_prefetch=1,
            grid=(seqs, subs),
            in_specs=[query, keys, keys_t, sq, sk],
            out_specs=[query, lse],
            scratch_shapes=[pltpu.VMEM((length, GROUP * half_rows), f32)],
        ),
        out_shape=[
            jax.ShapeDtypeStruct((seqs, subs, half_rows, GROUP * LANES), bf16),
            jax.ShapeDtypeStruct((seqs, subs, 1, GROUP * half_rows), f32),
        ],
        compiler_params=pltpu.CompilerParams(vmem_limit_bytes=48 << 20),
        cost_estimate=attention_cost(seqs, subs, half_rows, length, 2),
    )(bases, queries, k, vt, seg_q, seg_k)


def attend_back(bases, queries, k, kt, v, seg_q, seg_k, grads, lse_in, cosine, sine):
    seqs, subs, half_rows, _ = queries.shape
    length = k.shape[1]
    chunk = 256
    query, keys, keys_t, sq, sk, lse, table = attention_specs(half_rows, length)
    return pl.pallas_call(
        functools.partial(backward_kernel, chunk),
        grid_spec=pltpu.PrefetchScalarGridSpec(
            num_scalar_prefetch=1,
            grid=(seqs, subs),
            in_specs=[query, keys, keys_t, keys, sq, sk, query, lse, table, table],
            out_specs=[query, keys, keys],
            scratch_shapes=[pltpu.VMEM((length, GROUP * half_rows), f32)] * 2,
        ),
        out_shape=[
            jax.ShapeDtypeStruct((seqs, subs, half_rows, GROUP * LANES), bf16),
            jax.ShapeDtypeStruct((seqs, length, LANES), f32),
            jax.ShapeDtypeStruct((seqs, length, LANES), f32),
        ],
        compiler_params=pltpu.CompilerParams(vmem_limit_bytes=48 << 20),
        cost_estimate=attention_cost(seqs, subs, half_rows, length, 5),
    )(bases, queries, k, kt, v, seg_q, seg_k, grads, lse_in, cosine, sine)


def project_kernel(x_ref, w_ref, cos_ref, sin_ref, out_ref):
    product = dot_nn(x_ref[...], w_ref[...])
    cosine, sine = cos_ref[...], sin_ref[...]
    for g in range(GROUP + 1):
        at = slice(g * LANES, (g + 1) * LANES)
        one = product[:, at]
        out_ref[:, at] = (one * cosine + pltpu.roll(one, LANES // 2, 1) * sine).astype(bf16)
    at = slice((GROUP + 1) * LANES, (GROUP + 2) * LANES)
    out_ref[:, at] = product[:, at].astype(bf16)


def project(x, w, cosine, sine, tile):
    rows = x.shape[0]
    cols = w.shape[1]
    repeat = cosine.shape[0] // tile
    return pl.pallas_call(
        project_kernel,
        grid=(rows // tile,),
        in_specs=[
            pl.BlockSpec((tile, x.shape[1]), lambda i: (i, 0)),
            pl.BlockSpec(w.shape, lambda i: (0, 0)),
            pl.BlockSpec((tile, LANES), lambda i: (i % repeat, 0)),
            pl.BlockSpec((tile, LANES), lambda i: (i % repeat, 0)),
        ],
        out_specs=pl.BlockSpec((tile, cols), lambda i: (i, 0)),
        out_shape=jax.ShapeDtypeStruct((rows, cols), bf16),
        compiler_params=pltpu.CompilerParams(vmem_limit_bytes=48 << 20),
        cost_estimate=pl.CostEstimate(
            flops=2 * rows * x.shape[1] * cols,
            transcendentals=0,
            bytes_accessed=2 * (rows * x.shape[1] + rows * cols + w.size),
        ),
    )(x, w, cosine, sine)


class Place:
    def __init__(self):
        self.reps = lax.axis_size("rep")
        self.parts = lax.axis_size("dp")
        self.ctx = lax.axis_size("ctx")
        self.outer = self.ctx // INNER
        self.rep = lax.axis_index("rep")
        self.part = lax.axis_index("dp")
        ctx = lax.axis_index("ctx")
        self.inner = ctx % INNER
        self.hi = ctx // INNER
        self.core = self.inner % 2
        self.mid = self.inner // 2

    def flip(self, a, bits):
        return lax.ppermute(a, "ctx", [(i, i ^ bits) for i in range(self.ctx)])

    def swap_rep(self, a):
        return lax.ppermute(a, "rep", [(0, 1), (1, 0)])

    def shift_hi(self, a, by):
        pairs = [(i, (i + INNER * by) % self.ctx) for i in range(self.ctx)]
        return lax.ppermute(a, "ctx", pairs)


    def gather_rows(self, piece):
        n = self.parts
        right, left = [piece], [piece]
        for s in range(1, n):
            right.append(
                lax.ppermute(right[-1], "dp", [(i, i + 1) for i in range(s - 1, n - 1)])
            )
            left.append(lax.ppermute(left[-1], "dp", [(i, i - 1) for i in range(1, n - s + 1)]))
        slots = [piece]
        for s in range(1, n):
            slots.append(jnp.where(self.part >= s, right[s], left[n - s]))
        whole = jnp.concatenate(slots, axis=0)
        if self.outer > 1:
            whole = jnp.concatenate(
                [whole] + [self.shift_hi(whole, j) for j in range(1, self.outer)], axis=0
            )
        return whole

    def reduce_rows(self, whole, kind=bf16):
        n = self.parts
        rows = whole.shape[0] // (n * self.outer)
        whole = whole.reshape((self.outer, n * rows) + whole.shape[1:])
        mine = whole[0]
        for j in range(1, self.outer):
            mine = mine + self.shift_hi(whole[j], -j)
        own = [mine[s * rows : (s + 1) * rows] for s in range(n)]
        right = left = None
        for t in range(1, n):
            going_right = own[t] if right is None else own[t] + right
            going_left = own[n - t] if left is None else own[n - t] + left
            right = lax.ppermute(going_right, "dp", [(i, i + 1) for i in range(t)])
            left = lax.ppermute(going_left, "dp", [(i, i - 1) for i in range(n - t, n)])
        return own[0].astype(f32) + right.astype(f32) + left.astype(f32)

    def gather_inner(self, by_slice):
        got = jnp.zeros((INNER,) + by_slice.shape[1:], by_slice.dtype)
        for j in range(INNER):
            one = lax.dynamic_index_in_dim(
                by_slice, self.rep * INNER + (self.inner ^ j), 0, keepdims=False
            )
            one = self.flip(one, j) if j else one
            got = lax.dynamic_update_index_in_dim(got, one, self.inner ^ j, 0)
        return got.reshape((-1,) + by_slice.shape[2:])

    def scatter_inner(self, rows_in):
        pieces = []
        for j in range(INNER):
            one = lax.dynamic_index_in_dim(rows_in, self.inner ^ j, 0, keepdims=False)
            pieces.append(self.flip(one, j) if j else one)
        natural = []
        for c in range(INNER):
            pick = pieces[0]
            for j in range(1, INNER):
                pick = jnp.where(self.inner ^ j == c, pieces[j], pick)
            natural.append(pick)
        mine = jnp.stack(natural)
        other = self.swap_rep(mine)
        low = jnp.where(self.rep == 0, mine, other)
        high = jnp.where(self.rep == 0, other, mine)
        return jnp.concatenate([low, high], axis=0)


    def to_own_order(self, a):
        n, outer = self.parts, self.outer
        width = a.shape[-1] // (n * outer)
        cut = []
        for j in range(outer):
            for s in range(n):
                block = ((self.part - s) % n) * outer + (self.hi - j) % outer
                cut.append(lax.dynamic_slice_in_dim(a, block * width, width, a.ndim - 1))
        return jnp.concatenate(cut, axis=-1)

    def to_natural_order(self, a):
        n, outer = self.parts, self.outer
        width = a.shape[-1] // (n * outer)
        cut = []
        for part in range(n):
            for hi in range(outer):
                block = ((self.hi - hi) % outer) * n + (self.part - part) % n
                cut.append(lax.dynamic_slice_in_dim(a, block * width, width, a.ndim - 1))
        return jnp.concatenate(cut, axis=-1)


    def gather_plane(self, a, prepare=lambda block: block):
        half = a.shape[0] // 2
        by_rep = self.swap_rep(a)
        by_mid = self.flip(a, 2)
        first = self.flip(by_rep[:half], 2)
        second = self.swap_rep(by_mid[half:])
        diagonal = jnp.concatenate([first, second], axis=0)
        got = jnp.zeros((2, INNER) + a.shape, bf16)
        for r, m, block in ((0, 0, a), (0, 1, by_mid), (1, 0, by_rep), (1, 1, diagonal)):
            for k in range(2):
                one = prepare(self.flip(block, 1) if k else block)
                start = (r, self.inner ^ (2 * m + k), 0, 0)
                got = lax.dynamic_update_slice(got, one[None, None], start)
        return got

    def reduce_plane(self, partial):
        _, _, rows, width = partial.shape
        half = rows // 2
        split = partial.reshape(2, 2, 2, rows, width)
        keep = lax.dynamic_index_in_dim(split, self.core, 2, keepdims=False)
        give = lax.dynamic_index_in_dim(split, 1 - self.core, 2, keepdims=False)
        pair = (keep.astype(f32) + self.flip(give, 1).astype(f32)).astype(bf16)
        near = lax.dynamic_index_in_dim(pair, self.mid, 1, keepdims=False)
        far = lax.dynamic_index_in_dim(pair, 1 - self.mid, 1, keepdims=False)
        by_mid = self.flip(far[1, :half], 2)
        by_rep = self.swap_rep(far[1, half:])
        to_rep = jnp.concatenate([near[1, :half] + by_mid, near[1, half:]], axis=0)
        to_mid = jnp.concatenate([far[0, :half], far[0, half:] + by_rep], axis=0)
        return (
            near[0].astype(f32)
            + self.swap_rep(to_rep).astype(f32)
            + self.flip(to_mid, 2).astype(f32)
        )


    def gather_outer(self, a, axis):
        if self.outer == 1:
            return a
        shape = a.shape[:axis] + (self.outer,) + a.shape[axis:]
        got = jnp.zeros(shape, a.dtype)
        for j in range(self.outer):
            one = self.shift_hi(a, j) if j else a
            got = lax.dynamic_update_index_in_dim(got, one, (self.hi - j) % self.outer, axis)
        return got.reshape(a.shape[:axis] + (-1,) + a.shape[axis + 1 :])

    def reduce_outer(self, a, axis):
        if self.outer == 1:
            return a
        a = a.reshape(a.shape[:axis] + (self.outer, -1) + a.shape[axis + 1 :])
        total = None
        for j in range(self.outer):
            one = lax.dynamic_index_in_dim(a, (self.hi + j) % self.outer, axis, keepdims=False)
            one = self.shift_hi(one, j) if j else one
            total = one if total is None else total + one
        return total


def split_columns(w, widths, padded):
    rows = w.shape[0]
    pieces = w.reshape(rows, SHARE, -1, widths)
    pieces = jnp.pad(pieces, ((0, 0), (0, 0), (0, 0), (0, padded - widths)))
    return pieces.reshape(rows, SHARE, -1).transpose(1, 0, 2)


def join_columns(by_share, widths, padded):
    rows = by_share.shape[1]
    pieces = by_share.reshape(SHARE, rows, -1, padded)[..., :widths]
    return pieces.transpose(1, 0, 2, 3).reshape(rows, -1)


def rms_scale(values):
    return lax.rsqrt(jnp.mean(values * values, axis=-1, keepdims=True) + norm_epsilon)


def by_position(a, axis, half_rows):
    lead = a.shape[:axis]
    a = a.reshape(lead + (-1, 2, half_rows) + a.shape[axis + 1 :])
    early = lax.index_in_dim(a, 0, axis + 1, keepdims=False)
    late = jnp.flip(lax.index_in_dim(a, 1, axis + 1, keepdims=False), axis)
    both = jnp.concatenate([early, late], axis=axis)
    return both.reshape(lead + (-1,) + both.shape[axis + 2 :])


def by_storage(a, axis, half_rows):
    lead = a.shape[:axis]
    a = a.reshape(lead + (2, -1, half_rows) + a.shape[axis + 1 :])
    early = lax.index_in_dim(a, 0, axis, keepdims=False)
    late = jnp.flip(lax.index_in_dim(a, 1, axis, keepdims=False), axis)
    both = jnp.stack([early, late], axis=axis + 1)
    return both.reshape(lead + (-1,) + both.shape[axis + 3 :])


def body(
    tokens,
    cotangent,
    segments,
    attn_gain,
    w_query,
    w_key,
    w_value,
    w_out,
    mlp_gain,
    w_gate,
    w_up,
    w_down,
):
    at = Place()
    micro_count, local_batch, rows, model_width = tokens.shape
    streams = micro_count * local_batch
    seq_length = rows * at.ctx
    half_rows = rows // 2
    own_rows = w_query.shape[0]
    hidden = w_gate.shape[1]
    share = hidden // SHARE
    wide = round_up(share, LANES)

    qkv_shares = jnp.concatenate(
        [
            split_columns(w_query, HALF, LANES // 2),
            split_columns(w_key, HALF, LANES // 2),
            split_columns(w_value, HEAD_DIM, LANES),
        ],
        axis=2,
    )
    gains = jnp.stack([attn_gain, mlp_gain]).T
    gains_all = lax.all_gather(gains, ("dp", "ctx"), axis=0, tiled=True)
    gains_own = at.to_own_order(gains_all.T).astype(f32)
    gain_one, gain_two = gains_own[0], gains_own[1]
    x_all_raw = tokens.reshape(streams, rows, model_width)
    x_own = [at.to_own_order(x_all_raw[i]) for i in range(streams)]
    w_qkv = at.gather_rows(at.gather_inner(qkv_shares))
    w_o = at.gather_rows(at.gather_inner(split_columns(w_out, HEAD_DIM, LANES)))
    gate_up_shares = jnp.concatenate(
        [split_columns(w_gate, share, wide), split_columns(w_up, share, wide)], axis=2
    )
    w_gu = at.gather_rows(at.gather_inner(gate_up_shares))
    w_d = at.gather_rows(at.gather_inner(split_columns(w_down, share, wide)))

    positions = true_positions(seq_length, at.ctx)
    group_rows = INNER * rows
    group_pos = lax.dynamic_slice_in_dim(positions, at.hi * group_rows, group_rows)
    bases = group_pos.reshape(-1, half_rows)[:, 0]
    frequency = rope_base ** (-2.0 * jnp.arange(HALF, dtype=f32) / HEAD_DIM)
    angles = group_pos.astype(f32)[:, None] * frequency[None, :]
    gap = jnp.zeros((group_rows, LANES // 2 - HALF), f32)
    cos_half, sin_half = jnp.cos(angles), jnp.sin(angles)
    cosine = jnp.concatenate([cos_half, gap, cos_half, gap], axis=1)
    sine = jnp.concatenate([-sin_half, gap, sin_half, gap], axis=1)
    cosine_sub = cosine.reshape(-1, half_rows, LANES)
    sine_sub = sine.reshape(-1, half_rows, LANES)
    own_segments = segments.reshape(streams, seq_length)
    all_segments = jnp.stack([own_segments, at.swap_rep(own_segments)], axis=1)
    seg_k = by_position(all_segments, 2, half_rows)[..., None]
    seg_q = lax.dynamic_slice_in_dim(all_segments, at.hi * group_rows, group_rows, 2)
    seg_q = seg_q.reshape(streams, 2, -1, 1, half_rows)
    subs = group_rows // half_rows

    def normed(block):
        values = block.astype(f32)
        return (values * rms_scale(values) * gain_one).astype(bf16)

    kept = []
    for i in range(streams):
        xn = at.gather_plane(x_own[i], normed).reshape(-1, model_width)
        qkv = project(xn, w_qkv, cosine, sine, rows)
        qkv = qkv.reshape(2, group_rows, -1)
        queries = qkv[..., : GROUP * LANES].reshape(2, subs, half_rows, -1)
        kv = by_position(at.gather_outer(qkv[..., GROUP * LANES :], 1), 1, half_rows)
        k, v = kv[..., :LANES], kv[..., LANES:]
        attended, lse = attend(bases, queries, k, v.transpose(0, 2, 1), seg_q[i], seg_k[i])
        attended = attended.reshape(-1, GROUP * LANES)
        partial = dot_nt(attended, w_o, bf16)
        branch = at.reduce_plane(partial.reshape(2, INNER, rows, model_width))
        kept.append((xn, queries, k, v, attended, lse, branch))

    kept_two = []
    for i in range(streams):
        residual = x_own[i].astype(f32) + kept[i][-1]
        second_scale = rms_scale(residual)
        second_hat = residual * second_scale
        xn2 = at.gather_plane((second_hat * gain_two).astype(bf16)).reshape(-1, model_width)
        gate_up = dot_nn(xn2, w_gu)
        gate, up = gate_up[:, :wide], gate_up[:, wide:]
        sigma = jax.nn.sigmoid(gate)
        act = (gate * sigma * up).astype(bf16)
        partial = dot_nt(act, w_d, bf16)
        mlp_out = at.reduce_plane(partial.reshape(2, INNER, rows, model_width))
        output = at.to_natural_order((residual + mlp_out).astype(bf16))
        kept_two.append((residual, second_scale, second_hat, xn2, gate, up, sigma, act, output))

    kept_three = []
    for i in range(streams):
        residual, second_scale, second_hat, xn2, gate, up, sigma, act, output = kept_two[i]
        g_own = at.to_own_order(cotangent.reshape(streams, rows, model_width)[i])
        g_all = at.gather_plane(g_own).reshape(-1, model_width)
        d_act = dot_nn(g_all, w_d)
        d_gate = (d_act * up * sigma * (1.0 + gate * (1.0 - sigma))).astype(bf16)
        d_up = (d_act * gate * sigma).astype(bf16)
        d_gu = jnp.concatenate([d_gate, d_up], axis=1)
        partial = dot_nt(d_gu, w_gu, bf16)
        d_xn2 = at.reduce_plane(partial.reshape(2, INNER, rows, model_width))
        gain_grad = jnp.sum(d_xn2 * second_hat, axis=0)
        d_hat = d_xn2 * gain_two
        d_residual = g_own.astype(f32) + second_scale * (
            d_hat - second_hat * jnp.mean(d_hat * second_hat, axis=-1, keepdims=True)
        )
        kept_three.append((g_all, d_gu, gain_grad, d_residual))

    grad_d = sum(dot_tn(kept_three[i][0], kept_two[i][7]) for i in range(streams)).astype(bf16)
    grad_gu = sum(dot_tn(kept_two[i][3], kept_three[i][1]) for i in range(streams)).astype(bf16)
    shares_d = at.scatter_inner(at.reduce_rows(grad_d).astype(bf16).reshape(INNER, own_rows, -1))
    shares_gu = at.scatter_inner(at.reduce_rows(grad_gu).astype(bf16).reshape(INNER, own_rows, -1))

    kept_four = []
    for i in range(streams):
        xn, queries, k, v, attended, lse, _ = kept[i]
        d_residual = kept_three[i][3]
        d_branch = at.gather_plane(d_residual.astype(bf16)).reshape(-1, model_width)
        d_attended = dot_nn(d_branch, w_o, bf16).reshape(queries.shape)
        dq, dk, dv = attend_back(
            bases,
            queries,
            k,
            k.transpose(0, 2, 1),
            v,
            seg_q[i],
            seg_k[i],
            d_attended,
            lse,
            cosine_sub,
            sine_sub,
        )
        d_kv = jnp.concatenate([dk, dv], axis=2)
        if at.outer > 1:
            d_kv = d_kv.astype(bf16)
        d_kv = at.reduce_outer(by_storage(d_kv, 1, half_rows), 1).astype(f32)
        dk, dv = d_kv[..., :LANES], d_kv[..., LANES:]
        dk = dk * cosine - jnp.roll(dk, LANES // 2, axis=2) * sine
        d_qkv = jnp.concatenate(
            [dq.reshape(2, group_rows, -1), dk.astype(bf16), dv.astype(bf16)], axis=2
        ).reshape(2 * group_rows, -1)
        partial = dot_nt(d_qkv, w_qkv, bf16)
        d_xn = at.reduce_plane(partial.reshape(2, INNER, rows, model_width))
        values = x_own[i].astype(f32)
        first_scale = rms_scale(values)
        first_hat = values * first_scale
        gain_grad = jnp.sum(d_xn * first_hat, axis=0)
        d_hat = d_xn * gain_one
        input_grad = d_residual + first_scale * (
            d_hat - first_hat * jnp.mean(d_hat * first_hat, axis=-1, keepdims=True)
        )
        kept_four.append((d_branch, d_qkv, gain_grad, at.to_natural_order(input_grad)))

    grad_o = sum(dot_tn(kept_four[i][0], kept[i][4]) for i in range(streams)).astype(bf16)
    grad_qkv = sum(dot_tn(kept[i][0], kept_four[i][1]) for i in range(streams)).astype(bf16)
    shares_o = at.scatter_inner(at.reduce_rows(grad_o).astype(bf16).reshape(INNER, own_rows, -1))
    shares_qkv = at.scatter_inner(
        at.reduce_rows(grad_qkv).astype(bf16).reshape(INNER, own_rows, -1)
    )

    gain_grads = jnp.stack(
        [
            sum(kept_four[i][2] for i in range(streams)),
            sum(kept_three[i][2] for i in range(streams)),
        ]
    )
    gain_grads = gain_grads + at.flip(gain_grads, 1)
    gain_grads = gain_grads + at.flip(gain_grads, 2)
    gain_grads = gain_grads + at.swap_rep(gain_grads)
    gain_grads = at.reduce_rows(gain_grads.T, f32).reshape(INNER, own_rows, 2)
    gain_grads = lax.dynamic_index_in_dim(gain_grads, at.inner, 0, keepdims=False).astype(f32)

    wide_heads = GROUP * LANES
    return (
        jnp.stack([one[-1] for one in kept_two]).reshape(tokens.shape),
        jnp.stack([one[-1] for one in kept_four]).reshape(tokens.shape),
        gain_grads[:, 0],
        join_columns(shares_qkv[..., :wide_heads], HALF, LANES // 2).astype(f32),
        join_columns(shares_qkv[..., wide_heads : wide_heads + LANES], HALF, LANES // 2).astype(f32),
        join_columns(shares_qkv[..., wide_heads + LANES :], HEAD_DIM, LANES).astype(f32),
        join_columns(shares_o, HEAD_DIM, LANES).astype(f32),
        gain_grads[:, 1],
        join_columns(shares_gu[..., :wide], share, wide).astype(f32),
        join_columns(shares_gu[..., wide:], share, wide).astype(f32),
        join_columns(shares_d, share, wide).astype(f32),
    )


def solution(mesh):
    sequence = P(None, ("rep", "dp"), "ctx", None)
    rows = P(("dp", "ctx"), None)
    vector = P(("dp", "ctx"))
    return jax.shard_map(
        body,
        mesh=mesh,
        in_specs=(
            sequence,
            sequence,
            P(None, ("rep", "dp"), None),
            vector,
            rows,
            rows,
            rows,
            rows,
            vector,
            rows,
            rows,
            rows,
        ),
        out_specs=(sequence, sequence, vector, rows, rows, rows, rows, vector, rows, rows, rows),
        check_vma=False,
    )
```

```python
import functools

import jax
import jax.numpy as jnp
from jax import lax
from jax.experimental import pallas as pl
from jax.experimental.pallas import tpu as pltpu
from jax.sharding import PartitionSpec as P

D = 2560
HEADS = 32
KV_HEADS = 8
HEAD_DIM = 80
GROUP = HEADS // KV_HEADS
HALF = HEAD_DIM // 2
LANES = 128
SHARE = 8
INNER = 4

rope_base = 10000.0
norm_epsilon = 1e-05
log2_e = 1.4426950408889634
bf16 = jnp.bfloat16
f32 = jnp.float32


SPEED = 1e10


def lasting(microseconds):
    return pl.CostEstimate(flops=int(microseconds * SPEED), transcendentals=0, bytes_accessed=1)


def dense(rows, depth, cols):
    return lasting(4 + 2 * rows * depth * cols / 9.4e8)


def round_up(value, unit):
    return -(-value // unit) * unit


def true_positions(seq_length, ctx_parts):
    span_rows = seq_length // ctx_parts
    half_rows = span_rows // 2
    stored_index = jnp.arange(seq_length, dtype=jnp.int32)
    device_of = stored_index // span_rows
    within_rows = stored_index % span_rows
    block_of = jnp.where(within_rows < half_rows, device_of, 2 * ctx_parts - 1 - device_of)
    return block_of * half_rows + within_rows % half_rows


def dot_nn(left, right, out=f32):
    return lax.dot_general(left, right, (((1,), (0,)), ((), ())), preferred_element_type=out)


def dot_nt(left, right, out=f32):
    return lax.dot_general(left, right, (((1,), (1,)), ((), ())), preferred_element_type=out)


def dot_tn(left, right, out=f32):
    return lax.dot_general(left, right, (((0,), (0,)), ((), ())), preferred_element_type=out)


def rms_scale(values):
    return lax.rsqrt(jnp.mean(values * values, axis=-1, keepdims=True) + norm_epsilon)


def stack_heads(block):
    return jnp.concatenate(
        [block[:, g * LANES : (g + 1) * LANES] for g in range(GROUP)], axis=0
    )


def bias_of(seg_k, seg_q, first, base):
    rows, cols = seg_k.shape[0], seg_q.shape[1]
    key_pos = first + lax.broadcasted_iota(jnp.int32, (rows, cols), 0)
    query_pos = base + lax.broadcasted_iota(jnp.int32, (rows, cols), 1)
    bias = jnp.where((seg_k == seg_q) & (key_pos <= query_pos), 0.0, -1e30).astype(f32)
    return jnp.concatenate([bias] * GROUP, axis=1)


def forward_kernel(
    chunk, base_ref, q_ref, k_ref, vt_ref, segq_ref, segk_ref, o_ref, lse_ref, s_ref
):
    half_rows = q_ref.shape[3]
    length = k_ref.shape[1]
    base = base_ref[pl.program_id(1)]
    count = (base + half_rows - 1) // chunk + 1
    scale = HEAD_DIM**-0.5 * log2_e

    def run(chunks):
        queries = stack_heads(q_ref[0, 0, 0])
        seg_q = segq_ref[0, 0]
        top = None
        for c in range(chunks):
            at = pl.ds(c * chunk, chunk)
            s = dot_nt(k_ref[0, at], queries) * scale
            s = s + bias_of(segk_ref[0, at], seg_q, c * chunk, base)
            s_ref[at] = s
            now = jnp.max(s, axis=0, keepdims=True)
            top = now if top is None else jnp.maximum(top, now)
        total = None
        mixed = None
        for c in range(chunks):
            at = pl.ds(c * chunk, chunk)
            p = jnp.exp2(s_ref[at] - top)
            now = jnp.sum(p, axis=0, keepdims=True)
            total = now if total is None else total + now
            part = dot_nn(vt_ref[0, :, at], p.astype(bf16))
            mixed = part if mixed is None else mixed + part
        out = (mixed / total).T.astype(bf16)
        for g in range(GROUP):
            o_ref[0, 0, 0, :, g * LANES : (g + 1) * LANES] = out[g * half_rows : (g + 1) * half_rows]
        lse_ref[0, 0] = top + jnp.log2(total)

    for chunks in range(1, length // chunk + 1):
        pl.when(count == chunks)(functools.partial(run, chunks))


def backward_kernel(
    chunk,
    base_ref,
    q_ref,
    k_ref,
    kt_ref,
    v_ref,
    segq_ref,
    segk_ref,
    do_ref,
    lse_ref,
    cos_ref,
    sin_ref,
    dq_ref,
    dk_ref,
    dv_ref,
    p_ref,
    dp_ref,
):
    half_rows = q_ref.shape[3]
    length = k_ref.shape[1]
    base = base_ref[pl.program_id(1)]
    count = (base + half_rows - 1) // chunk + 1
    scale = HEAD_DIM**-0.5

    @pl.when(pl.program_id(1) == 0)
    def _():
        dk_ref[...] = jnp.zeros_like(dk_ref)
        dv_ref[...] = jnp.zeros_like(dv_ref)

    def run(chunks):
        queries = stack_heads(q_ref[0, 0, 0])
        grads = stack_heads(do_ref[0, 0, 0])
        seg_q = segq_ref[0, 0]
        log_total = lse_ref[0, 0]
        inner = None
        for c in range(chunks):
            at = pl.ds(c * chunk, chunk)
            s = dot_nt(k_ref[0, at], queries) * (scale * log2_e)
            s = s + bias_of(segk_ref[0, at], seg_q, c * chunk, base)
            p = jnp.exp2(s - log_total)
            dp = dot_nt(v_ref[0, at], grads)
            dv_ref[0, at] += dot_nn(p.astype(bf16), grads)
            now = jnp.sum(p * dp, axis=0, keepdims=True)
            inner = now if inner is None else inner + now
            p_ref[at] = p
            dp_ref[at] = dp
        dq = None
        for c in range(chunks):
            at = pl.ds(c * chunk, chunk)
            ds = (p_ref[at] * (dp_ref[at] - inner)).astype(bf16)
            dk_ref[0, at] += dot_nn(ds, queries) * scale
            part = dot_nn(kt_ref[0, :, at], ds)
            dq = part if dq is None else dq + part
        dq = (dq * scale).T
        cosine, sine = cos_ref[0], sin_ref[0]
        for g in range(GROUP):
            one = dq[g * half_rows : (g + 1) * half_rows]
            turned = one * cosine - pltpu.roll(one, LANES // 2, 1) * sine
            dq_ref[0, 0, 0, :, g * LANES : (g + 1) * LANES] = turned.astype(bf16)

    for chunks in range(1, length // chunk + 1):
        pl.when(count == chunks)(functools.partial(run, chunks))


def attention_specs(half_rows, length):
    wide = GROUP * LANES
    query = pl.BlockSpec((1, 1, 1, half_rows, wide), lambda s, j, *_: (j // 4, s, j % 4, 0, 0))
    keys = pl.BlockSpec((1, length, LANES), lambda s, j, *_: (s, 0, 0))
    keys_t = pl.BlockSpec((1, LANES, length), lambda s, j, *_: (s, 0, 0))
    seg_q = pl.BlockSpec((1, 1, 1, half_rows), lambda s, j, *_: (s, j, 0, 0))
    seg_k = pl.BlockSpec((1, length, 1), lambda s, j, *_: (s, 0, 0))
    lse = pl.BlockSpec((1, 1, 1, GROUP * half_rows), lambda s, j, *_: (s, j, 0, 0))
    table = pl.BlockSpec((1, half_rows, LANES), lambda s, j, *_: (j, 0, 0))
    return query, keys, keys_t, seg_q, seg_k, lse, table


def attend(bases, queries, k, vt, seg_q, seg_k):
    _, seqs, per_core, half_rows, _ = queries.shape
    subs = 2 * per_core
    length = k.shape[1]
    chunk = 256
    query, keys, keys_t, sq, sk, lse, _ = attention_specs(half_rows, length)
    return pl.pallas_call(
        functools.partial(forward_kernel, chunk),
        grid_spec=pltpu.PrefetchScalarGridSpec(
            num_scalar_prefetch=1,
            grid=(seqs, subs),
            in_specs=[query, keys, keys_t, sq, sk],
            out_specs=[query, lse],
            scratch_shapes=[pltpu.VMEM((length, GROUP * half_rows), f32)],
        ),
        out_shape=[
            jax.ShapeDtypeStruct((2, seqs, per_core, half_rows, GROUP * LANES), bf16),
            jax.ShapeDtypeStruct((seqs, subs, 1, GROUP * half_rows), f32),
        ],
        compiler_params=pltpu.CompilerParams(vmem_limit_bytes=48 << 20),
        cost_estimate=lasting(16),
    )(bases, queries, k, vt, seg_q, seg_k)


def attend_back(bases, queries, k, kt, v, seg_q, seg_k, grads, lse_in, cosine, sine):
    _, seqs, per_core, half_rows, _ = queries.shape
    subs = 2 * per_core
    length = k.shape[1]
    chunk = 256
    query, keys, keys_t, sq, sk, lse, table = attention_specs(half_rows, length)
    return pl.pallas_call(
        functools.partial(backward_kernel, chunk),
        grid_spec=pltpu.PrefetchScalarGridSpec(
            num_scalar_prefetch=1,
            grid=(seqs, subs),
            in_specs=[query, keys, keys_t, keys, sq, sk, query, lse, table, table],
            out_specs=[query, keys, keys],
            scratch_shapes=[pltpu.VMEM((length, GROUP * half_rows), f32)] * 2,
        ),
        out_shape=[
            jax.ShapeDtypeStruct((2, seqs, per_core, half_rows, GROUP * LANES), bf16),
            jax.ShapeDtypeStruct((seqs, length, LANES), f32),
            jax.ShapeDtypeStruct((seqs, length, LANES), f32),
        ],
        compiler_params=pltpu.CompilerParams(vmem_limit_bytes=48 << 20),
        cost_estimate=lasting(24),
    )(bases, queries, k, kt, v, seg_q, seg_k, grads, lse_in, cosine, sine)


def project_kernel(own_ref, other_ref, w_ref, gain_ref, cos_ref, sin_ref, norm_ref, out_ref):
    half = pl.num_programs(0) // 2

    def run(x_ref):
        values = x_ref[...].astype(f32)
        scale = lax.rsqrt(jnp.mean(values * values, axis=-1, keepdims=True) + norm_epsilon)
        normed = (values * scale * gain_ref[...]).astype(bf16)
        norm_ref[...] = normed
        product = dot_nn(normed, w_ref[...])
        cosine, sine = cos_ref[0], sin_ref[0]
        for g in range(GROUP + 1):
            at = slice(g * LANES, (g + 1) * LANES)
            one = product[:, at]
            turned = one * cosine + pltpu.roll(one, LANES // 2, 1) * sine
            out_ref[:, at] = turned.astype(bf16)
        at = slice((GROUP + 1) * LANES, (GROUP + 2) * LANES)
        out_ref[:, at] = product[:, at].astype(bf16)

    pl.when(pl.program_id(0) < half)(lambda: run(own_ref))
    pl.when(pl.program_id(0) >= half)(lambda: run(other_ref))


def project(own, other, w, gain, cosine, sine):
    rows, width = own.shape
    cols = w.shape[1]
    tile = cosine.shape[1]
    half = rows // tile
    table = pl.BlockSpec((1, tile, LANES), lambda i: (i // half, 0, 0))
    return pl.pallas_call(
        project_kernel,
        grid=(2 * half,),
        in_specs=[
            pl.BlockSpec((tile, width), lambda i: (jnp.minimum(i, half - 1), 0)),
            pl.BlockSpec((tile, width), lambda i: (jnp.maximum(i - half, 0), 0)),
            pl.BlockSpec(w.shape, lambda i: (0, 0)),
            pl.BlockSpec((1, width), lambda i: (0, 0)),
            table,
            table,
        ],
        out_specs=[
            pl.BlockSpec((tile, width), lambda i: (i, 0)),
            pl.BlockSpec((tile, cols), lambda i: (i, 0)),
        ],
        out_shape=[
            jax.ShapeDtypeStruct((2 * rows, width), bf16),
            jax.ShapeDtypeStruct((2 * rows, cols), bf16),
        ],
        compiler_params=pltpu.CompilerParams(vmem_limit_bytes=56 << 20),
        cost_estimate=lasting(18),
    )(own, other, w, gain, cosine, sine)


def weight_kernel(count, packed, *refs):
    total = None
    xs, ds = refs[: count[0]], refs[count[0] : sum(count)]
    each = count[0] // count[1]
    for i, x_ref in enumerate(xs):
        rows = x_ref.shape[0]
        at = pl.ds(i % each * rows, rows)
        part = dot_tn(x_ref[...], ds[i // each][at])
        total = part if total is None else total + part
    total = total.astype(bf16)
    if packed:
        total = dot_nt(total, refs[sum(count)][...]).astype(bf16)
    refs[-1][...] = total


def weight_grad(xs, ds, place=None, tile=256):
    xs, ds = list(xs), list(ds)
    count = (len(xs), len(ds))
    width, cols = xs[0].shape[1], ds[0].shape[1]
    places = [] if place is None else [place]
    out_cols = cols if place is None else place.shape[0]
    return pl.pallas_call(
        functools.partial(weight_kernel, count, bool(places)),
        grid=(width // tile,),
        in_specs=[pl.BlockSpec((x.shape[0], tile), lambda i: (0, i)) for x in xs]
        + [pl.BlockSpec(d.shape, lambda i: (0, 0)) for d in ds + places],
        out_specs=pl.BlockSpec((tile, out_cols), lambda i: (i, 0)),
        out_shape=jax.ShapeDtypeStruct((width, out_cols), bf16),
        compiler_params=pltpu.CompilerParams(vmem_limit_bytes=60 << 20),
        cost_estimate=dense(sum(x.shape[0] for x in xs), width, cols),
    )(*xs, *ds, *places)


PARAMS = pltpu.CompilerParams(vmem_limit_bytes=56 << 20)


def whole(a):
    return pl.BlockSpec(a.shape, lambda *_: (0,) * a.ndim)


def expand_kernel(own_ref, other_ref, w_ref, both_ref, act_ref):
    rows = own_ref.shape[0]
    for i, x_ref in enumerate((own_ref, other_ref)):
        at = slice(i * rows, (i + 1) * rows)
        both = dot_nn(x_ref[...], w_ref[...])
        gate, up = both[:, :LANES], both[:, LANES:]
        both_ref[at] = both
        act_ref[at] = (gate * jax.nn.sigmoid(gate) * up).astype(bf16)


def expand(own, other, w):
    rows, width = own.shape
    cols = w.shape[1]
    return pl.pallas_call(
        expand_kernel,
        grid=(cols // (2 * LANES),),
        in_specs=[whole(own), whole(other), pl.BlockSpec((width, 2 * LANES), lambda j: (0, j))],
        out_specs=[
            pl.BlockSpec((2 * rows, 2 * LANES), lambda j: (0, j)),
            pl.BlockSpec((2 * rows, LANES), lambda j: (0, j)),
        ],
        out_shape=[
            jax.ShapeDtypeStruct((2 * rows, cols), f32),
            jax.ShapeDtypeStruct((2 * rows, cols // 2), bf16),
        ],
        compiler_params=PARAMS,
        cost_estimate=dense(2 * rows, width, cols),
    )(own, other, w)


def expand_back_kernel(own_ref, other_ref, both_ref, w_ref, out_ref):
    half = pl.num_programs(0) // 2

    def run(g_ref):
        d_act = dot_nn(g_ref[...], w_ref[...])
        for j in range(d_act.shape[1] // LANES):
            gate = both_ref[:, 2 * j * LANES : (2 * j + 1) * LANES]
            up = both_ref[:, (2 * j + 1) * LANES : (2 * j + 2) * LANES]
            d = d_act[:, j * LANES : (j + 1) * LANES]
            sigma = jax.nn.sigmoid(gate)
            d_sigma = d * sigma
            d_gate = d_sigma * up * (1.0 + gate * (1.0 - sigma))
            out_ref[:, 2 * j * LANES : (2 * j + 1) * LANES] = d_gate.astype(bf16)
            out_ref[:, (2 * j + 1) * LANES : (2 * j + 2) * LANES] = (d_sigma * gate).astype(bf16)

    pl.when(pl.program_id(0) < half)(lambda: run(own_ref))
    pl.when(pl.program_id(0) >= half)(lambda: run(other_ref))


def expand_back(own, other, both, w):
    rows, width = own.shape
    cols = both.shape[1]
    tile = 256 if rows % 256 == 0 else rows
    half = rows // tile
    return pl.pallas_call(
        expand_back_kernel,
        grid=(2 * half,),
        in_specs=[
            pl.BlockSpec((tile, width), lambda i: (jnp.minimum(i, half - 1), 0)),
            pl.BlockSpec((tile, width), lambda i: (jnp.maximum(i - half, 0), 0)),
            pl.BlockSpec((tile, cols), lambda i: (i, 0)),
            whole(w),
        ],
        out_specs=pl.BlockSpec((tile, cols), lambda i: (i, 0)),
        out_shape=jax.ShapeDtypeStruct((2 * rows, cols), bf16),
        compiler_params=PARAMS,
        cost_estimate=dense(2 * rows, width, cols // 2),
    )(own, other, both, w)


def shrink_kernel(a_ref, b_ref, own_ref, other_ref):
    rows = own_ref.shape[0]
    b = b_ref[...]
    own_ref[...] = dot_nt(a_ref[:rows], b).astype(bf16)
    other_ref[...] = dot_nt(a_ref[rows:], b).astype(bf16)


def shrink(a, b, tile=256):
    rows, depth = a.shape
    cols = b.shape[0]
    block = pl.BlockSpec((rows // 2, tile), lambda j: (0, j))
    return pl.pallas_call(
        shrink_kernel,
        grid=(cols // tile,),
        in_specs=[whole(a), pl.BlockSpec((tile, depth), lambda j: (j, 0))],
        out_specs=[block, block],
        out_shape=[jax.ShapeDtypeStruct((rows // 2, cols), bf16)] * 2,
        compiler_params=PARAMS,
        cost_estimate=dense(rows, depth, cols),
    )(a, b)


def grow_kernel(own_ref, other_ref, w_ref, out_ref):
    rows = own_ref.shape[0]
    w = w_ref[...]
    out_ref[:rows] = dot_nn(own_ref[...], w).astype(bf16)
    out_ref[rows:] = dot_nn(other_ref[...], w).astype(bf16)


def grow(own, other, w, tile=256):
    rows, depth = own.shape
    cols = w.shape[1]
    return pl.pallas_call(
        grow_kernel,
        grid=(cols // tile,),
        in_specs=[whole(own), whole(other), pl.BlockSpec((depth, tile), lambda j: (0, j))],
        out_specs=pl.BlockSpec((2 * rows, tile), lambda j: (0, j)),
        out_shape=jax.ShapeDtypeStruct((2 * rows, cols), bf16),
        compiler_params=PARAMS,
        cost_estimate=dense(2 * rows, depth, cols),
    )(own, other, w)


def by_rows(kernel, ins, outs, vectors=()):
    rows, width = outs[0].shape
    tile = rows // 4 if rows % 64 == 0 else rows
    specs, arrays = [whole(v) for v in vectors], list(vectors)
    for one in ins:
        if not isinstance(one, tuple) and one.ndim == 3:
            one = (one, 0)
        if isinstance(one, tuple):
            one, at = one
            specs.append(pl.BlockSpec((None, tile, width), lambda i, at=at: (at, i, 0)))
        else:
            specs.append(pl.BlockSpec((tile, width), lambda i: (i, 0)))
        arrays.append(one)
    return pl.pallas_call(
        kernel,
        grid=(rows // tile,),
        in_specs=specs,
        out_specs=[pl.BlockSpec((tile, width), lambda i: (i, 0))] * len(outs),
        out_shape=outs,
        compiler_params=PARAMS,
        cost_estimate=lasting(5.5),
    )(*arrays)


def wide_sum(refs):
    total = refs[0][...].astype(f32)
    for ref in refs[1:]:
        total = total + ref[...].astype(f32)
    return total


def norm_kernel(gain_ref, *refs):
    residual = wide_sum(refs[:-2])
    refs[-2][...] = residual
    refs[-1][...] = (residual * rms_scale(residual) * gain_ref[...]).astype(bf16)


def norm_back_kernel(count, gain_ref, g_ref, residual_ref, *refs):
    residual = residual_ref[...].astype(f32)
    scale = rms_scale(residual)
    hat = residual * scale
    d_hat = wide_sum(refs[:count]) * gain_ref[...]
    inner = jnp.mean(d_hat * hat, axis=-1, keepdims=True)
    out = g_ref[...].astype(f32) + scale * (d_hat - hat * inner)
    for ref in refs[count:]:
        ref[...] = out.astype(ref.dtype)


def sum_kernel(*refs):
    refs[-1][...] = wide_sum(refs[:-1]).astype(refs[-1].dtype)


def relay_kernel(flag_ref, mid_own, mid_other, rep_own, rep_other, got_ref, mid_ref, rep_ref):
    got = got_ref[...].astype(f32)
    by_mid = flag_ref[...]
    rep_ref[...] = (wide_sum((rep_own, rep_other)) + by_mid * got).astype(bf16)
    mid_ref[...] = (wide_sum((mid_own, mid_other)) + (1.0 - by_mid) * got).astype(bf16)


def stack_kernel(*refs):
    for i, ref in enumerate(refs[:-1]):
        pl.when(pl.program_id(0) == i)(functools.partial(copy_into, ref, refs[-1]))


def copy_into(source, target):
    target[...] = source[...]


def stack_rows(*blocks):
    rows, width = blocks[0].shape
    return pl.pallas_call(
        stack_kernel,
        grid=(len(blocks),),
        in_specs=[whole(b) for b in blocks],
        out_specs=pl.BlockSpec((rows, width), lambda i: (i, 0)),
        out_shape=jax.ShapeDtypeStruct((len(blocks) * rows, width), bf16),
        compiler_params=PARAMS,
        cost_estimate=lasting(5.4),
    )(*blocks)


def shaped(a, kind):
    return jax.ShapeDtypeStruct(a.shape, kind)


def finish_mlp_kernel(hidden, rep_ref, mine_ref, other_ref, wg_ref, wu_ref, *outs):
    gate_ref, up_ref, down_ref, sum_ref = outs
    t = pl.program_id(0)
    wide = gate_ref.shape[1]
    own = jnp.broadcast_to((t // INNER == rep_ref[0]).astype(f32), (1, LANES))
    total = None
    for j in range(wide // LANES):
        cut = slice(j * LANES, (j + 1) * LANES)
        keep = t * wide + j * LANES < hidden

        def taken(column):
            at = slice(column * LANES, (column + 1) * LANES)
            mine, other = mine_ref[0, :, at].astype(f32), other_ref[0, :, at].astype(f32)
            return jnp.where(own > 0.5, mine, other)

        gate, up = taken(2 * j), taken(2 * j + 1)
        gate_ref[:, cut] = gate
        up_ref[:, cut] = up
        down_ref[:, cut] = taken(2 * (wide // LANES) + j)
        part = wg_ref[:, cut].astype(f32) * gate + wu_ref[:, cut].astype(f32) * up
        part = jnp.where(jnp.broadcast_to(keep, part.shape), part, 0.0)
        total = part if total is None else total + part

    @pl.when(t == 0)
    def _():
        sum_ref[...] = jnp.zeros_like(sum_ref)

    sum_ref[...] += total


def finish_mlp(rep, mine, other, w_gate, w_up):
    _, rows, cols = mine.shape
    wide = cols // 3
    hidden = w_gate.shape[1]
    share = pl.BlockSpec((1, rows, cols), lambda t, *_: (t % INNER, 0, 0))
    block = pl.BlockSpec((rows, wide), lambda t, *_: (0, t))
    return pl.pallas_call(
        functools.partial(finish_mlp_kernel, hidden),
        grid_spec=pltpu.PrefetchScalarGridSpec(
            num_scalar_prefetch=1,
            grid=(SHARE,),
            in_specs=[share, share, block, block],
            out_specs=[block, block, block, pl.BlockSpec((rows, LANES), lambda t, *_: (0, 0))],
        ),
        out_shape=[jax.ShapeDtypeStruct((rows, hidden), f32)] * 3
        + [jax.ShapeDtypeStruct((rows, LANES), f32)],
        compiler_params=PARAMS,
        cost_estimate=lasting(13),
    )(rep, mine, other, w_gate, w_up)


def after(a, *others):
    return lax.optimization_barrier((a, *others))[0]


ORDER = (
    "xd1", "Wa", "ca", "tb", "xd0", "na", "xr1", "Wm", "cm", "xc1", "xr0", "gd0", "wq", "P1",
    "gd1", "nm", "T1", "xc0", "wo", "O1", "gr0", "Of1", "P0", "Oa1", "T0", "gr1", "N1", "nd1",
    "O0", "Of0", "nr1", "Oa0", "gc0", "nc1", "gc1", "N0", "nd0", "E1", "nr0", "B1", "nc0", "X1",
    "E0", "Xf1", "B0", "Xa1", "Wg", "M1", "bd1", "X0", "S0", "Xf0", "S1", "br1", "Xa0", "Wd",
    "Sf0", "bc1", "Sf1", "M0", "bd0", "A1", "Q1", "br0", "Sa1", "Y1", "bc0", "Sa0", "Yf1", "Wo",
    "gpm", "A0", "gcm", "Ya1", "Q0", "glm", "Wq", "Y0", "Yf0", "F1", "gpa", "Ya0", "out0", "gca",
    "out1", "gla", "jm", "F0", "ja",
)


class Place:
    def __init__(self):
        self.parts = lax.axis_size("dp")
        self.ctx = lax.axis_size("ctx")
        self.outer = self.ctx // INNER
        self.rep = lax.axis_index("rep")
        self.part = lax.axis_index("dp")
        self.at_ctx = lax.axis_index("ctx")
        self.inner = self.at_ctx % INNER
        self.hi = self.at_ctx // INNER
        self.core = self.inner % 2
        self.mid = self.inner // 2
        self.last = None

    def run(self, work, *inputs, waits=()):
        held = () if self.last is None else (self.last,)
        inputs, _, _ = lax.optimization_barrier((inputs, held, tuple(waits)))
        out = work(*inputs)
        self.last = jax.tree.leaves(out)[-1]
        return out

    def gate(self, a):
        return a if self.last is None else after(a, self.last)

    def flip(self, a, bits):
        return lax.ppermute(a, "ctx", [(i, i ^ bits) for i in range(self.ctx)])

    def swap_rep(self, a):
        return lax.ppermute(a, "rep", [(0, 1), (1, 0)])

    def shift_hi(self, a, by):
        pairs = [(i, (i + INNER * by) % self.ctx) for i in range(self.ctx)]
        return lax.ppermute(a, "ctx", pairs)


    def gather_rows(self, piece):
        whole = lax.all_gather(piece, "dp", axis=0, tiled=True)
        if self.outer > 1:
            whole = jnp.concatenate(
                [whole] + [self.shift_hi(whole, j) for j in range(1, self.outer)], axis=0
            )
        return whole

    def reduce_rows(self, whole):
        whole = whole.reshape((self.outer, -1) + whole.shape[1:])
        mine = whole[0]
        for j in range(1, self.outer):
            mine = mine + self.shift_hi(whole[j], -j)
        return lax.psum_scatter(mine, "dp", scatter_dimension=0, tiled=True)

    def by_core(self, keep, got):
        return jnp.where(self.core == 0, jnp.stack([keep, got]), jnp.stack([got, keep]))

    def by_mid(self, keep, got):
        return jnp.where(self.mid == 0, jnp.stack([keep, got]), jnp.stack([got, keep]))

    def pick(self, a, index, axis):
        return lax.dynamic_index_in_dim(a, index, axis, keepdims=False)

    def spread_core(self, parts):
        return self.flip(self.gate(self.pick(parts, 1 - self.core, 1)), 1)

    def spread_mid(self, parts, got):
        both = self.run(
            lambda parts, got: self.by_core(self.pick(parts, self.core, 1), got), parts, got
        )
        return both, self.flip(self.gate(self.pick(both, 1 - self.mid, 1)), 2)

    def spread_close(self, both, got):
        return self.by_mid(self.pick(both, self.mid, 1), got)

    def join_shares(self, mine, other):
        low = jnp.where(self.rep == 0, mine, other)
        high = jnp.where(self.rep == 0, other, mine)
        return jnp.concatenate([low, high], axis=0)


    def to_own_order(self, a):
        if self.outer == 1:
            return a
        n, outer = self.parts, self.outer
        width = a.shape[-1] // (n * outer)
        cut = []
        for j in range(outer):
            for part in range(n):
                block = part * outer + (self.hi - j) % outer
                cut.append(lax.dynamic_slice_in_dim(a, block * width, width, a.ndim - 1))
        return jnp.concatenate(cut, axis=-1)

    def to_natural_order(self, a):
        if self.outer == 1:
            return a
        n, outer = self.parts, self.outer
        width = a.shape[-1] // (n * outer)
        cut = []
        for part in range(n):
            for hi in range(outer):
                block = ((self.hi - hi) % outer) * n + part
                cut.append(lax.dynamic_slice_in_dim(a, block * width, width, a.ndim - 1))
        return jnp.concatenate(cut, axis=-1)


    def gather_start(self, a):
        a = self.gate(a)
        return self.swap_rep(a), self.flip(a, 2)

    def relay(self, a):
        pairs = []
        for r in range(2):
            for i in range(self.ctx):
                to = (1 - r) * self.ctx + i if i % 2 else r * self.ctx + (i ^ 2)
                pairs.append((r * self.ctx + i, to))
        return lax.ppermute(a, ("rep", "ctx"), pairs)

    def gather_relay(self, by_rep, by_mid):
        return self.relay(self.gate(jnp.where(self.core == 0, by_rep, by_mid)))

    def gather_close(self, a, direct, relayed):
        by_rep, by_mid = direct
        own = self.run(stack_rows, a, by_mid, by_rep, relayed)
        return own, self.flip(own, 1)


    def reduce_far(self, own, got):
        rows = own.shape[0] // 4
        far = self.run(
            lambda own, got: by_rows(
                sum_kernel,
                [(own.reshape(4, rows, -1), 3), (got.reshape(4, rows, -1), 3)],
                [jax.ShapeDtypeStruct((rows, own.shape[1]), bf16)],
            )[0],
            own,
            got,
        )
        return self.relay(far)

    def reduce_send(self, own, got, relayed):
        own, got = (a.reshape(4, -1, a.shape[1]) for a in (own, got))
        one = shaped(relayed, bf16)
        by_mid = jnp.where(self.core == 0, 1.0, 0.0).astype(f32).reshape(1, 1)
        to_mid, to_rep = self.run(
            lambda own, got, relayed, flag: by_rows(
                relay_kernel,
                [(own, 1), (got, 1), (own, 2), (got, 2), relayed],
                [one, one],
                [flag],
            ),
            own,
            got,
            relayed,
            by_mid,
        )
        return own, got, self.swap_rep(to_rep), self.flip(to_mid, 2)

    def natural_rows(self, a):
        a = jnp.where(self.core == 0, a, jnp.flip(a, 0))
        a = jnp.where(self.mid == 0, a, jnp.flip(a, 2))
        return jnp.moveaxis(a, 0, 2)

    def relative_rows(self, a):
        a = jnp.moveaxis(a, 2, 0)
        a = jnp.where(self.core == 0, a, jnp.flip(a, 0))
        return jnp.where(self.mid == 0, a, jnp.flip(a, 2))


    def gather_outer(self, a, axis):
        if self.outer == 1:
            return a
        shape = a.shape[:axis] + (self.outer,) + a.shape[axis:]
        got = jnp.zeros(shape, a.dtype)
        for j in range(self.outer):
            one = self.shift_hi(a, j) if j else a
            got = lax.dynamic_update_index_in_dim(got, one, (self.hi - j) % self.outer, axis)
        return got.reshape(a.shape[:axis] + (-1,) + a.shape[axis + 1 :])

    def reduce_outer(self, a, axis):
        if self.outer == 1:
            return a
        a = a.reshape(a.shape[:axis] + (self.outer, -1) + a.shape[axis + 1 :]).astype(bf16)
        total = None
        for j in range(self.outer):
            one = lax.dynamic_index_in_dim(a, (self.hi + j) % self.outer, axis, keepdims=False)
            one = self.shift_hi(one, j) if j else one
            total = one.astype(f32) if total is None else total + one.astype(f32)
        return total


def place_matrix(shape, pairs):
    row = lax.broadcasted_iota(jnp.int32, shape, 0)
    col = lax.broadcasted_iota(jnp.int32, shape, 1)
    hit = jnp.zeros(shape, jnp.bool_)
    for at_row, at_col, width in pairs:
        hit |= (row - at_row == col - at_col) & (row >= at_row) & (row < at_row + width)
    return hit.astype(bf16)


def head_halves(row, col):
    return [(row + i * HALF, col + i * (LANES // 2), HALF) for i in range(2)]


def half_of(w, rep):
    cols = w.shape[1] // 2
    return lax.dynamic_slice_in_dim(w, rep * cols, cols, 1)


def join_columns(by_share):
    return jnp.concatenate(list(by_share), axis=1)


def half_even(w, rep, wide):
    w = jnp.pad(w, ((0, 0), (0, SHARE * wide - w.shape[1])))
    return lax.dynamic_slice_in_dim(w, rep * INNER * wide, INNER * wide, 1)


def alternate(gate, up):
    tiles = gate.shape[1] // LANES
    cut = [one[:, j * LANES : (j + 1) * LANES] for j in range(tiles) for one in (gate, up)]
    return jnp.concatenate(cut, axis=1)


def by_position(a, axis, half_rows):
    lead = a.shape[:axis]
    a = a.reshape(lead + (-1, 2, half_rows) + a.shape[axis + 1 :])
    early = lax.index_in_dim(a, 0, axis + 1, keepdims=False)
    late = jnp.flip(lax.index_in_dim(a, 1, axis + 1, keepdims=False), axis)
    both = jnp.concatenate([early, late], axis=axis)
    return both.reshape(lead + (-1,) + both.shape[axis + 2 :])


def by_storage(a, axis, half_rows):
    lead = a.shape[:axis]
    a = a.reshape(lead + (2, -1, half_rows) + a.shape[axis + 1 :])
    early = lax.index_in_dim(a, 0, axis, keepdims=False)
    late = jnp.flip(lax.index_in_dim(a, 1, axis, keepdims=False), axis)
    both = jnp.stack([early, late], axis=axis + 1)
    return both.reshape(lead + (-1,) + both.shape[axis + 3 :])


def body(
    tokens,
    cotangent,
    segments,
    attn_gain,
    w_query,
    w_key,
    w_value,
    w_out,
    mlp_gain,
    w_gate,
    w_up,
    w_down,
):
    at = Place()
    micro_count, local_batch, rows, model_width = tokens.shape
    streams = micro_count * local_batch
    seq_length = rows * at.ctx
    half_rows = rows // 2
    own_rows = w_query.shape[0]
    hidden = w_gate.shape[1]
    wide = round_up(-(-hidden // SHARE), LANES)
    heads_wide = GROUP * LANES

    x_own = [at.to_own_order(one) for one in tokens.reshape(streams, rows, model_width)]
    g_own = [at.to_own_order(one) for one in cotangent.reshape(streams, rows, model_width)]
    every = range(streams)
    qkv_wide = heads_wide + 2 * LANES
    q_cols, k_cols = GROUP * HEAD_DIM, HEAD_DIM
    qkv_cols = round_up(q_cols + 2 * k_cols + 2, LANES)
    o_cols = round_up(q_cols, LANES)
    qkv_place = place_matrix(
        (qkv_cols, qkv_wide),
        [
            pair
            for g in range(GROUP + 1)
            for pair in head_halves(g * HEAD_DIM, g * LANES)
        ]
        + [(q_cols + k_cols, heads_wide + LANES, HEAD_DIM)],
    )
    o_place = place_matrix(
        (o_cols, heads_wide), [(g * HEAD_DIM, g * LANES, HEAD_DIM) for g in range(GROUP)]
    )
    gain_place = place_matrix((8, qkv_cols), [(0, q_cols + 2 * k_cols, 2)])

    def attn_shares(w_query, w_key, w_value, w_out, attn_gain, mlp_gain):
        both = jnp.stack([attn_gain, mlp_gain], axis=1)
        gap = jnp.zeros((own_rows, qkv_cols - q_cols - 2 * k_cols - 2), bf16)
        gap_o = jnp.zeros((own_rows, o_cols - q_cols), bf16)
        w_query, w_key, w_value, w_out = (
            half_of(w, at.rep) for w in (w_query, w_key, w_value, w_out)
        )
        shares = [
            jnp.concatenate(
                [
                    w_query[:, i * q_cols : (i + 1) * q_cols],
                    w_key[:, i * k_cols : (i + 1) * k_cols],
                    w_value[:, i * k_cols : (i + 1) * k_cols],
                    both,
                    gap,
                    w_out[:, i * q_cols : (i + 1) * q_cols],
                    gap_o,
                ],
                axis=1,
            )
            for i in range(INNER)
        ]
        return jnp.stack(shares).reshape(2, 2, own_rows, -1)

    def mlp_shares(*ws):
        gate, up, down = (half_even(w, at.rep, wide) for w in ws)
        shares = []
        for i in range(INNER):
            cut = slice(i * wide, (i + 1) * wide)
            shares.append(
                jnp.concatenate([alternate(gate[:, cut], up[:, cut]), down[:, cut]], axis=1)
            )
        return jnp.stack(shares).reshape(2, 2, own_rows, -1)

    positions = true_positions(seq_length, at.ctx)
    rel_pos = jnp.stack(
        [
            lax.dynamic_slice_in_dim(positions, (at.at_ctx ^ (2 * m + k)) * rows, rows)
            for k in range(2)
            for m in range(2)
        ]
    )
    bases = rel_pos.reshape(-1, half_rows)[:, 0]
    frequency = rope_base ** (-2.0 * jnp.arange(HALF, dtype=f32) / HEAD_DIM)
    angles = rel_pos.reshape(2, 2 * rows, 1).astype(f32) * frequency
    gap = jnp.zeros((2, 2 * rows, LANES // 2 - HALF), f32)
    cos_half, sin_half = jnp.cos(angles), jnp.sin(angles)
    cosine = jnp.concatenate([cos_half, gap, cos_half, gap], axis=2)
    sine = jnp.concatenate([-sin_half, gap, sin_half, gap], axis=2)
    own_segments = segments.reshape(streams, seq_length)
    all_segments = jnp.stack([own_segments, at.swap_rep(own_segments)], axis=1)
    seg_k = by_position(all_segments, 2, half_rows)[..., None]
    seg_q = jnp.stack(
        [
            lax.dynamic_slice_in_dim(all_segments, (at.at_ctx ^ (2 * m + k)) * rows, rows, 2)
            for k in range(2)
            for m in range(2)
        ],
        axis=2,
    ).reshape(streams, 2, -1, 1, half_rows)

    cosine_sub = cosine.reshape(-1, half_rows, LANES)
    sine_sub = sine.reshape(-1, half_rows, LANES)
    tables = (bases, cosine, sine, cosine_sub, sine_sub, seg_q, seg_k)

    def attention_part(qkv, bases, seg_q, seg_k):
        queries = qkv[:, :heads_wide].reshape(2, 2, 4, half_rows, -1)
        kv = at.natural_rows(qkv[:, heads_wide:].reshape(2, 2, 2, rows, -1))
        kv = at.gather_outer(kv.reshape(2, INNER * rows, -1), 1)
        kv = by_position(kv, 1, half_rows)
        k, v = kv[..., :LANES], kv[..., LANES:]
        attended, lse = attend(bases, queries, k, v.transpose(0, 2, 1), seg_q, seg_k)
        return queries, k, v, lse, attended.reshape(-1, heads_wide)

    def attention_back(d_attended, queries, k, v, lse, bases, cosine, sine, cos_sub, sin_sub, seg_q, seg_k):
        dq, dk, dv = attend_back(
            bases,
            queries,
            k,
            k.transpose(0, 2, 1),
            v,
            seg_q,
            seg_k,
            d_attended.reshape(queries.shape),
            lse,
            cos_sub,
            sin_sub,
        )
        d_kv = at.reduce_outer(by_storage(jnp.concatenate([dk, dv], axis=2), 1, half_rows), 1)
        d_kv = at.relative_rows(d_kv.reshape(2, 2, 2, rows, -1)).reshape(2, 2, 2 * rows, -1)
        dk, dv = d_kv[..., :LANES], d_kv[..., LANES:]
        dk = dk * cosine[:, None] - jnp.roll(dk, LANES // 2, axis=3) * sine[:, None]
        return jnp.concatenate(
            [dq.reshape(2, 2, 2 * rows, -1), dk.astype(bf16), dv.astype(bf16)], axis=3
        ).reshape(8 * rows, -1)

    def second_norm(x, gain, *parts):
        return by_rows(norm_kernel, [x, *parts], [shaped(x, f32), shaped(x, bf16)], [gain])

    def second_norm_back(g, residual, gain, *parts):
        return by_rows(
            functools.partial(norm_back_kernel, len(parts)),
            [g, residual, *parts],
            [shaped(g, f32), shaped(g, bf16)],
            [gain],
        )

    def first_norm_back(x, d_residual, gain, *parts):
        return by_rows(
            functools.partial(norm_back_kernel, len(parts)),
            [d_residual, x, *parts],
            [shaped(x, f32)],
            [gain],
        )[0]

    def add_up(*parts):
        return by_rows(sum_kernel, parts, [shaped(parts[0], bf16)])[0]

    def expand_weights(w, gain_place, qkv_place):
        return dot_nt(gain_place, w), dot_nn(w, qkv_place, bf16)

    def grad_parts(*parts):
        return jnp.concatenate(parts, axis=1).reshape(2, 2, own_rows, -1)

    def close_rows(*cuts):
        def work(both, got):
            whole_rows = at.spread_close(both, got).reshape(INNER * own_rows, -1)
            return [whole_rows[:, a:b] for a, b in cuts]

        return work

    def close_shares(both, got):
        return at.spread_close(both, got).reshape(INNER, own_rows, -1)

    v = {}
    task = {}

    def put(name, work):
        task[name] = lambda: v.__setitem__(name, work())

    def gather_tasks(p, i, source):
        put(p + "d" + i, lambda: at.gather_start(source()))
        put(p + "r" + i, lambda: at.gather_relay(*v[p + "d" + i]))
        put(p + "c" + i, lambda: at.gather_close(source(), v[p + "d" + i], v[p + "r" + i]))

    def reduce_tasks(p, i, left, right):
        def first():
            own, other = at.run(shrink, left(), right())
            return own, at.flip(other, 1)

        put(p + i, first)
        put(p + "f" + i, lambda: at.reduce_far(*v[p + i]))
        put(p + "a" + i, lambda: at.reduce_send(*v[p + i], v[p + "f" + i]))

    def grad_task(name, lefts, rights, *place):
        def work():
            xs, ds = lefts(), rights()
            return at.reduce_rows(
                at.run(
                    lambda *parts: weight_grad(
                        parts[: len(xs)],
                        parts[len(xs) : len(xs) + len(ds)],
                        *parts[len(xs) + len(ds) :],
                    ),
                    *xs,
                    *ds,
                    *place,
                )
            )

        put(name, work)

    def start_exchange(work, *parts):
        whole_parts = at.run(work, *parts)
        return whole_parts, at.spread_core(whole_parts)

    every = range(streams)
    for i in every:
        one = str(i)
        gather_tasks("x", one, lambda i=i: x_own[i])
        gather_tasks("g", one, lambda i=i: g_own[i])
        gather_tasks("n", one, lambda i=i: v[f"N{i}"][1])
        gather_tasks("b", one, lambda i=i: v[f"M{i}"][1])
        put(f"P{i}", lambda i=i: at.run(project, *v[f"xc{i}"], v["wq"][1], v["gain"][0], *v["tb"][1:3]))
        put(
            f"T{i}",
            lambda i=i: at.run(
                attention_part, v[f"P{i}"][1], v["tb"][0], v["tb"][5][i], v["tb"][6][i]
            ),
        )
        reduce_tasks("O", one, lambda i=i: v[f"T{i}"][4], lambda: v["wo"])
        put(f"N{i}", lambda i=i: at.run(second_norm, x_own[i], v["gain"][1], *v[f"Oa{i}"]))
        put(f"E{i}", lambda i=i: at.run(expand, *v[f"nc{i}"], v["nm"][0]))
        reduce_tasks("S", one, lambda i=i: v[f"E{i}"][1], lambda: v["nm"][1])
        put(f"out{i}", lambda i=i: at.run(add_up, v[f"N{i}"][0], *v[f"Sa{i}"]))
        put(f"B{i}", lambda i=i: at.run(expand_back, *v[f"gc{i}"], v[f"E{i}"][0], v["nm"][1]))
        reduce_tasks("X", one, lambda i=i: v[f"B{i}"], lambda: v["nm"][0])
        put(
            f"M{i}",
            lambda i=i: at.run(
                second_norm_back, g_own[i], v[f"N{i}"][0], v["gain"][1], *v[f"Xa{i}"]
            ),
        )
        put(f"A{i}", lambda i=i: at.run(grow, *v[f"bc{i}"], v["wo"]))
        put(
            f"Q{i}",
            lambda i=i: at.run(
                attention_back,
                v[f"A{i}"],
                *v[f"T{i}"][:4],
                *v["tb"][:5],
                v["tb"][5][i],
                v["tb"][6][i],
            ),
        )
        reduce_tasks("Y", one, lambda i=i: v[f"Q{i}"], lambda: v["wq"][1])
        put(
            f"F{i}",
            lambda i=i: at.run(
                first_norm_back, x_own[i], v[f"M{i}"][0], v["gain"][0], *v[f"Ya{i}"]
            ),
        )
    put("tb", lambda: at.run(lambda *parts: parts, *tables))
    put(
        "Wa",
        lambda: start_exchange(
            attn_shares, w_query, w_key, w_value, w_out, attn_gain, mlp_gain
        ),
    )
    put("ca", lambda: at.spread_mid(*v["Wa"]))
    put(
        "na",
        lambda: [
            at.gather_rows(one)
            for one in at.run(
                close_rows((0, qkv_cols), (qkv_cols, qkv_cols + o_cols)), *v["ca"]
            )
        ],
    )
    put("Wm", lambda: start_exchange(mlp_shares, w_gate, w_up, w_down))
    put("cm", lambda: at.spread_mid(*v["Wm"]))
    put(
        "nm",
        lambda: [
            at.gather_rows(one)
            for one in at.run(close_rows((0, 2 * wide), (2 * wide, 3 * wide)), *v["cm"])
        ],
    )

    def expanded_weights():
        gains, w = at.run(expand_weights, v["na"][0], gain_place, qkv_place)
        v["gain"] = (gains[0:1], gains[1:2])
        return gains, w

    put("wq", expanded_weights)
    put("wo", lambda: at.run(lambda w, place: dot_nn(w, place, bf16), v["na"][1], o_place))
    def both_cores(p):
        return lambda: [v[f"{p}c{i}"][k] for i in every for k in range(2)]

    grad_task("Wd", both_cores("g"), lambda: [v[f"E{i}"][1] for i in every])
    grad_task("Wg", both_cores("n"), lambda: [v[f"B{i}"] for i in every])
    grad_task("Wo", both_cores("b"), lambda: [v[f"T{i}"][4] for i in every], o_place)
    grad_task(
        "Wq", lambda: [v[f"P{i}"][0] for i in every], lambda: [v[f"Q{i}"] for i in every], qkv_place
    )
    put("gpm", lambda: start_exchange(grad_parts, v["Wg"], v["Wd"]))
    put("gcm", lambda: at.spread_mid(*v["gpm"]))

    def swapped(both, got):
        mine = at.run(close_shares, both, got)
        return mine, at.swap_rep(mine)

    put("glm", lambda: swapped(*v["gcm"]))
    put("gpa", lambda: start_exchange(grad_parts, v["Wq"], v["Wo"]))
    put("gca", lambda: at.spread_mid(*v["gpa"]))
    put("gla", lambda: swapped(*v["gca"]))
    rep_number = at.rep.astype(jnp.int32).reshape(1)
    put("jm", lambda: at.run(finish_mlp, rep_number, *v["glm"], w_gate, w_up))

    def attn_grads(mine, other):
        shares = at.join_shares(mine, other)
        cuts = (0, q_cols, q_cols + k_cols, q_cols + 2 * k_cols)
        parts = [shares[..., a:b] for a, b in zip(cuts, cuts[1:])]
        parts.append(shares[..., qkv_cols : qkv_cols + q_cols])
        return [join_columns(part).astype(f32) for part in parts]

    put("ja", lambda: at.run(attn_grads, *v["gla"]))
    for name in ORDER:
        task[name]()
    outputs = [at.to_natural_order(v[f"out{i}"]) for i in every]
    input_grads = [at.to_natural_order(v[f"F{i}"]) for i in every]
    gate_grad, up_grad, down_grad, mlp_sums = v["jm"]
    query_grad, key_grad, value_grad, out_grad = v["ja"]

    def along(w, grad):
        return jnp.sum(w.astype(f32) * grad, axis=1)

    attn_gain_grad = (
        along(w_query, query_grad) + along(w_key, key_grad) + along(w_value, value_grad)
    ) / attn_gain.astype(f32)
    mlp_gain_grad = jnp.sum(mlp_sums, axis=1) / mlp_gain.astype(f32)

    return (
        jnp.stack(outputs).reshape(tokens.shape),
        jnp.stack(input_grads).reshape(tokens.shape),
        attn_gain_grad,
        query_grad,
        key_grad,
        value_grad,
        out_grad,
        mlp_gain_grad,
        gate_grad,
        up_grad,
        down_grad,
    )


def solution(mesh):
    sequence = P(None, ("rep", "dp"), "ctx", None)
    rows = P(("dp", "ctx"), None)
    vector = P(("dp", "ctx"))
    return jax.shard_map(
        body,
        mesh=mesh,
        in_specs=(
            sequence,
            sequence,
            P(None, ("rep", "dp"), None),
            vector,
            rows,
            rows,
            rows,
            rows,
            vector,
            rows,
            rows,
            rows,
        ),
        out_specs=(sequence, sequence, vector, rows, rows, rows, rows, vector, rows, rows, rows),
        check_vma=False,
    )
```

```python
import functools

import jax
import jax.numpy as jnp
from jax import lax
from jax.experimental import pallas as pl
from jax.experimental.pallas import tpu as pltpu
from jax.sharding import PartitionSpec as P

D = 2560
HEADS = 32
KV_HEADS = 8
HEAD_DIM = 80
GROUP = HEADS // KV_HEADS
HALF = HEAD_DIM // 2
LANES = 128
SHARE = 8
INNER = 4

rope_base = 10000.0
norm_epsilon = 1e-05
log2_e = 1.4426950408889634
bf16 = jnp.bfloat16
f32 = jnp.float32


SPEED = 1e11


def lasting(microseconds):
    return pl.CostEstimate(flops=int(microseconds * SPEED), transcendentals=0, bytes_accessed=1)


def dense(rows, depth, cols):
    return lasting(4 + 2 * rows * depth * cols / 9.4e8)


def round_up(value, unit):
    return -(-value // unit) * unit


def true_positions(seq_length, ctx_parts):
    span_rows = seq_length // ctx_parts
    half_rows = span_rows // 2
    stored_index = jnp.arange(seq_length, dtype=jnp.int32)
    device_of = stored_index // span_rows
    within_rows = stored_index % span_rows
    block_of = jnp.where(within_rows < half_rows, device_of, 2 * ctx_parts - 1 - device_of)
    return block_of * half_rows + within_rows % half_rows


def dot_nn(left, right, out=f32):
    return lax.dot_general(left, right, (((1,), (0,)), ((), ())), preferred_element_type=out)


def dot_nt(left, right, out=f32):
    return lax.dot_general(left, right, (((1,), (1,)), ((), ())), preferred_element_type=out)


def dot_tn(left, right, out=f32):
    return lax.dot_general(left, right, (((0,), (0,)), ((), ())), preferred_element_type=out)


def rms_scale(values):
    return lax.rsqrt(jnp.mean(values * values, axis=-1, keepdims=True) + norm_epsilon)


def stack_heads(block):
    return jnp.concatenate(
        [block[:, g * LANES : (g + 1) * LANES] for g in range(GROUP)], axis=0
    )


def bias_of(seg_k, seg_q, first, base):
    rows, cols = seg_k.shape[0], seg_q.shape[1]
    key_pos = first + lax.broadcasted_iota(jnp.int32, (rows, cols), 0)
    query_pos = base + lax.broadcasted_iota(jnp.int32, (rows, cols), 1)
    bias = jnp.where((seg_k == seg_q) & (key_pos <= query_pos), 0.0, -1e30).astype(f32)
    return jnp.concatenate([bias] * GROUP, axis=1)


def forward_kernel(
    chunk, base_ref, q_ref, k_ref, vt_ref, segq_ref, segk_ref, o_ref, lse_ref, s_ref
):
    half_rows = q_ref.shape[2]
    length = k_ref.shape[1]
    base = base_ref[pl.program_id(2)]
    count = (base + half_rows - 1) // chunk + 1
    scale = HEAD_DIM**-0.5 * log2_e

    def run(chunks):
        queries = stack_heads(q_ref[0, 0])
        seg_q = segq_ref[0, 0]
        top = None
        for c in range(chunks):
            at = pl.ds(c * chunk, chunk)
            s = dot_nt(k_ref[0, at], queries) * scale
            s = s + bias_of(segk_ref[0, at], seg_q, c * chunk, base)
            s_ref[at] = s
            now = jnp.max(s, axis=0, keepdims=True)
            top = now if top is None else jnp.maximum(top, now)
        total = None
        mixed = None
        for c in range(chunks):
            at = pl.ds(c * chunk, chunk)
            p = jnp.exp2(s_ref[at] - top)
            now = jnp.sum(p, axis=0, keepdims=True)
            total = now if total is None else total + now
            part = dot_nn(vt_ref[0, :, at], p.astype(bf16))
            mixed = part if mixed is None else mixed + part
        out = (mixed / total).T.astype(bf16)
        for g in range(GROUP):
            o_ref[0, 0, :, g * LANES : (g + 1) * LANES] = out[g * half_rows : (g + 1) * half_rows]
        lse_ref[0, 0, 0] = top + jnp.log2(total)

    for chunks in range(1, length // chunk + 1):
        pl.when(count == chunks)(functools.partial(run, chunks))


def backward_kernel(
    chunk,
    base_ref,
    q_ref,
    k_ref,
    kt_ref,
    v_ref,
    segq_ref,
    segk_ref,
    do_ref,
    lse_ref,
    cos_ref,
    sin_ref,
    dq_ref,
    dk_ref,
    dv_ref,
    p_ref,
    dp_ref,
):
    half_rows = q_ref.shape[2]
    length = k_ref.shape[1]
    base = base_ref[pl.program_id(2)]
    count = (base + half_rows - 1) // chunk + 1
    scale = HEAD_DIM**-0.5

    @pl.when(pl.program_id(2) == 0)
    def _():
        dk_ref[...] = jnp.zeros_like(dk_ref)
        dv_ref[...] = jnp.zeros_like(dv_ref)

    def run(chunks):
        queries = stack_heads(q_ref[0, 0])
        grads = stack_heads(do_ref[0, 0])
        seg_q = segq_ref[0, 0]
        log_total = lse_ref[0, 0, 0]
        inner = None
        for c in range(chunks):
            at = pl.ds(c * chunk, chunk)
            s = dot_nt(k_ref[0, at], queries) * (scale * log2_e)
            s = s + bias_of(segk_ref[0, at], seg_q, c * chunk, base)
            p = jnp.exp2(s - log_total)
            dp = dot_nt(v_ref[0, at], grads)
            dv_ref[0, at] += dot_nn(p.astype(bf16), grads)
            now = jnp.sum(p * dp, axis=0, keepdims=True)
            inner = now if inner is None else inner + now
            p_ref[at] = p
            dp_ref[at] = dp
        dq = None
        for c in range(chunks):
            at = pl.ds(c * chunk, chunk)
            ds = (p_ref[at] * (dp_ref[at] - inner)).astype(bf16)
            dk_ref[0, at] += dot_nn(ds, queries) * scale
            part = dot_nn(kt_ref[0, :, at], ds)
            dq = part if dq is None else dq + part
        dq = (dq * scale).T
        cosine, sine = cos_ref[0], sin_ref[0]
        for g in range(GROUP):
            one = dq[g * half_rows : (g + 1) * half_rows]
            turned = one * cosine - pltpu.roll(one, LANES // 2, 1) * sine
            dq_ref[0, 0, :, g * LANES : (g + 1) * LANES] = turned.astype(bf16)

    for chunks in range(1, length // chunk + 1):
        pl.when(count == chunks)(functools.partial(run, chunks))


def attention_specs(half_rows, length):
    wide = GROUP * LANES
    query = pl.BlockSpec((1, 1, half_rows, wide), lambda s, e, j, *_: (s, j, 0, e))
    keys = pl.BlockSpec((1, length, LANES), lambda s, e, j, *_: (s, 0, 2 * e))
    values = pl.BlockSpec((1, length, LANES), lambda s, e, j, *_: (s, 0, 2 * e + 1))
    keys_t = pl.BlockSpec((1, LANES, length), lambda s, e, j, *_: (s, 2 * e, 0))
    values_t = pl.BlockSpec((1, LANES, length), lambda s, e, j, *_: (s, 2 * e + 1, 0))
    seg_q = pl.BlockSpec((1, 1, 1, half_rows), lambda s, e, j, *_: (s, j, 0, 0))
    seg_k = pl.BlockSpec((1, length, 1), lambda s, e, j, *_: (s, 0, 0))
    lse = pl.BlockSpec((1, 1, 1, 1, GROUP * half_rows), lambda s, e, j, *_: (s, j, e, 0, 0))
    table = pl.BlockSpec((1, half_rows, LANES), lambda s, e, j, *_: (j, 0, 0))
    summed = pl.BlockSpec((1, length, LANES), lambda s, e, j, *_: (s, 0, e))
    return query, keys, values, keys_t, values_t, seg_q, seg_k, lse, table, summed


def attend(bases, queries, kv, kv_t, seg_q, seg_k):
    seqs, subs, half_rows, wide = queries.shape
    length = kv.shape[1]
    chunk = 256
    query, keys, _, _, values_t, sq, sk, lse, _, _ = attention_specs(half_rows, length)
    return pl.pallas_call(
        functools.partial(forward_kernel, chunk),
        grid_spec=pltpu.PrefetchScalarGridSpec(
            num_scalar_prefetch=1,
            grid=(seqs, 2, subs),
            in_specs=[query, keys, values_t, sq, sk],
            out_specs=[query, lse],
            scratch_shapes=[pltpu.VMEM((length, GROUP * half_rows), f32)],
        ),
        out_shape=[
            jax.ShapeDtypeStruct(queries.shape, bf16),
            jax.ShapeDtypeStruct((seqs, subs, 2, 1, GROUP * half_rows), f32),
        ],
        compiler_params=pltpu.CompilerParams(vmem_limit_bytes=48 << 20),
        cost_estimate=lasting(16),
    )(bases, queries, kv, kv_t, seg_q, seg_k)


def attend_back(bases, queries, kv, kv_t, seg_q, seg_k, grads, lse_in, cosine, sine):
    seqs, subs, half_rows, wide = queries.shape
    length = kv.shape[1]
    chunk = 256
    query, keys, values, keys_t, _, sq, sk, lse, table, summed = attention_specs(half_rows, length)
    return pl.pallas_call(
        functools.partial(backward_kernel, chunk),
        grid_spec=pltpu.PrefetchScalarGridSpec(
            num_scalar_prefetch=1,
            grid=(seqs, 2, subs),
            in_specs=[query, keys, keys_t, values, sq, sk, query, lse, table, table],
            out_specs=[query, summed, summed],
            scratch_shapes=[pltpu.VMEM((length, GROUP * half_rows), f32)] * 2,
        ),
        out_shape=[
            jax.ShapeDtypeStruct(queries.shape, bf16),
            jax.ShapeDtypeStruct((seqs, length, 2 * LANES), f32),
            jax.ShapeDtypeStruct((seqs, length, 2 * LANES), f32),
        ],
        compiler_params=pltpu.CompilerParams(vmem_limit_bytes=48 << 20),
        cost_estimate=lasting(24),
    )(bases, queries, kv, kv_t, kv, seg_q, seg_k, grads, lse_in, cosine, sine)


def project_kernel(*refs):
    blocks, (w_own, w_other, gain_ref, cos_ref, sin_ref, norm_ref, q_ref, kv_ref) = refs[:4], refs[4:]

    def run(x_ref):
        values = x_ref[...].astype(f32)
        normed = (values * rms_scale(values) * gain_ref[...]).astype(bf16)
        norm_ref[...] = normed
        cosine, sine = cos_ref[0], sin_ref[0]
        for e, w_ref in enumerate((w_own, w_other)):
            product = dot_nn(normed, w_ref[...])
            for g in range(GROUP + 1):
                one = product[:, g * LANES : (g + 1) * LANES]
                turned = (one * cosine + pltpu.roll(one, LANES // 2, 1) * sine).astype(bf16)
                if g < GROUP:
                    at = e * GROUP + g
                    q_ref[:, at * LANES : (at + 1) * LANES] = turned
                else:
                    kv_ref[:, 2 * e * LANES : (2 * e + 1) * LANES] = turned
            one = product[:, (GROUP + 1) * LANES :]
            kv_ref[:, (2 * e + 1) * LANES : (2 * e + 2) * LANES] = one.astype(bf16)

    for i, ref in enumerate(blocks):
        pl.when(pl.program_id(0) == i)(functools.partial(run, ref))


def project(blocks, weights, gain, cosine, sine):
    rows, width = blocks[0].shape
    table = pl.BlockSpec((1, rows, LANES), lambda i: (i % 2, 0, 0))
    columns = (width, 2 * GROUP * LANES, 4 * LANES)
    return pl.pallas_call(
        project_kernel,
        grid=(4,),
        in_specs=[whole(a) for a in (*blocks, *weights, gain)] + [table, table],
        out_specs=[pl.BlockSpec((rows, cols), lambda i: (i, 0)) for cols in columns],
        out_shape=[jax.ShapeDtypeStruct((4 * rows, cols), bf16) for cols in columns],
        compiler_params=pltpu.CompilerParams(vmem_limit_bytes=56 << 20),
        cost_estimate=lasting(18),
    )(*blocks, *weights, gain, cosine, sine)


def weight_kernel(count, packed, added, *refs):
    xs, ds, rest = refs[: count[0]], refs[count[0] : sum(count)], list(refs[sum(count) : -1])
    total = None
    each = count[0] // count[1]
    for i, x_ref in enumerate(xs):
        rows = x_ref.shape[0]
        at = pl.ds(i % each * rows, rows)
        part = dot_tn(x_ref[...], ds[i // each][at])
        total = part if total is None else total + part
    if packed:
        total = dot_nt(total.astype(bf16), rest.pop(0)[...])
    if added:
        total = total + rest.pop(0)[...].astype(f32)
    refs[-1][...] = total.astype(bf16)


def weight_grad(xs, ds, half, place=None, more=None, tile=256):
    count = (len(xs), len(ds))
    width, cols = xs[0].shape[1], ds[0].shape[1] // 2
    places = [] if place is None else [place]
    out_cols = cols if place is None else place.shape[0]
    block = pl.BlockSpec((tile, out_cols), lambda i: (i, 0))
    adds = [] if more is None else [more]
    return pl.pallas_call(
        functools.partial(weight_kernel, count, bool(places), bool(adds)),
        grid=(width // tile,),
        in_specs=[pl.BlockSpec((x.shape[0], tile), lambda i: (0, i)) for x in xs]
        + [pl.BlockSpec((d.shape[0], cols), lambda i: (0, half)) for d in ds]
        + [whole(p) for p in places]
        + [block] * len(adds),
        out_specs=block,
        out_shape=jax.ShapeDtypeStruct((width, out_cols), bf16),
        compiler_params=pltpu.CompilerParams(vmem_limit_bytes=60 << 20),
        cost_estimate=dense(sum(d.shape[0] for d in ds), width, cols),
    )(*xs, *ds, *places, *adds)


PARAMS = pltpu.CompilerParams(vmem_limit_bytes=56 << 20)


def whole(a):
    return pl.BlockSpec(a.shape, lambda *_: (0,) * a.ndim)


def expand_kernel(*refs):
    blocks, (w_own, w_other, both_ref, act_ref) = refs[:4], refs[4:]
    half = pl.num_programs(0) // 2

    def run(w_ref):
        w = w_ref[...]
        for i, x_ref in enumerate(blocks):
            rows = x_ref.shape[0]
            at = slice(i * rows, (i + 1) * rows)
            both = dot_nn(x_ref[...], w)
            gate, up = both[:, :LANES], both[:, LANES:]
            both_ref[at] = both
            act_ref[at] = (gate * jax.nn.sigmoid(gate) * up).astype(bf16)

    pl.when(pl.program_id(0) < half)(lambda: run(w_own))
    pl.when(pl.program_id(0) >= half)(lambda: run(w_other))


def halves_spec(shape, axis, tiles):
    first = [lambda j: (0, jnp.minimum(j, tiles - 1)), lambda j: (jnp.minimum(j, tiles - 1), 0)]
    second = [
        lambda j: (0, jnp.maximum(j - tiles, 0)),
        lambda j: (jnp.maximum(j - tiles, 0), 0),
    ]
    return [pl.BlockSpec(shape, first[1 - axis]), pl.BlockSpec(shape, second[1 - axis])]


def expand(blocks, weights):
    rows, width = blocks[0].shape
    cols = 2 * weights[0].shape[1]
    tiles = cols // (4 * LANES)
    return pl.pallas_call(
        expand_kernel,
        grid=(2 * tiles,),
        in_specs=[whole(b) for b in blocks] + halves_spec((width, 2 * LANES), 1, tiles),
        out_specs=[
            pl.BlockSpec((4 * rows, 2 * LANES), lambda j: (0, j)),
            pl.BlockSpec((4 * rows, LANES), lambda j: (0, j)),
        ],
        out_shape=[
            jax.ShapeDtypeStruct((4 * rows, cols), f32),
            jax.ShapeDtypeStruct((4 * rows, cols // 2), bf16),
        ],
        compiler_params=PARAMS,
        cost_estimate=dense(4 * rows, width, cols),
    )(*blocks, *weights)


def expand_back_kernel(*refs):
    blocks, (both_ref, w_own, w_other, out_ref) = refs[:4], refs[4:]

    def run(g_ref):
        g = g_ref[...]
        for e, w_ref in enumerate((w_own, w_other)):
            d_act = dot_nn(g, w_ref[...])
            tiles = d_act.shape[1] // LANES
            for j in range(tiles):
                first = 2 * (e * tiles + j) * LANES
                gate = both_ref[:, first : first + LANES]
                up = both_ref[:, first + LANES : first + 2 * LANES]
                d = d_act[:, j * LANES : (j + 1) * LANES]
                sigma = jax.nn.sigmoid(gate)
                d_sigma = d * sigma
                d_gate = d_sigma * up * (1.0 + gate * (1.0 - sigma))
                out_ref[:, first : first + LANES] = d_gate.astype(bf16)
                out_ref[:, first + LANES : first + 2 * LANES] = (d_sigma * gate).astype(bf16)

    for i, ref in enumerate(blocks):
        pl.when(pl.program_id(0) == i)(functools.partial(run, ref))


def expand_back(blocks, both, weights):
    rows, width = blocks[0].shape
    cols = both.shape[1]
    return pl.pallas_call(
        expand_back_kernel,
        grid=(4,),
        in_specs=[whole(b) for b in blocks]
        + [pl.BlockSpec((rows, cols), lambda i: (i, 0))]
        + [whole(w) for w in weights],
        out_specs=pl.BlockSpec((rows, cols), lambda i: (i, 0)),
        out_shape=jax.ShapeDtypeStruct((4 * rows, cols), bf16),
        compiler_params=PARAMS,
        cost_estimate=dense(4 * rows, width, cols // 2),
    )(*blocks, both, *weights)


def shrink_kernel(a_ref, own_ref, other_ref, *outs):
    depth = own_ref.shape[1]
    rows = outs[0].shape[0]
    own, other = own_ref[...], other_ref[...]
    for i, ref in enumerate(outs):
        at = slice(i * rows, (i + 1) * rows)
        out = dot_nt(a_ref[at, :depth], own) + dot_nt(a_ref[at, depth:], other)
        ref[...] = out.astype(bf16)


def shrink(a, weights, tile=256):
    rows, depth = a.shape
    cols = weights[0].shape[0]
    block = pl.BlockSpec((rows // 4, tile), lambda j: (0, j))
    return pl.pallas_call(
        shrink_kernel,
        grid=(cols // tile,),
        in_specs=[whole(a)] + [pl.BlockSpec((tile, depth // 2), lambda j: (j, 0))] * 2,
        out_specs=[block] * 4,
        out_shape=[jax.ShapeDtypeStruct((rows // 4, cols), bf16)] * 4,
        compiler_params=PARAMS,
        cost_estimate=dense(rows, depth, cols),
    )(a, *weights)


def grow_kernel(*refs):
    blocks, (w_own, w_other, out_ref) = refs[:4], refs[4:]
    half = pl.num_programs(0) // 2

    def run(w_ref):
        w = w_ref[...]
        for i, x_ref in enumerate(blocks):
            rows = x_ref.shape[0]
            out_ref[i * rows : (i + 1) * rows] = dot_nn(x_ref[...], w).astype(bf16)

    pl.when(pl.program_id(0) < half)(lambda: run(w_own))
    pl.when(pl.program_id(0) >= half)(lambda: run(w_other))


def grow(blocks, weights, tile=256):
    rows, depth = blocks[0].shape
    cols = 2 * weights[0].shape[1]
    tiles = cols // (2 * tile)
    return pl.pallas_call(
        grow_kernel,
        grid=(2 * tiles,),
        in_specs=[whole(b) for b in blocks] + halves_spec((depth, tile), 1, tiles),
        out_specs=pl.BlockSpec((4 * rows, tile), lambda j: (0, j)),
        out_shape=jax.ShapeDtypeStruct((4 * rows, cols), bf16),
        compiler_params=PARAMS,
        cost_estimate=dense(4 * rows, depth, cols),
    )(*blocks, *weights)


def by_rows(kernel, ins, outs, vectors=()):
    rows, width = outs[0].shape
    tile = rows // 4 if rows % 64 == 0 else rows
    specs, arrays = [whole(v) for v in vectors], list(vectors)
    for one in ins:
        if not isinstance(one, tuple) and one.ndim == 3:
            one = (one, 0)
        if isinstance(one, tuple):
            one, at = one
            specs.append(pl.BlockSpec((None, tile, width), lambda i, at=at: (at, i, 0)))
        else:
            specs.append(pl.BlockSpec((tile, width), lambda i: (i, 0)))
        arrays.append(one)
    return pl.pallas_call(
        kernel,
        grid=(rows // tile,),
        in_specs=specs,
        out_specs=[pl.BlockSpec((tile, width), lambda i: (i, 0))] * len(outs),
        out_shape=outs,
        compiler_params=PARAMS,
        cost_estimate=lasting(5.5),
    )(*arrays)


def wide_sum(refs):
    total = refs[0][...].astype(f32)
    for ref in refs[1:]:
        total = total + ref[...].astype(f32)
    return total


def norm_kernel(gain_ref, *refs):
    residual = wide_sum(refs[:-2])
    refs[-2][...] = residual
    refs[-1][...] = (residual * rms_scale(residual) * gain_ref[...]).astype(bf16)


def norm_back_kernel(count, gain_ref, g_ref, residual_ref, *refs):
    residual = residual_ref[...].astype(f32)
    scale = rms_scale(residual)
    hat = residual * scale
    d_hat = wide_sum(refs[:count]) * gain_ref[...]
    inner = jnp.mean(d_hat * hat, axis=-1, keepdims=True)
    out = g_ref[...].astype(f32) + scale * (d_hat - hat * inner)
    for ref in refs[count:]:
        ref[...] = out.astype(ref.dtype)


def sum_kernel(*refs):
    refs[-1][...] = wide_sum(refs[:-1]).astype(refs[-1].dtype)


def relay_kernel(flag_ref, to_mid_ref, to_rep_ref, got_ref, mid_ref, rep_ref):
    got = got_ref[...].astype(f32)
    by_mid = flag_ref[...]
    rep_ref[...] = (to_rep_ref[...].astype(f32) + by_mid * got).astype(bf16)
    mid_ref[...] = (to_mid_ref[...].astype(f32) + (1.0 - by_mid) * got).astype(bf16)


def pick_kernel(flag_ref, rep_ref, mid_ref, out_ref):
    by_mid = flag_ref[...]
    rep, mid = rep_ref[...].astype(f32), mid_ref[...].astype(f32)
    out_ref[...] = (by_mid * rep + (1.0 - by_mid) * mid).astype(bf16)


def shaped(a, kind):
    return jax.ShapeDtypeStruct(a.shape, kind)


def finish_mlp_kernel(hidden, rep_ref, mine_ref, other_ref, wg_ref, wu_ref, *outs):
    gate_ref, up_ref, down_ref, sum_ref = outs
    t = pl.program_id(0)
    wide = gate_ref.shape[1]
    own = jnp.broadcast_to((t // INNER == rep_ref[0]).astype(f32), (1, LANES))
    total = None
    for j in range(wide // LANES):
        cut = slice(j * LANES, (j + 1) * LANES)
        keep = t * wide + j * LANES < hidden

        def taken(column):
            at = slice(column * LANES, (column + 1) * LANES)
            mine, other = mine_ref[0, :, at].astype(f32), other_ref[0, :, at].astype(f32)
            return jnp.where(own > 0.5, mine, other)

        gate, up = taken(2 * j), taken(2 * j + 1)
        gate_ref[:, cut] = gate
        up_ref[:, cut] = up
        down_ref[:, cut] = taken(2 * (wide // LANES) + j)
        part = wg_ref[:, cut].astype(f32) * gate + wu_ref[:, cut].astype(f32) * up
        part = jnp.where(jnp.broadcast_to(keep, part.shape), part, 0.0)
        total = part if total is None else total + part

    @pl.when(t == 0)
    def _():
        sum_ref[...] = jnp.zeros_like(sum_ref)

    sum_ref[...] += total


def finish_mlp(rep, mine, other, w_gate, w_up):
    _, rows, cols = mine.shape
    wide = cols // 3
    hidden = w_gate.shape[1]
    share = pl.BlockSpec((1, rows, cols), lambda t, *_: (t % INNER, 0, 0))
    block = pl.BlockSpec((rows, wide), lambda t, *_: (0, t))
    return pl.pallas_call(
        functools.partial(finish_mlp_kernel, hidden),
        grid_spec=pltpu.PrefetchScalarGridSpec(
            num_scalar_prefetch=1,
            grid=(SHARE,),
            in_specs=[share, share, block, block],
            out_specs=[block, block, block, pl.BlockSpec((rows, LANES), lambda t, *_: (0, 0))],
        ),
        out_shape=[jax.ShapeDtypeStruct((rows, hidden), f32)] * 3
        + [jax.ShapeDtypeStruct((rows, LANES), f32)],
        compiler_params=PARAMS,
        cost_estimate=lasting(13),
    )(rep, mine, other, w_gate, w_up)


def after(a, *others):
    return lax.optimization_barrier((a, *others))[0]


ORDER = (
    "Wa", "ca", "xd0", "tb", "na", "Wm", "xr0", "cm", "wq", "nm", "xd1", "gd0", "P0", "gr0", "wo",
    "T0", "xr1", "O0", "P1", "Oa0", "T1", "N0", "nd0", "O1", "nr0", "gd1", "wg", "Oa1", "E0", "N1",
    "wd", "nd1", "B0", "nr1", "X0", "E1", "gr1", "S0", "B1", "Xa0", "X1", "M0", "Wdo", "Xa1",
    "Wgo", "M1", "bd0", "bd1", "Wd", "Wg", "br0", "S1", "A0", "Q0", "br1", "J0", "Y0", "A1", "Sa1",
    "Woo", "Sa0", "out1", "Q1", "out0", "J1", "Wo", "Ya0", "Y1", "F0", "gpm", "Wqo", "Ya1", "gcm",
    "Wq", "F1", "glm", "gpa", "gca", "gla", "jm", "ja",
)


class Place:
    def __init__(self):
        self.parts = lax.axis_size("dp")
        self.ctx = lax.axis_size("ctx")
        self.outer = self.ctx // INNER
        self.rep = lax.axis_index("rep")
        self.part = lax.axis_index("dp")
        self.at_ctx = lax.axis_index("ctx")
        self.inner = self.at_ctx % INNER
        self.hi = self.at_ctx // INNER
        self.core = self.inner % 2
        self.mid = self.inner // 2
        self.last = None

    def run(self, work, *inputs, waits=()):
        held = () if self.last is None else (self.last,)
        inputs, _, _ = lax.optimization_barrier((inputs, held, tuple(waits)))
        out = work(*inputs)
        self.last = jax.tree.leaves(out)[-1]
        return out

    def gate(self, a):
        return a if self.last is None else after(a, self.last)

    def flip(self, a, bits):
        return lax.ppermute(a, "ctx", [(i, i ^ bits) for i in range(self.ctx)])

    def swap_rep(self, a):
        return lax.ppermute(a, "rep", [(0, 1), (1, 0)])

    def shift_hi(self, a, by):
        pairs = [(i, (i + INNER * by) % self.ctx) for i in range(self.ctx)]
        return lax.ppermute(a, "ctx", pairs)


    def gather_rows(self, piece):
        whole = lax.all_gather(piece, "dp", axis=0, tiled=True)
        if self.outer > 1:
            whole = jnp.concatenate(
                [whole] + [self.shift_hi(whole, j) for j in range(1, self.outer)], axis=0
            )
        return whole

    def reduce_rows(self, whole):
        whole = whole.reshape((self.outer, -1) + whole.shape[1:])
        mine = whole[0]
        for j in range(1, self.outer):
            mine = mine + self.shift_hi(whole[j], -j)
        return lax.psum_scatter(mine, "dp", scatter_dimension=0, tiled=True)

    def by_core(self, keep, got):
        return jnp.where(self.core == 0, jnp.stack([keep, got]), jnp.stack([got, keep]))

    def by_mid(self, keep, got):
        return jnp.where(self.mid == 0, jnp.stack([keep, got]), jnp.stack([got, keep]))

    def pick(self, a, index, axis):
        return lax.dynamic_index_in_dim(a, index, axis, keepdims=False)

    def spread_core(self, parts):
        return self.flip(self.gate(self.pick(parts, 1 - self.core, 1)), 1)

    def spread_mid(self, parts, got):
        both = self.run(
            lambda parts, got: self.by_core(self.pick(parts, self.core, 1), got), parts, got
        )
        return both, self.flip(self.gate(self.pick(both, 1 - self.mid, 1)), 2)

    def spread_close(self, both, got):
        return self.by_mid(self.pick(both, self.mid, 1), got)

    def join_shares(self, mine, other):
        low = jnp.where(self.rep == 0, mine, other)
        high = jnp.where(self.rep == 0, other, mine)
        return jnp.concatenate([low, high], axis=0)


    def to_own_order(self, a):
        if self.outer == 1:
            return a
        n, outer = self.parts, self.outer
        width = a.shape[-1] // (n * outer)
        cut = []
        for j in range(outer):
            for part in range(n):
                block = part * outer + (self.hi - j) % outer
                cut.append(lax.dynamic_slice_in_dim(a, block * width, width, a.ndim - 1))
        return jnp.concatenate(cut, axis=-1)

    def to_natural_order(self, a):
        if self.outer == 1:
            return a
        n, outer = self.parts, self.outer
        width = a.shape[-1] // (n * outer)
        cut = []
        for part in range(n):
            for hi in range(outer):
                block = ((self.hi - hi) % outer) * n + part
                cut.append(lax.dynamic_slice_in_dim(a, block * width, width, a.ndim - 1))
        return jnp.concatenate(cut, axis=-1)


    def gather_start(self, a):
        a = self.gate(a)
        return self.swap_rep(a), self.flip(a, 2)

    def relay(self, a):
        pairs = []
        for r in range(2):
            for i in range(self.ctx):
                to = (1 - r) * self.ctx + i if i % 2 else r * self.ctx + (i ^ 2)
                pairs.append((r * self.ctx + i, to))
        return lax.ppermute(a, ("rep", "ctx"), pairs)

    def relays_by_mid(self):
        return jnp.where(self.core == 0, 1.0, 0.0).astype(f32).reshape(1, 1)

    def gather_relay(self, a, by_rep, by_mid):
        chosen = self.run(
            lambda flag, *both: by_rows(pick_kernel, both, [shaped(a, bf16)], [flag])[0],
            self.relays_by_mid(),
            by_rep,
            by_mid,
        )
        return a, by_mid, by_rep, self.relay(chosen)


    def reduce_start(self, here, to_mid, to_rep, far):
        return here, to_mid, to_rep, self.relay(self.gate(far))

    def reduce_send(self, here, to_mid, to_rep, got):
        one = shaped(got, bf16)
        to_mid, to_rep = self.run(
            lambda flag, *parts: by_rows(relay_kernel, parts, [one, one], [flag]),
            self.relays_by_mid(),
            to_mid,
            to_rep,
            got,
        )
        return here, self.swap_rep(to_rep), self.flip(to_mid, 2)

    def natural_rows(self, a):
        a = jnp.where(self.core == 0, a, jnp.flip(a, 0))
        a = jnp.where(self.mid == 0, a, jnp.flip(a, 2))
        return jnp.moveaxis(a, 0, 2)

    def relative_rows(self, a):
        a = jnp.moveaxis(a, 2, 0)
        a = jnp.where(self.core == 0, a, jnp.flip(a, 0))
        return jnp.where(self.mid == 0, a, jnp.flip(a, 2))


    def gather_outer(self, a, axis):
        if self.outer == 1:
            return a
        shape = a.shape[:axis] + (self.outer,) + a.shape[axis:]
        got = jnp.zeros(shape, a.dtype)
        for j in range(self.outer):
            one = self.shift_hi(a, j) if j else a
            got = lax.dynamic_update_index_in_dim(got, one, (self.hi - j) % self.outer, axis)
        return got.reshape(a.shape[:axis] + (-1,) + a.shape[axis + 1 :])

    def reduce_outer(self, a, axis):
        if self.outer == 1:
            return a
        a = a.reshape(a.shape[:axis] + (self.outer, -1) + a.shape[axis + 1 :]).astype(bf16)
        total = None
        for j in range(self.outer):
            one = lax.dynamic_index_in_dim(a, (self.hi + j) % self.outer, axis, keepdims=False)
            one = self.shift_hi(one, j) if j else one
            total = one.astype(f32) if total is None else total + one.astype(f32)
        return total


def place_matrix(shape, pairs):
    row = lax.broadcasted_iota(jnp.int32, shape, 0)
    col = lax.broadcasted_iota(jnp.int32, shape, 1)
    hit = jnp.zeros(shape, jnp.bool_)
    for at_row, at_col, width in pairs:
        hit |= (row - at_row == col - at_col) & (row >= at_row) & (row < at_row + width)
    return hit.astype(bf16)


def head_halves(row, col):
    return [(row + i * HALF, col + i * (LANES // 2), HALF) for i in range(2)]


def half_of(w, rep):
    cols = w.shape[1] // 2
    return lax.dynamic_slice_in_dim(w, rep * cols, cols, 1)


def join_columns(by_share):
    return jnp.concatenate(list(by_share), axis=1)


def half_even(w, rep, wide):
    w = jnp.pad(w, ((0, 0), (0, SHARE * wide - w.shape[1])))
    return lax.dynamic_slice_in_dim(w, rep * INNER * wide, INNER * wide, 1)


def alternate(gate, up):
    tiles = gate.shape[1] // LANES
    cut = [one[:, j * LANES : (j + 1) * LANES] for j in range(tiles) for one in (gate, up)]
    return jnp.concatenate(cut, axis=1)


def by_position(a, axis, half_rows):
    lead = a.shape[:axis]
    a = a.reshape(lead + (-1, 2, half_rows) + a.shape[axis + 1 :])
    early = lax.index_in_dim(a, 0, axis + 1, keepdims=False)
    late = jnp.flip(lax.index_in_dim(a, 1, axis + 1, keepdims=False), axis)
    both = jnp.concatenate([early, late], axis=axis)
    return both.reshape(lead + (-1,) + both.shape[axis + 2 :])


def by_storage(a, axis, half_rows):
    lead = a.shape[:axis]
    a = a.reshape(lead + (2, -1, half_rows) + a.shape[axis + 1 :])
    early = lax.index_in_dim(a, 0, axis, keepdims=False)
    late = jnp.flip(lax.index_in_dim(a, 1, axis, keepdims=False), axis)
    both = jnp.stack([early, late], axis=axis + 1)
    return both.reshape(lead + (-1,) + both.shape[axis + 3 :])


def body(
    tokens,
    cotangent,
    segments,
    attn_gain,
    w_query,
    w_key,
    w_value,
    w_out,
    mlp_gain,
    w_gate,
    w_up,
    w_down,
):
    at = Place()
    micro_count, local_batch, rows, model_width = tokens.shape
    streams = micro_count * local_batch
    seq_length = rows * at.ctx
    half_rows = rows // 2
    own_rows = w_query.shape[0]
    hidden = w_gate.shape[1]
    wide = round_up(-(-hidden // SHARE), LANES)
    heads_wide = GROUP * LANES

    x_own = [at.to_own_order(one) for one in tokens.reshape(streams, rows, model_width)]
    g_own = [at.to_own_order(one) for one in cotangent.reshape(streams, rows, model_width)]
    every = range(streams)
    qkv_wide = heads_wide + 2 * LANES
    q_cols, k_cols = GROUP * HEAD_DIM, HEAD_DIM
    qkv_cols = round_up(q_cols + 2 * k_cols + 2, LANES)
    o_cols = round_up(q_cols, LANES)
    qkv_place = place_matrix(
        (qkv_cols, qkv_wide),
        [
            pair
            for g in range(GROUP + 1)
            for pair in head_halves(g * HEAD_DIM, g * LANES)
        ]
        + [(q_cols + k_cols, heads_wide + LANES, HEAD_DIM)],
    )
    o_place = place_matrix(
        (o_cols, heads_wide), [(g * HEAD_DIM, g * LANES, HEAD_DIM) for g in range(GROUP)]
    )
    gain_place = place_matrix((8, qkv_cols), [(0, q_cols + 2 * k_cols, 2)])

    def attn_shares(w_query, w_key, w_value, w_out, attn_gain, mlp_gain):
        both = jnp.stack([attn_gain, mlp_gain], axis=1)
        gap = jnp.zeros((own_rows, qkv_cols - q_cols - 2 * k_cols - 2), bf16)
        gap_o = jnp.zeros((own_rows, o_cols - q_cols), bf16)
        w_query, w_key, w_value, w_out = (
            half_of(w, at.rep) for w in (w_query, w_key, w_value, w_out)
        )
        shares = [
            jnp.concatenate(
                [
                    w_query[:, i * q_cols : (i + 1) * q_cols],
                    w_key[:, i * k_cols : (i + 1) * k_cols],
                    w_value[:, i * k_cols : (i + 1) * k_cols],
                    both,
                    gap,
                    w_out[:, i * q_cols : (i + 1) * q_cols],
                    gap_o,
                ],
                axis=1,
            )
            for i in range(INNER)
        ]
        return jnp.stack(shares).reshape(2, 2, own_rows, -1)

    def mlp_shares(*ws):
        gate, up, down = (half_even(w, at.rep, wide) for w in ws)
        shares = []
        for i in range(INNER):
            cut = slice(i * wide, (i + 1) * wide)
            shares.append(
                jnp.concatenate([alternate(gate[:, cut], up[:, cut]), down[:, cut]], axis=1)
            )
        return jnp.stack(shares).reshape(2, 2, own_rows, -1)

    positions = true_positions(seq_length, at.ctx)
    rel_pos = jnp.stack(
        [
            lax.dynamic_slice_in_dim(positions, (at.at_ctx ^ (2 * m)) * rows, rows)
            for m in range(2)
        ]
    )
    bases = rel_pos.reshape(-1, half_rows)[:, 0]
    frequency = rope_base ** (-2.0 * jnp.arange(HALF, dtype=f32) / HEAD_DIM)
    angles = rel_pos.reshape(2, rows, 1).astype(f32) * frequency
    gap = jnp.zeros((2, rows, LANES // 2 - HALF), f32)
    cos_half, sin_half = jnp.cos(angles), jnp.sin(angles)
    cosine = jnp.concatenate([cos_half, gap, cos_half, gap], axis=2)
    sine = jnp.concatenate([-sin_half, gap, sin_half, gap], axis=2)
    own_segments = segments.reshape(streams, seq_length)
    all_segments = jnp.stack([own_segments, at.swap_rep(own_segments)], axis=1)
    seg_k = by_position(all_segments, 2, half_rows)[..., None]
    seg_q = jnp.stack(
        [
            lax.dynamic_slice_in_dim(all_segments, (at.at_ctx ^ (2 * m)) * rows, rows, 2)
            for m in range(2)
        ],
        axis=2,
    ).reshape(streams, 2, -1, 1, half_rows)

    cosine_sub = cosine.reshape(-1, half_rows, LANES)
    sine_sub = sine.reshape(-1, half_rows, LANES)
    tables = (bases, cosine, sine, cosine_sub, sine_sub, seg_q, seg_k)

    def swap_shares(kv):
        half = kv.shape[-1] // 2
        return jnp.concatenate([kv[..., half:], kv[..., :half]], axis=-1)

    def attention_part(queries, kv, kv_got, bases, seg_q, seg_k):
        queries = queries.reshape(2, 4, half_rows, -1)
        kv = jnp.stack([kv, swap_shares(kv_got)]).reshape(2, 2, 2, rows, -1)
        kv = at.gather_outer(at.natural_rows(kv).reshape(2, INNER * rows, -1), 1)
        kv = by_position(kv, 1, half_rows)
        kv_t = kv.transpose(0, 2, 1)
        attended, lse = attend(bases, queries, kv, kv_t, seg_q, seg_k)
        return queries, kv, kv_t, lse, attended.reshape(4 * rows, -1)

    def attention_back(d_attended, queries, kv, kv_t, lse, bases, cos_sub, sin_sub, seg_q, seg_k):
        dq, dk, dv = attend_back(
            bases,
            queries,
            kv,
            kv_t,
            seg_q,
            seg_k,
            d_attended.reshape(queries.shape),
            lse,
            cos_sub,
            sin_sub,
        )
        parts = [d[..., e * LANES : (e + 1) * LANES] for e in range(2) for d in (dk, dv)]
        d_kv = jnp.concatenate(parts, axis=2)
        d_kv = at.reduce_outer(by_storage(d_kv, 1, half_rows), 1)
        d_kv = at.relative_rows(d_kv.reshape(2, 2, 2, rows, -1)).reshape(2, 4 * rows, -1)
        return dq.reshape(4 * rows, -1), d_kv[0], swap_shares(d_kv[1]).astype(bf16)

    def attention_join(dq, d_kv, got, cosine, sine):
        d_kv = d_kv + got.astype(f32)
        cosine, sine = (t.reshape(1, 2 * rows, LANES) for t in (cosine, sine))
        parts = []
        for e in range(2):
            dk = d_kv[:, 2 * e * LANES : (2 * e + 1) * LANES].reshape(2, 2 * rows, LANES)
            dk = dk * cosine - jnp.roll(dk, LANES // 2, axis=2) * sine
            parts.append(dq[:, e * heads_wide : (e + 1) * heads_wide])
            parts.append(dk.reshape(4 * rows, LANES).astype(bf16))
            parts.append(d_kv[:, (2 * e + 1) * LANES : (2 * e + 2) * LANES].astype(bf16))
        return jnp.concatenate(parts, axis=1)

    def second_norm(x, gain, *parts):
        return by_rows(norm_kernel, [x, *parts], [shaped(x, f32), shaped(x, bf16)], [gain])

    def second_norm_back(g, residual, gain, *parts):
        return by_rows(
            functools.partial(norm_back_kernel, len(parts)),
            [g, residual, *parts],
            [shaped(g, f32), shaped(g, bf16)],
            [gain],
        )

    def first_norm_back(x, d_residual, gain, *parts):
        return by_rows(
            functools.partial(norm_back_kernel, len(parts)),
            [d_residual, x, *parts],
            [shaped(x, f32)],
            [gain],
        )[0]

    def add_up(*parts):
        return by_rows(sum_kernel, parts, [shaped(parts[0], bf16)])[0]

    def expand_weights(w, gain_place, qkv_place):
        return dot_nt(gain_place, w), dot_nn(w, qkv_place, bf16)

    def grad_parts(*parts):
        return jnp.concatenate(parts, axis=1).reshape(2, 2, own_rows, -1)

    def close_rows(*cuts):
        def work(both, got):
            whole_rows = at.spread_close(both, got).reshape(INNER * own_rows, -1)
            return [whole_rows[:, a:b] for a, b in cuts]

        return work

    def close_shares(both, got):
        return at.spread_close(both, got).reshape(INNER, own_rows, -1)

    v = {}
    task = {}

    def put(name, work):
        task[name] = lambda: v.__setitem__(name, work())

    def gather_tasks(p, i, source):
        put(p + "d" + i, lambda: at.gather_start(source()))
        put(p + "r" + i, lambda: at.gather_relay(source(), *v[p + "d" + i]))

    def reduce_tasks(p, i, left, right):
        put(p + i, lambda: at.reduce_start(*at.run(shrink, left(), right())))
        put(p + "a" + i, lambda: at.reduce_send(*v[p + i]))

    def grad_tasks(name, lefts, rights, place=None):
        def grad(half, *more):
            xs, ds = lefts(), rights()
            count = len(xs) + len(ds)
            return at.run(
                lambda *parts: weight_grad(
                    parts[: len(xs)], parts[len(xs) : count], half, place, *parts[count:]
                ),
                *xs,
                *ds,
                *more,
            )

        put(name + "o", lambda: at.flip(grad(1), 1))
        put(name, lambda: at.reduce_rows(grad(0, v[name + "o"])))

    def start_exchange(work, *parts):
        whole_parts = at.run(work, *parts)
        return whole_parts, at.spread_core(whole_parts)

    def project_task(i):
        normed, queries, kv = at.run(project, v[f"xr{i}"], v["wq"], v["gain"][0], *v["tb"][1:3])
        return normed, queries, kv, at.flip(kv, 1)

    def back_task(i):
        dq, d_kv, sent = at.run(
            attention_back,
            v[f"A{i}"],
            *v[f"T{i}"][:4],
            v["tb"][0],
            *v["tb"][3:5],
            v["tb"][5][i],
            v["tb"][6][i],
        )
        return dq, d_kv, at.flip(sent, 1)

    every = range(streams)
    for i in every:
        one = str(i)
        gather_tasks("x", one, lambda i=i: x_own[i])
        gather_tasks("g", one, lambda i=i: g_own[i])
        gather_tasks("n", one, lambda i=i: v[f"N{i}"][1])
        gather_tasks("b", one, lambda i=i: v[f"M{i}"][1])
        put(f"P{i}", lambda i=i: project_task(i))
        put(
            f"T{i}",
            lambda i=i: at.run(
                attention_part, *v[f"P{i}"][1:], v["tb"][0], v["tb"][5][i], v["tb"][6][i]
            ),
        )
        reduce_tasks("O", one, lambda i=i: v[f"T{i}"][4], lambda: v["wo"])
        put(f"N{i}", lambda i=i: at.run(second_norm, x_own[i], v["gain"][1], *v[f"Oa{i}"]))
        put(f"E{i}", lambda i=i: at.run(expand, v[f"nr{i}"], v["wg"]))
        reduce_tasks("S", one, lambda i=i: v[f"E{i}"][1], lambda: v["wd"])
        put(f"out{i}", lambda i=i: at.run(add_up, v[f"N{i}"][0], *v[f"Sa{i}"]))
        put(f"B{i}", lambda i=i: at.run(expand_back, v[f"gr{i}"], v[f"E{i}"][0], v["wd"]))
        reduce_tasks("X", one, lambda i=i: v[f"B{i}"], lambda: v["wg"])
        put(
            f"M{i}",
            lambda i=i: at.run(
                second_norm_back, g_own[i], v[f"N{i}"][0], v["gain"][1], *v[f"Xa{i}"]
            ),
        )
        put(f"A{i}", lambda i=i: at.run(grow, v[f"br{i}"], v["wo"]))
        put(f"Q{i}", lambda i=i: back_task(i))
        put(f"J{i}", lambda i=i: at.run(attention_join, *v[f"Q{i}"], *v["tb"][1:3]))
        reduce_tasks("Y", one, lambda i=i: v[f"J{i}"], lambda: v["wq"])
        put(
            f"F{i}",
            lambda i=i: at.run(
                first_norm_back, x_own[i], v[f"M{i}"][0], v["gain"][0], *v[f"Ya{i}"]
            ),
        )
    put("tb", lambda: at.run(lambda *parts: parts, *tables))
    put(
        "Wa",
        lambda: start_exchange(
            attn_shares, w_query, w_key, w_value, w_out, attn_gain, mlp_gain
        ),
    )
    put("ca", lambda: at.spread_mid(*v["Wa"]))
    put(
        "na",
        lambda: [
            at.gather_rows(one)
            for one in at.run(
                close_rows((0, qkv_cols), (qkv_cols, qkv_cols + o_cols)), *v["ca"]
            )
        ],
    )
    put("Wm", lambda: start_exchange(mlp_shares, w_gate, w_up, w_down))
    put("cm", lambda: at.spread_mid(*v["Wm"]))
    put(
        "nm",
        lambda: [
            at.gather_rows(one)
            for one in at.run(close_rows((0, 2 * wide), (2 * wide, 3 * wide)), *v["cm"])
        ],
    )

    def expanded_weights():
        gains, w = at.run(expand_weights, v["na"][0], gain_place, qkv_place)
        v["gain"] = (gains[0:1], gains[1:2])
        return w, at.flip(w, 1)

    def expanded_out():
        w = at.run(lambda w, place: dot_nn(w, place, bf16), v["na"][1], o_place)
        return w, at.flip(w, 1)

    put("wq", expanded_weights)
    put("wo", expanded_out)
    put("wg", lambda: (v["nm"][0], at.flip(at.gate(v["nm"][0]), 1)))
    put("wd", lambda: (v["nm"][1], at.flip(at.gate(v["nm"][1]), 1)))

    def over_blocks(p):
        return lambda: [one for i in every for one in v[f"{p}r{i}"]]

    grad_tasks("Wd", over_blocks("g"), lambda: [v[f"E{i}"][1] for i in every])
    grad_tasks("Wg", over_blocks("n"), lambda: [v[f"B{i}"] for i in every])
    grad_tasks("Wo", over_blocks("b"), lambda: [v[f"T{i}"][4] for i in every], o_place)
    grad_tasks(
        "Wq", lambda: [v[f"P{i}"][0] for i in every], lambda: [v[f"J{i}"] for i in every], qkv_place
    )
    put("gpm", lambda: start_exchange(grad_parts, v["Wg"], v["Wd"]))
    put("gcm", lambda: at.spread_mid(*v["gpm"]))

    def swapped(both, got):
        mine = at.run(close_shares, both, got)
        return mine, at.swap_rep(mine)

    put("glm", lambda: swapped(*v["gcm"]))
    put("gpa", lambda: start_exchange(grad_parts, v["Wq"], v["Wo"]))
    put("gca", lambda: at.spread_mid(*v["gpa"]))
    put("gla", lambda: swapped(*v["gca"]))
    rep_number = at.rep.astype(jnp.int32).reshape(1)
    put("jm", lambda: at.run(finish_mlp, rep_number, *v["glm"], w_gate, w_up))

    def attn_grads(mine, other):
        shares = at.join_shares(mine, other)
        cuts = (0, q_cols, q_cols + k_cols, q_cols + 2 * k_cols)
        parts = [shares[..., a:b] for a, b in zip(cuts, cuts[1:])]
        parts.append(shares[..., qkv_cols : qkv_cols + q_cols])
        return [join_columns(part).astype(f32) for part in parts]

    put("ja", lambda: at.run(attn_grads, *v["gla"]))
    for name in ORDER:
        task[name]()
    outputs = [at.to_natural_order(v[f"out{i}"]) for i in every]
    input_grads = [at.to_natural_order(v[f"F{i}"]) for i in every]
    gate_grad, up_grad, down_grad, mlp_sums = v["jm"]
    query_grad, key_grad, value_grad, out_grad = v["ja"]

    def along(w, grad):
        return jnp.sum(w.astype(f32) * grad, axis=1)

    attn_gain_grad = (
        along(w_query, query_grad) + along(w_key, key_grad) + along(w_value, value_grad)
    ) / attn_gain.astype(f32)
    mlp_gain_grad = jnp.sum(mlp_sums, axis=1) / mlp_gain.astype(f32)

    return (
        jnp.stack(outputs).reshape(tokens.shape),
        jnp.stack(input_grads).reshape(tokens.shape),
        attn_gain_grad,
        query_grad,
        key_grad,
        value_grad,
        out_grad,
        mlp_gain_grad,
        gate_grad,
        up_grad,
        down_grad,
    )


def solution(mesh):
    sequence = P(None, ("rep", "dp"), "ctx", None)
    rows = P(("dp", "ctx"), None)
    vector = P(("dp", "ctx"))
    return jax.shard_map(
        body,
        mesh=mesh,
        in_specs=(
            sequence,
            sequence,
            P(None, ("rep", "dp"), None),
            vector,
            rows,
            rows,
            rows,
            rows,
            vector,
            rows,
            rows,
            rows,
        ),
        out_specs=(sequence, sequence, vector, rows, rows, rows, rows, vector, rows, rows, rows),
        check_vma=False,
    )
```

```python
import functools

import jax
import jax.numpy as jnp
from jax import lax
from jax.experimental import pallas as pl
from jax.experimental.pallas import tpu as pltpu
from jax.sharding import PartitionSpec as P

D = 2560
HEADS = 32
KV_HEADS = 8
HEAD_DIM = 80
GROUP = HEADS // KV_HEADS
HALF = HEAD_DIM // 2
LANES = 128
SHARE = 8
INNER = 4

rope_base = 10000.0
norm_epsilon = 1e-05
log2_e = 1.4426950408889634
bf16 = jnp.bfloat16
f32 = jnp.float32


SPEED = 1e10


def lasting(microseconds):
    return pl.CostEstimate(flops=int(microseconds * SPEED), transcendentals=0, bytes_accessed=1)


def dense(rows, depth, cols):
    return lasting(4 + 2 * rows * depth * cols / 9.4e8)


def round_up(value, unit):
    return -(-value // unit) * unit


def true_positions(seq_length, ctx_parts):
    span_rows = seq_length // ctx_parts
    half_rows = span_rows // 2
    stored_index = jnp.arange(seq_length, dtype=jnp.int32)
    device_of = stored_index // span_rows
    within_rows = stored_index % span_rows
    block_of = jnp.where(within_rows < half_rows, device_of, 2 * ctx_parts - 1 - device_of)
    return block_of * half_rows + within_rows % half_rows


def dot_nn(left, right, out=f32):
    return lax.dot_general(left, right, (((1,), (0,)), ((), ())), preferred_element_type=out)


def dot_nt(left, right, out=f32):
    return lax.dot_general(left, right, (((1,), (1,)), ((), ())), preferred_element_type=out)


def dot_tn(left, right, out=f32):
    return lax.dot_general(left, right, (((0,), (0,)), ((), ())), preferred_element_type=out)


def rms_scale(values):
    return lax.rsqrt(jnp.mean(values * values, axis=-1, keepdims=True) + norm_epsilon)


def stack_heads(block):
    return jnp.concatenate(
        [block[:, g * LANES : (g + 1) * LANES] for g in range(GROUP)], axis=0
    )


def bias_of(seg_k, seg_q, first, base):
    rows, cols = seg_k.shape[0], seg_q.shape[1]
    key_pos = first + lax.broadcasted_iota(jnp.int32, (rows, cols), 0)
    query_pos = base + lax.broadcasted_iota(jnp.int32, (rows, cols), 1)
    bias = jnp.where((seg_k == seg_q) & (key_pos <= query_pos), 0.0, -1e30).astype(f32)
    return jnp.concatenate([bias] * GROUP, axis=1)


def limits(base_ref, low_ref, half_rows, chunk):
    at = pl.program_id(0) * pl.num_programs(2) + pl.program_id(2)
    base = base_ref[pl.program_id(2)]
    return base, low_ref[at] // chunk, (base + half_rows - 1) // chunk


def forward_kernel(
    chunk, base_ref, low_ref, q_ref, k_ref, vt_ref, segq_ref, segk_ref, o_ref, lse_ref, s_ref
):
    half_rows = q_ref.shape[2]
    length = k_ref.shape[1]
    base, low, high = limits(base_ref, low_ref, half_rows, chunk)
    scale = HEAD_DIM**-0.5 * log2_e

    def run(seen):
        queries = stack_heads(q_ref[0, 0])
        seg_q = segq_ref[0, 0]
        top = None
        for c in seen:
            at = pl.ds(c * chunk, chunk)
            s = dot_nt(k_ref[0, at], queries) * scale
            s = s + bias_of(segk_ref[0, at], seg_q, c * chunk, base)
            s_ref[at] = s
            now = jnp.max(s, axis=0, keepdims=True)
            top = now if top is None else jnp.maximum(top, now)
        total = None
        mixed = None
        for c in seen:
            at = pl.ds(c * chunk, chunk)
            p = jnp.exp2(s_ref[at] - top)
            now = jnp.sum(p, axis=0, keepdims=True)
            total = now if total is None else total + now
            part = dot_nn(vt_ref[0, :, at], p.astype(bf16))
            mixed = part if mixed is None else mixed + part
        out = (mixed / total).T.astype(bf16)
        for g in range(GROUP):
            o_ref[0, 0, :, g * LANES : (g + 1) * LANES] = out[g * half_rows : (g + 1) * half_rows]
        lse_ref[0, 0, 0] = top + jnp.log2(total)

    for one in range(length // chunk):
        for two in range(one, length // chunk):
            seen = range(one, two + 1)
            pl.when((low == one) & (high == two))(functools.partial(run, seen))


def backward_kernel(
    chunk,
    base_ref,
    low_ref,
    q_ref,
    k_ref,
    kt_ref,
    v_ref,
    segq_ref,
    segk_ref,
    do_ref,
    lse_ref,
    cos_ref,
    sin_ref,
    dq_ref,
    dk_ref,
    dv_ref,
    p_ref,
    dp_ref,
):
    half_rows = q_ref.shape[2]
    length = k_ref.shape[1]
    base, low, high = limits(base_ref, low_ref, half_rows, chunk)
    scale = HEAD_DIM**-0.5

    @pl.when(pl.program_id(2) == 0)
    def _():
        dk_ref[...] = jnp.zeros_like(dk_ref)
        dv_ref[...] = jnp.zeros_like(dv_ref)

    def run(seen):
        queries = stack_heads(q_ref[0, 0])
        grads = stack_heads(do_ref[0, 0])
        seg_q = segq_ref[0, 0]
        log_total = lse_ref[0, 0, 0]
        inner = None
        for c in seen:
            at = pl.ds(c * chunk, chunk)
            s = dot_nt(k_ref[0, at], queries) * (scale * log2_e)
            s = s + bias_of(segk_ref[0, at], seg_q, c * chunk, base)
            p = jnp.exp2(s - log_total)
            dp = dot_nt(v_ref[0, at], grads)
            dv_ref[0, at] += dot_nn(p.astype(bf16), grads)
            now = jnp.sum(p * dp, axis=0, keepdims=True)
            inner = now if inner is None else inner + now
            p_ref[at] = p
            dp_ref[at] = dp
        dq = None
        for c in seen:
            at = pl.ds(c * chunk, chunk)
            ds = (p_ref[at] * (dp_ref[at] - inner)).astype(bf16)
            dk_ref[0, at] += dot_nn(ds, queries) * scale
            part = dot_nn(kt_ref[0, :, at], ds)
            dq = part if dq is None else dq + part
        dq = (dq * scale).T
        cosine, sine = cos_ref[0], sin_ref[0]
        for g in range(GROUP):
            one = dq[g * half_rows : (g + 1) * half_rows]
            turned = one * cosine - pltpu.roll(one, LANES // 2, 1) * sine
            dq_ref[0, 0, :, g * LANES : (g + 1) * LANES] = turned.astype(bf16)

    for one in range(length // chunk):
        for two in range(one, length // chunk):
            seen = range(one, two + 1)
            pl.when((low == one) & (high == two))(functools.partial(run, seen))


def attention_specs(half_rows, length):
    wide = GROUP * LANES
    query = pl.BlockSpec((1, 1, half_rows, wide), lambda s, e, j, *_: (s, j, 0, e))
    keys = pl.BlockSpec((1, length, LANES), lambda s, e, j, *_: (s, 0, 2 * e))
    values = pl.BlockSpec((1, length, LANES), lambda s, e, j, *_: (s, 0, 2 * e + 1))
    keys_t = pl.BlockSpec((1, LANES, length), lambda s, e, j, *_: (s, 2 * e, 0))
    values_t = pl.BlockSpec((1, LANES, length), lambda s, e, j, *_: (s, 2 * e + 1, 0))
    seg_q = pl.BlockSpec((1, 1, 1, half_rows), lambda s, e, j, *_: (s, j, 0, 0))
    seg_k = pl.BlockSpec((1, length, 1), lambda s, e, j, *_: (s, 0, 0))
    lse = pl.BlockSpec((1, 1, 1, 1, GROUP * half_rows), lambda s, e, j, *_: (s, j, e, 0, 0))
    table = pl.BlockSpec((1, half_rows, LANES), lambda s, e, j, *_: (j, 0, 0))
    summed = pl.BlockSpec((1, length, LANES), lambda s, e, j, *_: (s, 0, e))
    return query, keys, values, keys_t, values_t, seg_q, seg_k, lse, table, summed


def attend(bases, lows, queries, kv, kv_t, seg_q, seg_k):
    seqs, subs, half_rows, wide = queries.shape
    length = kv.shape[1]
    chunk = 256
    query, keys, _, _, values_t, sq, sk, lse, _, _ = attention_specs(half_rows, length)
    return pl.pallas_call(
        functools.partial(forward_kernel, chunk),
        grid_spec=pltpu.PrefetchScalarGridSpec(
            num_scalar_prefetch=2,
            grid=(seqs, 2, subs),
            in_specs=[query, keys, values_t, sq, sk],
            out_specs=[query, lse],
            scratch_shapes=[pltpu.VMEM((length, GROUP * half_rows), f32)],
        ),
        out_shape=[
            jax.ShapeDtypeStruct(queries.shape, bf16),
            jax.ShapeDtypeStruct((seqs, subs, 2, 1, GROUP * half_rows), f32),
        ],
        compiler_params=pltpu.CompilerParams(vmem_limit_bytes=48 << 20),
        cost_estimate=lasting(16),
    )(bases, lows, queries, kv, kv_t, seg_q, seg_k)


def attend_back(bases, lows, queries, kv, kv_t, seg_q, seg_k, grads, lse_in, cosine, sine):
    seqs, subs, half_rows, wide = queries.shape
    length = kv.shape[1]
    chunk = 256
    query, keys, values, keys_t, _, sq, sk, lse, table, summed = attention_specs(half_rows, length)
    return pl.pallas_call(
        functools.partial(backward_kernel, chunk),
        grid_spec=pltpu.PrefetchScalarGridSpec(
            num_scalar_prefetch=2,
            grid=(seqs, 2, subs),
            in_specs=[query, keys, keys_t, values, sq, sk, query, lse, table, table],
            out_specs=[query, summed, summed],
            scratch_shapes=[pltpu.VMEM((length, GROUP * half_rows), f32)] * 2,
        ),
        out_shape=[
            jax.ShapeDtypeStruct(queries.shape, bf16),
            jax.ShapeDtypeStruct((seqs, length, 2 * LANES), f32),
            jax.ShapeDtypeStruct((seqs, length, 2 * LANES), f32),
        ],
        compiler_params=pltpu.CompilerParams(vmem_limit_bytes=48 << 20),
        cost_estimate=lasting(24),
    )(bases, lows, queries, kv, kv_t, kv, seg_q, seg_k, grads, lse_in, cosine, sine)


def project_kernel(order_ref, *refs):
    blocks, (w_own, w_other, gain_ref, cos_ref, sin_ref, norm_ref, q_ref, kv_ref) = refs[:4], refs[4:]

    def run(x_ref):
        values = x_ref[...].astype(f32)
        normed = (values * rms_scale(values) * gain_ref[...]).astype(bf16)
        norm_ref[...] = normed
        cosine, sine = cos_ref[0], sin_ref[0]
        for e, w_ref in enumerate((w_own, w_other)):
            product = dot_nn(normed, w_ref[...])
            for g in range(GROUP + 1):
                one = product[:, g * LANES : (g + 1) * LANES]
                turned = (one * cosine + pltpu.roll(one, LANES // 2, 1) * sine).astype(bf16)
                if g < GROUP:
                    at = e * GROUP + g
                    q_ref[:, at * LANES : (at + 1) * LANES] = turned
                else:
                    kv_ref[:, 2 * e * LANES : (2 * e + 1) * LANES] = turned
            one = product[:, (GROUP + 1) * LANES :]
            kv_ref[:, (2 * e + 1) * LANES : (2 * e + 2) * LANES] = one.astype(bf16)

    for i, ref in enumerate(blocks):
        pl.when(pl.program_id(0) == i)(functools.partial(run, ref))


def project(order, blocks, weights, gain, cosine, sine):
    rows, width = blocks[0].shape
    table = pl.BlockSpec((1, rows, LANES), lambda i, order: (order[i] % 2, 0, 0))
    columns = (width, 2 * GROUP * LANES, 4 * LANES)
    return pl.pallas_call(
        project_kernel,
        grid_spec=pltpu.PrefetchScalarGridSpec(
            num_scalar_prefetch=1,
            grid=(4,),
            in_specs=[whole(a) for a in (*blocks, *weights, gain)] + [table, table],
            out_specs=[
                pl.BlockSpec((rows, cols), lambda i, order: (order[i], 0)) for cols in columns
            ],
        ),
        out_shape=[jax.ShapeDtypeStruct((4 * rows, cols), bf16) for cols in columns],
        compiler_params=pltpu.CompilerParams(vmem_limit_bytes=56 << 20),
        cost_estimate=lasting(18),
    )(order, *blocks, *weights, gain, cosine, sine)


def weight_kernel(count, packed, added, order_ref, *refs):
    xs, ds, rest = refs[: count[0]], refs[count[0] : sum(count)], list(refs[sum(count) : -1])
    total = None
    each = count[0] // count[1]
    for i, x_ref in enumerate(xs):
        rows = x_ref.shape[0]
        at = pl.ds(pl.multiple_of(order_ref[i % each] * rows, rows), rows)
        part = dot_tn(x_ref[...], ds[i // each][at])
        total = part if total is None else total + part
    if packed:
        total = dot_nt(total.astype(bf16), rest.pop(0)[...])
    if added:
        total = total + rest.pop(0)[...].astype(f32)
    refs[-1][...] = total.astype(bf16)


def weight_grad(order, xs, ds, half, place=None, more=None, tile=256):
    count = (len(xs), len(ds))
    width, cols = xs[0].shape[1], ds[0].shape[1] // 2
    places = [] if place is None else [place]
    out_cols = cols if place is None else place.shape[0]
    block = pl.BlockSpec((tile, out_cols), lambda i, _: (i, 0))
    adds = [] if more is None else [more]
    return pl.pallas_call(
        functools.partial(weight_kernel, count, bool(places), bool(adds)),
        grid_spec=pltpu.PrefetchScalarGridSpec(
            num_scalar_prefetch=1,
            grid=(width // tile,),
            in_specs=[pl.BlockSpec((x.shape[0], tile), lambda i, _: (0, i)) for x in xs]
            + [pl.BlockSpec((d.shape[0], cols), lambda i, _: (0, half)) for d in ds]
            + [whole(p) for p in places]
            + [block] * len(adds),
            out_specs=block,
        ),
        out_shape=jax.ShapeDtypeStruct((width, out_cols), bf16),
        compiler_params=pltpu.CompilerParams(vmem_limit_bytes=60 << 20),
        cost_estimate=dense(sum(d.shape[0] for d in ds), width, cols),
    )(order, *xs, *ds, *places, *adds)


PARAMS = pltpu.CompilerParams(vmem_limit_bytes=56 << 20)


def whole(a):
    return pl.BlockSpec(a.shape, lambda *_: (0,) * a.ndim)


def expand_kernel(*refs):
    blocks, (w_own, w_other, both_ref, act_ref) = refs[:4], refs[4:]
    half = pl.num_programs(0) // 2

    def run(w_ref):
        w = w_ref[...]
        for i, x_ref in enumerate(blocks):
            rows = x_ref.shape[0]
            at = slice(i * rows, (i + 1) * rows)
            both = dot_nn(x_ref[...], w)
            gate, up = both[:, :LANES], both[:, LANES:]
            both_ref[at] = both
            act_ref[at] = (gate * jax.nn.sigmoid(gate) * up).astype(bf16)

    pl.when(pl.program_id(0) < half)(lambda: run(w_own))
    pl.when(pl.program_id(0) >= half)(lambda: run(w_other))


def halves_spec(shape, axis, tiles):
    def place(at):
        return (0, at) if axis else (at, 0)

    return [
        pl.BlockSpec(shape, lambda j, *_: place(jnp.minimum(j, tiles - 1))),
        pl.BlockSpec(shape, lambda j, *_: place(jnp.maximum(j - tiles, 0))),
    ]


def expand(blocks, weights):
    rows, width = blocks[0].shape
    cols = 2 * weights[0].shape[1]
    tiles = cols // (4 * LANES)
    return pl.pallas_call(
        expand_kernel,
        grid=(2 * tiles,),
        in_specs=[whole(b) for b in blocks] + halves_spec((width, 2 * LANES), 1, tiles),
        out_specs=[
            pl.BlockSpec((4 * rows, 2 * LANES), lambda j: (0, j)),
            pl.BlockSpec((4 * rows, LANES), lambda j: (0, j)),
        ],
        out_shape=[
            jax.ShapeDtypeStruct((4 * rows, cols), f32),
            jax.ShapeDtypeStruct((4 * rows, cols // 2), bf16),
        ],
        compiler_params=PARAMS,
        cost_estimate=dense(4 * rows, width, cols),
    )(*blocks, *weights)


def expand_back_kernel(*refs):
    blocks, (both_ref, w_own, w_other, out_ref) = refs[:4], refs[4:]

    def run(g_ref):
        g = g_ref[...]
        for e, w_ref in enumerate((w_own, w_other)):
            d_act = dot_nn(g, w_ref[...])
            tiles = d_act.shape[1] // LANES
            for j in range(tiles):
                first = 2 * (e * tiles + j) * LANES
                gate = both_ref[:, first : first + LANES]
                up = both_ref[:, first + LANES : first + 2 * LANES]
                d = d_act[:, j * LANES : (j + 1) * LANES]
                sigma = jax.nn.sigmoid(gate)
                d_sigma = d * sigma
                d_gate = d_sigma * up * (1.0 + gate * (1.0 - sigma))
                out_ref[:, first : first + LANES] = d_gate.astype(bf16)
                out_ref[:, first + LANES : first + 2 * LANES] = (d_sigma * gate).astype(bf16)

    for i, ref in enumerate(blocks):
        pl.when(pl.program_id(0) == i)(functools.partial(run, ref))


def expand_back(blocks, both, weights):
    rows, width = blocks[0].shape
    cols = both.shape[1]
    return pl.pallas_call(
        expand_back_kernel,
        grid=(4,),
        in_specs=[whole(b) for b in blocks]
        + [pl.BlockSpec((rows, cols), lambda i: (i, 0))]
        + [whole(w) for w in weights],
        out_specs=pl.BlockSpec((rows, cols), lambda i: (i, 0)),
        out_shape=jax.ShapeDtypeStruct((4 * rows, cols), bf16),
        compiler_params=PARAMS,
        cost_estimate=dense(4 * rows, width, cols // 2),
    )(*blocks, both, *weights)


def shrink_kernel(order_ref, a_ref, own_ref, other_ref, *outs):
    depth = own_ref.shape[1]
    rows = outs[0].shape[0]
    own, other = own_ref[...], other_ref[...]
    for i, ref in enumerate(outs):
        at = pl.ds(pl.multiple_of(order_ref[i] * rows, rows), rows)
        out = dot_nt(a_ref[at, :depth], own) + dot_nt(a_ref[at, depth:], other)
        ref[...] = out.astype(bf16)


def shrink(order, a, weights, tile=256):
    rows, depth = a.shape
    cols = weights[0].shape[0]
    block = pl.BlockSpec((rows // 4, tile), lambda j, _: (0, j))
    return pl.pallas_call(
        shrink_kernel,
        grid_spec=pltpu.PrefetchScalarGridSpec(
            num_scalar_prefetch=1,
            grid=(cols // tile,),
            in_specs=[whole(a)] + [pl.BlockSpec((tile, depth // 2), lambda j, _: (j, 0))] * 2,
            out_specs=[block] * 4,
        ),
        out_shape=[jax.ShapeDtypeStruct((rows // 4, cols), bf16)] * 4,
        compiler_params=PARAMS,
        cost_estimate=dense(rows, depth, cols),
    )(order, a, *weights)


def grow_kernel(order_ref, *refs):
    blocks, (w_own, w_other, out_ref) = refs[:4], refs[4:]
    half = pl.num_programs(0) // 2

    def run(w_ref):
        w = w_ref[...]
        for i, x_ref in enumerate(blocks):
            rows = x_ref.shape[0]
            at = pl.ds(pl.multiple_of(order_ref[i] * rows, rows), rows)
            out_ref[at] = dot_nn(x_ref[...], w).astype(bf16)

    pl.when(pl.program_id(0) < half)(lambda: run(w_own))
    pl.when(pl.program_id(0) >= half)(lambda: run(w_other))


def grow(order, blocks, weights, tile=256):
    rows, depth = blocks[0].shape
    cols = 2 * weights[0].shape[1]
    tiles = cols // (2 * tile)
    return pl.pallas_call(
        grow_kernel,
        grid_spec=pltpu.PrefetchScalarGridSpec(
            num_scalar_prefetch=1,
            grid=(2 * tiles,),
            in_specs=[whole(b) for b in blocks] + halves_spec((depth, tile), 1, tiles),
            out_specs=pl.BlockSpec((4 * rows, tile), lambda j, _: (0, j)),
        ),
        out_shape=jax.ShapeDtypeStruct((4 * rows, cols), bf16),
        compiler_params=PARAMS,
        cost_estimate=dense(4 * rows, depth, cols),
    )(order, *blocks, *weights)


def by_rows(kernel, ins, outs, vectors=()):
    rows, width = outs[0].shape
    tile = rows // 4 if rows % 64 == 0 else rows
    specs, arrays = [whole(v) for v in vectors], list(vectors)
    for one in ins:
        if not isinstance(one, tuple) and one.ndim == 3:
            one = (one, 0)
        if isinstance(one, tuple):
            one, at = one
            specs.append(pl.BlockSpec((None, tile, width), lambda i, at=at: (at, i, 0)))
        else:
            specs.append(pl.BlockSpec((tile, width), lambda i: (i, 0)))
        arrays.append(one)
    return pl.pallas_call(
        kernel,
        grid=(rows // tile,),
        in_specs=specs,
        out_specs=[pl.BlockSpec((tile, width), lambda i: (i, 0))] * len(outs),
        out_shape=outs,
        compiler_params=PARAMS,
        cost_estimate=lasting(5.5),
    )(*arrays)


def wide_sum(refs):
    total = refs[0][...].astype(f32)
    for ref in refs[1:]:
        total = total + ref[...].astype(f32)
    return total


def norm_kernel(gain_ref, *refs):
    residual = wide_sum(refs[:-2])
    refs[-2][...] = residual
    refs[-1][...] = (residual * rms_scale(residual) * gain_ref[...]).astype(bf16)


def norm_back_kernel(count, gain_ref, g_ref, residual_ref, *refs):
    residual = residual_ref[...].astype(f32)
    scale = rms_scale(residual)
    hat = residual * scale
    d_hat = wide_sum(refs[:count]) * gain_ref[...]
    inner = jnp.mean(d_hat * hat, axis=-1, keepdims=True)
    out = g_ref[...].astype(f32) + scale * (d_hat - hat * inner)
    for ref in refs[count:]:
        ref[...] = out.astype(ref.dtype)


def sum_kernel(*refs):
    refs[-1][...] = wide_sum(refs[:-1]).astype(refs[-1].dtype)


def shaped(a, kind):
    return jax.ShapeDtypeStruct(a.shape, kind)


def finish_mlp_kernel(hidden, rep_ref, mine_ref, other_ref, wg_ref, wu_ref, *outs):
    gate_ref, up_ref, down_ref, sum_ref = outs
    t = pl.program_id(0)
    wide = gate_ref.shape[1]
    own = jnp.broadcast_to((t // INNER == rep_ref[0]).astype(f32), (1, LANES))
    total = None
    for j in range(wide // LANES):
        cut = slice(j * LANES, (j + 1) * LANES)
        keep = t * wide + j * LANES < hidden

        def taken(column):
            at = slice(column * LANES, (column + 1) * LANES)
            mine, other = mine_ref[0, :, at].astype(f32), other_ref[0, :, at].astype(f32)
            return jnp.where(own > 0.5, mine, other)

        gate, up = taken(2 * j), taken(2 * j + 1)
        gate_ref[:, cut] = gate
        up_ref[:, cut] = up
        down_ref[:, cut] = taken(2 * (wide // LANES) + j)
        part = wg_ref[:, cut].astype(f32) * gate + wu_ref[:, cut].astype(f32) * up
        part = jnp.where(jnp.broadcast_to(keep, part.shape), part, 0.0)
        total = part if total is None else total + part

    @pl.when(t == 0)
    def _():
        sum_ref[...] = jnp.zeros_like(sum_ref)

    sum_ref[...] += total


def finish_mlp(rep, mine, other, w_gate, w_up):
    _, rows, cols = mine.shape
    wide = cols // 3
    hidden = w_gate.shape[1]
    share = pl.BlockSpec((1, rows, cols), lambda t, *_: (t % INNER, 0, 0))
    block = pl.BlockSpec((rows, wide), lambda t, *_: (0, t))
    return pl.pallas_call(
        functools.partial(finish_mlp_kernel, hidden),
        grid_spec=pltpu.PrefetchScalarGridSpec(
            num_scalar_prefetch=1,
            grid=(SHARE,),
            in_specs=[share, share, block, block],
            out_specs=[block, block, block, pl.BlockSpec((rows, LANES), lambda t, *_: (0, 0))],
        ),
        out_shape=[jax.ShapeDtypeStruct((rows, hidden), f32)] * 3
        + [jax.ShapeDtypeStruct((rows, LANES), f32)],
        compiler_params=PARAMS,
        cost_estimate=lasting(13),
    )(rep, mine, other, w_gate, w_up)


def after(a, *others):
    return lax.optimization_barrier((a, *others))[0]


ORDER = (
    "Wa", "ca", "na", "xd0", "Wm", "cm", "xr0", "xz0", "tb", "wq", "P0", "xd1", "gd0", "wo", "nm",
    "xr1", "T0", "O0", "xz1", "P1", "Oa0", "gr0", "T1", "N0", "nd0", "gz0", "O1", "nr0", "gd1",
    "wg", "Oa1", "nz0", "E0", "N1", "wd", "B0", "nd1", "gr1", "X0", "nr1", "nz1", "E1", "gz1",
    "S0", "B1", "Xa0", "X1", "M0", "Wdo", "Xa1", "Wgo", "bd0", "M1", "bd1", "Wd", "Wg", "br1",
    "br0", "S1", "bz0", "A0", "Q0", "J0", "bz1", "Y0", "A1", "Sa1", "Woo", "Sa0", "out1", "Q1",
    "out0", "J1", "Ya0", "Y1", "F0", "Wo", "Wqo", "Ya1", "gpm", "gcm", "Wq", "F1", "gpo", "glm",
    "gco", "gpa", "gca", "glo", "gla", "jm", "jo", "ja",
)


class Place:
    def __init__(self):
        self.parts = lax.axis_size("dp")
        self.ctx = lax.axis_size("ctx")
        self.outer = self.ctx // INNER
        self.rep = lax.axis_index("rep")
        self.part = lax.axis_index("dp")
        self.at_ctx = lax.axis_index("ctx")
        self.inner = self.at_ctx % INNER
        self.hi = self.at_ctx // INNER
        self.core = self.inner % 2
        self.mid = self.inner // 2
        self.last = None
        self.order = jnp.where(self.core == 0, jnp.array([0, 2, 1, 3]), jnp.arange(4)).astype(jnp.int32)

    def run(self, work, *inputs, waits=()):
        held = () if self.last is None else (self.last,)
        inputs, _, _ = lax.optimization_barrier((inputs, held, tuple(waits)))
        out = work(*inputs)
        self.last = jax.tree.leaves(out)[-1]
        return out

    def gate(self, a):
        return a if self.last is None else after(a, self.last)

    def flip(self, a, bits):
        return lax.ppermute(a, "ctx", [(i, i ^ bits) for i in range(self.ctx)])

    def swap_rep(self, a):
        return lax.ppermute(a, "rep", [(0, 1), (1, 0)])

    def shift_hi(self, a, by):
        pairs = [(i, (i + INNER * by) % self.ctx) for i in range(self.ctx)]
        return lax.ppermute(a, "ctx", pairs)


    def gather_rows(self, piece):
        whole = lax.all_gather(piece, "dp", axis=0, tiled=True)
        if self.outer > 1:
            whole = jnp.concatenate(
                [whole] + [self.shift_hi(whole, j) for j in range(1, self.outer)], axis=0
            )
        return whole

    def reduce_rows(self, whole):
        whole = whole.reshape((self.outer, -1) + whole.shape[1:])
        mine = whole[0]
        for j in range(1, self.outer):
            mine = mine + self.shift_hi(whole[j], -j)
        return lax.psum_scatter(mine, "dp", scatter_dimension=0, tiled=True)

    def by_core(self, keep, got):
        return jnp.where(self.core == 0, jnp.stack([keep, got]), jnp.stack([got, keep]))

    def by_mid(self, keep, got):
        return jnp.where(self.mid == 0, jnp.stack([keep, got]), jnp.stack([got, keep]))

    def pick(self, a, index, axis):
        return lax.dynamic_index_in_dim(a, index, axis, keepdims=False)

    def spread_core(self, parts):
        return self.flip(self.gate(self.pick(parts, 1 - self.core, 1)), 1)

    def spread_mid(self, parts, got):
        both = self.run(
            lambda parts, got: self.by_core(self.pick(parts, self.core, 1), got), parts, got
        )
        return both, self.flip(self.gate(self.pick(both, 1 - self.mid, 1)), 2)

    def spread_close(self, both, got):
        return self.by_mid(self.pick(both, self.mid, 1), got)

    def join_shares(self, mine, other):
        low = jnp.where(self.rep == 0, mine, other)
        high = jnp.where(self.rep == 0, other, mine)
        return jnp.concatenate([low, high], axis=0)


    def to_own_order(self, a):
        if self.outer == 1:
            return a
        n, outer = self.parts, self.outer
        width = a.shape[-1] // (n * outer)
        cut = []
        for j in range(outer):
            for part in range(n):
                block = part * outer + (self.hi - j) % outer
                cut.append(lax.dynamic_slice_in_dim(a, block * width, width, a.ndim - 1))
        return jnp.concatenate(cut, axis=-1)

    def to_natural_order(self, a):
        if self.outer == 1:
            return a
        n, outer = self.parts, self.outer
        width = a.shape[-1] // (n * outer)
        cut = []
        for part in range(n):
            for hi in range(outer):
                block = ((self.hi - hi) % outer) * n + part
                cut.append(lax.dynamic_slice_in_dim(a, block * width, width, a.ndim - 1))
        return jnp.concatenate(cut, axis=-1)


    def by_core_pairs(self, rep_core):
        pairs = []
        for r in range(2):
            for i in range(self.ctx):
                to = (1 - r) * self.ctx + i if i % 2 == rep_core else r * self.ctx + (i ^ 2)
                pairs.append((r * self.ctx + i, to))
        return pairs

    def send_first(self, a):
        return lax.ppermute(a, ("rep", "ctx"), self.by_core_pairs(0))

    def send_second(self, a):
        return lax.ppermute(a, ("rep", "ctx"), self.by_core_pairs(1))

    def gather_start(self, a):
        a = self.gate(a)
        return self.send_first(a), self.send_second(a)

    def gather_relay(self, a, first, second):
        first, second = self.run(lambda *both: both, first, second)
        return a, first, second, self.send_second(first)

    def gather_close(self, *blocks):
        return self.run(lambda *blocks: blocks, *blocks)


    def reduce_start(self, here, to_first, to_second, far):
        return here, to_first, self.send_second(self.gate(far)), self.send_second(self.gate(to_second))

    def reduce_send(self, here, to_first, got, from_second):
        from_second, to_first = self.run(
            lambda second, *parts: (second, by_rows(sum_kernel, parts, [shaped(got, bf16)])[0]),
            from_second,
            to_first,
            got,
        )
        return here, from_second, self.send_first(to_first)

    def natural_rows(self, a):
        a = jnp.where(self.core == 0, a, jnp.flip(a, 0))
        a = jnp.where(self.mid == 0, a, jnp.flip(a, 2))
        return jnp.moveaxis(a, 0, 2)

    def relative_rows(self, a):
        a = jnp.moveaxis(a, 2, 0)
        a = jnp.where(self.core == 0, a, jnp.flip(a, 0))
        return jnp.where(self.mid == 0, a, jnp.flip(a, 2))


    def gather_outer(self, a, axis):
        if self.outer == 1:
            return a
        shape = a.shape[:axis] + (self.outer,) + a.shape[axis:]
        got = jnp.zeros(shape, a.dtype)
        for j in range(self.outer):
            one = self.shift_hi(a, j) if j else a
            got = lax.dynamic_update_index_in_dim(got, one, (self.hi - j) % self.outer, axis)
        return got.reshape(a.shape[:axis] + (-1,) + a.shape[axis + 1 :])

    def reduce_outer(self, a, axis):
        if self.outer == 1:
            return a
        a = a.reshape(a.shape[:axis] + (self.outer, -1) + a.shape[axis + 1 :]).astype(bf16)
        total = None
        for j in range(self.outer):
            one = lax.dynamic_index_in_dim(a, (self.hi + j) % self.outer, axis, keepdims=False)
            one = self.shift_hi(one, j) if j else one
            total = one.astype(f32) if total is None else total + one.astype(f32)
        return total


def place_matrix(shape, pairs):
    row = lax.broadcasted_iota(jnp.int32, shape, 0)
    col = lax.broadcasted_iota(jnp.int32, shape, 1)
    hit = jnp.zeros(shape, jnp.bool_)
    for at_row, at_col, width in pairs:
        hit |= (row - at_row == col - at_col) & (row >= at_row) & (row < at_row + width)
    return hit.astype(bf16)


def head_halves(row, col):
    return [(row + i * HALF, col + i * (LANES // 2), HALF) for i in range(2)]


def half_of(w, rep):
    cols = w.shape[1] // 2
    return lax.dynamic_slice_in_dim(w, rep * cols, cols, 1)


def join_columns(by_share):
    return jnp.concatenate(list(by_share), axis=1)


def half_even(w, rep, wide):
    w = jnp.pad(w, ((0, 0), (0, SHARE * wide - w.shape[1])))
    return lax.dynamic_slice_in_dim(w, rep * INNER * wide, INNER * wide, 1)


def alternate(gate, up):
    tiles = gate.shape[1] // LANES
    cut = [one[:, j * LANES : (j + 1) * LANES] for j in range(tiles) for one in (gate, up)]
    return jnp.concatenate(cut, axis=1)


def by_position(a, axis, half_rows):
    lead = a.shape[:axis]
    a = a.reshape(lead + (-1, 2, half_rows) + a.shape[axis + 1 :])
    early = lax.index_in_dim(a, 0, axis + 1, keepdims=False)
    late = jnp.flip(lax.index_in_dim(a, 1, axis + 1, keepdims=False), axis)
    both = jnp.concatenate([early, late], axis=axis)
    return both.reshape(lead + (-1,) + both.shape[axis + 2 :])


def by_storage(a, axis, half_rows):
    lead = a.shape[:axis]
    a = a.reshape(lead + (2, -1, half_rows) + a.shape[axis + 1 :])
    early = lax.index_in_dim(a, 0, axis, keepdims=False)
    late = jnp.flip(lax.index_in_dim(a, 1, axis, keepdims=False), axis)
    both = jnp.stack([early, late], axis=axis + 1)
    return both.reshape(lead + (-1,) + both.shape[axis + 3 :])


def body(
    tokens,
    cotangent,
    segments,
    attn_gain,
    w_query,
    w_key,
    w_value,
    w_out,
    mlp_gain,
    w_gate,
    w_up,
    w_down,
):
    at = Place()
    micro_count, local_batch, rows, model_width = tokens.shape
    streams = micro_count * local_batch
    seq_length = rows * at.ctx
    half_rows = rows // 2
    own_rows = w_query.shape[0]
    hidden = w_gate.shape[1]
    wide = round_up(-(-hidden // SHARE), LANES)
    heads_wide = GROUP * LANES

    x_own = [at.to_own_order(one) for one in tokens.reshape(streams, rows, model_width)]
    g_own = [at.to_own_order(one) for one in cotangent.reshape(streams, rows, model_width)]
    every = range(streams)
    qkv_wide = heads_wide + 2 * LANES
    q_cols, k_cols = GROUP * HEAD_DIM, HEAD_DIM
    qkv_cols = round_up(q_cols + 2 * k_cols + 2, LANES)
    o_cols = round_up(q_cols, LANES)
    qkv_place = place_matrix(
        (qkv_cols, qkv_wide),
        [
            pair
            for g in range(GROUP + 1)
            for pair in head_halves(g * HEAD_DIM, g * LANES)
        ]
        + [(q_cols + k_cols, heads_wide + LANES, HEAD_DIM)],
    )
    o_place = place_matrix(
        (o_cols, heads_wide), [(g * HEAD_DIM, g * LANES, HEAD_DIM) for g in range(GROUP)]
    )
    gain_place = place_matrix((8, qkv_cols), [(0, q_cols + 2 * k_cols, 2)])

    def attn_shares(w_query, w_key, w_value, w_out, attn_gain, mlp_gain):
        both = jnp.stack([attn_gain, mlp_gain], axis=1)
        gap = jnp.zeros((own_rows, qkv_cols - q_cols - 2 * k_cols - 2), bf16)
        gap_o = jnp.zeros((own_rows, o_cols - q_cols), bf16)
        w_query, w_key, w_value, w_out = (
            half_of(w, at.rep) for w in (w_query, w_key, w_value, w_out)
        )
        shares = [
            jnp.concatenate(
                [
                    w_query[:, i * q_cols : (i + 1) * q_cols],
                    w_key[:, i * k_cols : (i + 1) * k_cols],
                    w_value[:, i * k_cols : (i + 1) * k_cols],
                    both,
                    gap,
                    w_out[:, i * q_cols : (i + 1) * q_cols],
                    gap_o,
                ],
                axis=1,
            )
            for i in range(INNER)
        ]
        return jnp.stack(shares).reshape(2, 2, own_rows, -1)

    def mlp_shares(*ws):
        gate, up, down = (half_even(w, at.rep, wide) for w in ws)
        shares = []
        for i in range(INNER):
            cut = slice(i * wide, (i + 1) * wide)
            shares.append(
                jnp.concatenate([alternate(gate[:, cut], up[:, cut]), down[:, cut]], axis=1)
            )
        return jnp.stack(shares).reshape(2, 2, own_rows, -1)

    positions = true_positions(seq_length, at.ctx)
    rel_pos = jnp.stack(
        [
            lax.dynamic_slice_in_dim(positions, (at.at_ctx ^ (2 * m)) * rows, rows)
            for m in range(2)
        ]
    )
    bases = rel_pos.reshape(-1, half_rows)[:, 0]
    frequency = rope_base ** (-2.0 * jnp.arange(HALF, dtype=f32) / HEAD_DIM)
    angles = rel_pos.reshape(2, rows, 1).astype(f32) * frequency
    gap = jnp.zeros((2, rows, LANES // 2 - HALF), f32)
    cos_half, sin_half = jnp.cos(angles), jnp.sin(angles)
    cosine = jnp.concatenate([cos_half, gap, cos_half, gap], axis=2)
    sine = jnp.concatenate([-sin_half, gap, sin_half, gap], axis=2)
    own_segments = segments.reshape(streams, seq_length)
    all_segments = jnp.stack([own_segments, at.swap_rep(own_segments)], axis=1)
    seg_k = by_position(all_segments, 2, half_rows)[..., None]
    seg_q = jnp.stack(
        [
            lax.dynamic_slice_in_dim(all_segments, (at.at_ctx ^ (2 * m)) * rows, rows, 2)
            for m in range(2)
        ],
        axis=2,
    ).reshape(streams, 2, -1, 1, half_rows)

    cosine_sub = cosine.reshape(-1, half_rows, LANES)
    sine_sub = sine.reshape(-1, half_rows, LANES)
    lowest = jnp.min(seg_q, axis=(3, 4))
    lows = jnp.sum(seg_k[:, :, None, :, 0] < lowest[..., None], axis=3, dtype=jnp.int32)
    lows = lows.reshape(streams, -1)
    tables = (bases, cosine, sine, cosine_sub, sine_sub, seg_q, seg_k, lows)

    def swap_shares(kv):
        half = kv.shape[-1] // 2
        return jnp.concatenate([kv[..., half:], kv[..., :half]], axis=-1)

    def attention_part(queries, kv, kv_got, bases, lows, seg_q, seg_k):
        queries = queries.reshape(2, 4, half_rows, -1)
        kv = jnp.stack([kv, swap_shares(kv_got)]).reshape(2, 2, 2, rows, -1)
        kv = at.gather_outer(at.natural_rows(kv).reshape(2, INNER * rows, -1), 1)
        kv = by_position(kv, 1, half_rows)
        kv_t = kv.transpose(0, 2, 1)
        attended, lse = attend(bases, lows, queries, kv, kv_t, seg_q, seg_k)
        return queries, kv, kv_t, lse, attended.reshape(4 * rows, -1)

    def attention_back(
        d_attended, queries, kv, kv_t, lse, bases, lows, cos_sub, sin_sub, seg_q, seg_k
    ):
        dq, dk, dv = attend_back(
            bases,
            lows,
            queries,
            kv,
            kv_t,
            seg_q,
            seg_k,
            d_attended.reshape(queries.shape),
            lse,
            cos_sub,
            sin_sub,
        )
        parts = [d[..., e * LANES : (e + 1) * LANES] for e in range(2) for d in (dk, dv)]
        d_kv = jnp.concatenate(parts, axis=2)
        d_kv = at.reduce_outer(by_storage(d_kv, 1, half_rows), 1)
        d_kv = at.relative_rows(d_kv.reshape(2, 2, 2, rows, -1)).reshape(2, 4 * rows, -1)
        return dq.reshape(4 * rows, -1), d_kv[0], swap_shares(d_kv[1]).astype(bf16)

    def attention_join(dq, d_kv, got, cosine, sine):
        d_kv = d_kv + got.astype(f32)
        cosine, sine = (t.reshape(1, 2 * rows, LANES) for t in (cosine, sine))
        parts = []
        for e in range(2):
            dk = d_kv[:, 2 * e * LANES : (2 * e + 1) * LANES].reshape(2, 2 * rows, LANES)
            dk = dk * cosine - jnp.roll(dk, LANES // 2, axis=2) * sine
            parts.append(dq[:, e * heads_wide : (e + 1) * heads_wide])
            parts.append(dk.reshape(4 * rows, LANES).astype(bf16))
            parts.append(d_kv[:, (2 * e + 1) * LANES : (2 * e + 2) * LANES].astype(bf16))
        return jnp.concatenate(parts, axis=1)

    def second_norm(x, gain, *parts):
        return by_rows(norm_kernel, [x, *parts], [shaped(x, f32), shaped(x, bf16)], [gain])

    def second_norm_back(g, residual, gain, *parts):
        return by_rows(
            functools.partial(norm_back_kernel, len(parts)),
            [g, residual, *parts],
            [shaped(g, f32), shaped(g, bf16)],
            [gain],
        )

    def first_norm_back(x, d_residual, gain, *parts):
        return by_rows(
            functools.partial(norm_back_kernel, len(parts)),
            [d_residual, x, *parts],
            [shaped(x, f32)],
            [gain],
        )[0]

    def add_up(*parts):
        return by_rows(sum_kernel, parts, [shaped(parts[0], bf16)])[0]

    def expand_weights(w, gain_place, qkv_place):
        return dot_nt(gain_place, w), dot_nn(w, qkv_place, bf16)

    def grad_parts(*parts):
        return jnp.concatenate(parts, axis=1).reshape(2, 2, own_rows, -1)

    def close_rows(*cuts):
        def work(both, got):
            whole_rows = at.spread_close(both, got).reshape(INNER * own_rows, -1)
            return [whole_rows[:, a:b] for a, b in cuts]

        return work

    def close_shares(both, got):
        return at.spread_close(both, got).reshape(INNER, own_rows, -1)

    v = {}
    task = {}

    def put(name, work):
        task[name] = lambda: v.__setitem__(name, work())

    def gather_tasks(p, i, source):
        put(p + "d" + i, lambda: at.gather_start(source()))
        put(p + "r" + i, lambda: at.gather_relay(source(), *v[p + "d" + i]))
        put(p + "z" + i, lambda: at.gather_close(*v[p + "r" + i]))

    def reduce_tasks(p, i, order, left, right):
        put(p + i, lambda: at.reduce_start(*at.run(shrink, order, left(), right())))
        put(p + "a" + i, lambda: at.reduce_send(*v[p + i]))

    def grad_tasks(name, order, lefts, rights, place=None):
        def grad(half, *more):
            xs, ds = lefts(), rights()
            count = len(xs) + len(ds)
            return at.run(
                lambda order, *parts: weight_grad(
                    order, parts[: len(xs)], parts[len(xs) : count], half, place, *parts[count:]
                ),
                order,
                *xs,
                *ds,
                *more,
            )

        put(name + "o", lambda: at.flip(grad(1), 1))
        put(name, lambda: at.reduce_rows(grad(0, v[name + "o"])))

    def start_exchange(work, *parts):
        whole_parts = at.run(work, *parts)
        return whole_parts, at.spread_core(whole_parts)

    def project_task(i):
        normed, queries, kv = at.run(project, at.order, v[f"xz{i}"], v["wq"], v["gain"][0], *v["tb"][1:3])
        return normed, queries, kv, at.flip(kv, 1)

    def back_task(i):
        dq, d_kv, sent = at.run(
            attention_back,
            v[f"A{i}"],
            *v[f"T{i}"][:4],
            v["tb"][0],
            v["tb"][7][i],
            *v["tb"][3:5],
            v["tb"][5][i],
            v["tb"][6][i],
        )
        return dq, d_kv, at.flip(sent, 1)

    as_is = jnp.arange(4, dtype=jnp.int32)
    every = range(streams)
    for i in every:
        one = str(i)
        gather_tasks("x", one, lambda i=i: x_own[i])
        gather_tasks("g", one, lambda i=i: g_own[i])
        gather_tasks("n", one, lambda i=i: v[f"N{i}"][1])
        gather_tasks("b", one, lambda i=i: v[f"M{i}"][1])
        put(f"P{i}", lambda i=i: project_task(i))
        put(
            f"T{i}",
            lambda i=i: at.run(
                attention_part, *v[f"P{i}"][1:], v["tb"][0], v["tb"][7][i], v["tb"][5][i], v["tb"][6][i]
            ),
        )
        reduce_tasks("O", one, at.order, lambda i=i: v[f"T{i}"][4], lambda: v["wo"])
        put(f"N{i}", lambda i=i: at.run(second_norm, x_own[i], v["gain"][1], *v[f"Oa{i}"]))
        put(f"E{i}", lambda i=i: at.run(expand, v[f"nz{i}"], v["wg"]))
        reduce_tasks("S", one, as_is, lambda i=i: v[f"E{i}"][1], lambda: v["wd"])
        put(f"out{i}", lambda i=i: at.run(add_up, v[f"N{i}"][0], *v[f"Sa{i}"]))
        put(f"B{i}", lambda i=i: at.run(expand_back, v[f"gz{i}"], v[f"E{i}"][0], v["wd"]))
        reduce_tasks("X", one, as_is, lambda i=i: v[f"B{i}"], lambda: v["wg"])
        put(
            f"M{i}",
            lambda i=i: at.run(
                second_norm_back, g_own[i], v[f"N{i}"][0], v["gain"][1], *v[f"Xa{i}"]
            ),
        )
        put(f"A{i}", lambda i=i: at.run(grow, at.order, v[f"bz{i}"], v["wo"]))
        put(f"Q{i}", lambda i=i: back_task(i))
        put(f"J{i}", lambda i=i: at.run(attention_join, *v[f"Q{i}"], *v["tb"][1:3]))
        reduce_tasks("Y", one, at.order, lambda i=i: v[f"J{i}"], lambda: v["wq"])
        put(
            f"F{i}",
            lambda i=i: at.run(
                first_norm_back, x_own[i], v[f"M{i}"][0], v["gain"][0], *v[f"Ya{i}"]
            ),
        )
    put("tb", lambda: at.run(lambda *parts: parts, *tables))
    put(
        "Wa",
        lambda: start_exchange(
            attn_shares, w_query, w_key, w_value, w_out, attn_gain, mlp_gain
        ),
    )
    put("ca", lambda: at.spread_mid(*v["Wa"]))
    put(
        "na",
        lambda: [
            at.gather_rows(one)
            for one in at.run(
                close_rows((0, qkv_cols), (qkv_cols, qkv_cols + o_cols)), *v["ca"]
            )
        ],
    )
    put("Wm", lambda: start_exchange(mlp_shares, w_gate, w_up, w_down))
    put("cm", lambda: at.spread_mid(*v["Wm"]))
    put(
        "nm",
        lambda: [
            at.gather_rows(one)
            for one in at.run(close_rows((0, 2 * wide), (2 * wide, 3 * wide)), *v["cm"])
        ],
    )

    def expanded_weights():
        gains, w = at.run(expand_weights, v["na"][0], gain_place, qkv_place)
        v["gain"] = (gains[0:1], gains[1:2])
        return w, at.flip(w, 1)

    def expanded_out():
        w = at.run(lambda w, place: dot_nn(w, place, bf16), v["na"][1], o_place)
        return w, at.flip(w, 1)

    put("wq", expanded_weights)
    put("wo", expanded_out)
    put("wg", lambda: (v["nm"][0], at.flip(at.gate(v["nm"][0]), 1)))
    put("wd", lambda: (v["nm"][1], at.flip(at.gate(v["nm"][1]), 1)))

    def over_blocks(p):
        return lambda: [one for i in every for one in v[f"{p}z{i}"]]

    grad_tasks("Wd", as_is, over_blocks("g"), lambda: [v[f"E{i}"][1] for i in every])
    grad_tasks("Wg", as_is, over_blocks("n"), lambda: [v[f"B{i}"] for i in every])
    grad_tasks(
        "Wo", at.order, over_blocks("b"), lambda: [v[f"T{i}"][4] for i in every], o_place
    )
    grad_tasks(
        "Wq",
        as_is,
        lambda: [v[f"P{i}"][0] for i in every],
        lambda: [v[f"J{i}"] for i in every],
        qkv_place,
    )
    put("gpm", lambda: start_exchange(grad_parts, v["Wg"], v["Wd"]))
    put("gcm", lambda: at.spread_mid(*v["gpm"]))

    def swapped(both, got):
        mine = at.run(close_shares, both, got)
        return mine, at.swap_rep(mine)

    put("glm", lambda: swapped(*v["gcm"]))
    put("gpa", lambda: start_exchange(grad_parts, v["Wq"]))
    put("gca", lambda: at.spread_mid(*v["gpa"]))
    put("gla", lambda: swapped(*v["gca"]))
    put("gpo", lambda: start_exchange(grad_parts, v["Wo"]))
    put("gco", lambda: at.spread_mid(*v["gpo"]))
    put("glo", lambda: swapped(*v["gco"]))
    rep_number = at.rep.astype(jnp.int32).reshape(1)
    put("jm", lambda: at.run(finish_mlp, rep_number, *v["glm"], w_gate, w_up))

    def grad_columns(*cuts):
        def work(mine, other):
            shares = at.join_shares(mine, other)
            return [join_columns(shares[..., a:b]).astype(f32) for a, b in zip(cuts, cuts[1:])]

        return work

    ends = (0, q_cols, q_cols + k_cols, q_cols + 2 * k_cols)
    put("ja", lambda: at.run(grad_columns(*ends), *v["gla"]))
    put("jo", lambda: at.run(grad_columns(0, q_cols), *v["glo"]))
    for name in ORDER:
        task[name]()
    outputs = [at.to_natural_order(v[f"out{i}"]) for i in every]
    input_grads = [at.to_natural_order(v[f"F{i}"]) for i in every]
    gate_grad, up_grad, down_grad, mlp_sums = v["jm"]
    query_grad, key_grad, value_grad = v["ja"]
    (out_grad,) = v["jo"]

    def along(w, grad):
        return jnp.sum(w.astype(f32) * grad, axis=1)

    attn_gain_grad = (
        along(w_query, query_grad) + along(w_key, key_grad) + along(w_value, value_grad)
    ) / attn_gain.astype(f32)
    mlp_gain_grad = jnp.sum(mlp_sums, axis=1) / mlp_gain.astype(f32)

    return (
        jnp.stack(outputs).reshape(tokens.shape),
        jnp.stack(input_grads).reshape(tokens.shape),
        attn_gain_grad,
        query_grad,
        key_grad,
        value_grad,
        out_grad,
        mlp_gain_grad,
        gate_grad,
        up_grad,
        down_grad,
    )


def solution(mesh):
    sequence = P(None, ("rep", "dp"), "ctx", None)
    rows = P(("dp", "ctx"), None)
    vector = P(("dp", "ctx"))
    return jax.shard_map(
        body,
        mesh=mesh,
        in_specs=(
            sequence,
            sequence,
            P(None, ("rep", "dp"), None),
            vector,
            rows,
            rows,
            rows,
            rows,
            vector,
            rows,
            rows,
            rows,
        ),
        out_specs=(sequence, sequence, vector, rows, rows, rows, rows, vector, rows, rows, rows),
        check_vma=False,
    )
```

```python
import functools

import jax
import jax.numpy as jnp
from jax import lax
from jax.experimental import pallas as pl
from jax.experimental.pallas import tpu as pltpu
from jax.sharding import PartitionSpec as P

D = 2560
HEADS = 32
KV_HEADS = 8
HEAD_DIM = 80
GROUP = HEADS // KV_HEADS
HALF = HEAD_DIM // 2
LANES = 128
SHARE = 8
INNER = 4

rope_base = 10000.0
norm_epsilon = 1e-05
log2_e = 1.4426950408889634
bf16 = jnp.bfloat16
f32 = jnp.float32


SPEED = 1e10


def lasting(microseconds):
    return pl.CostEstimate(flops=int(microseconds * SPEED), transcendentals=0, bytes_accessed=1)


def dense(rows, depth, cols):
    return lasting(4 + 2 * rows * depth * cols / 9.4e8)


def round_up(value, unit):
    return -(-value // unit) * unit


def true_positions(seq_length, ctx_parts):
    span_rows = seq_length // ctx_parts
    half_rows = span_rows // 2
    stored_index = jnp.arange(seq_length, dtype=jnp.int32)
    device_of = stored_index // span_rows
    within_rows = stored_index % span_rows
    block_of = jnp.where(within_rows < half_rows, device_of, 2 * ctx_parts - 1 - device_of)
    return block_of * half_rows + within_rows % half_rows


def dot_nn(left, right, out=f32):
    return lax.dot_general(left, right, (((1,), (0,)), ((), ())), preferred_element_type=out)


def dot_nt(left, right, out=f32):
    return lax.dot_general(left, right, (((1,), (1,)), ((), ())), preferred_element_type=out)


def dot_tn(left, right, out=f32):
    return lax.dot_general(left, right, (((0,), (0,)), ((), ())), preferred_element_type=out)


def rms_scale(values):
    return lax.rsqrt(jnp.mean(values * values, axis=-1, keepdims=True) + norm_epsilon)


def stack_heads(block):
    return jnp.concatenate(
        [block[:, g * LANES : (g + 1) * LANES] for g in range(GROUP)], axis=0
    )


def bias_of(seg_k, seg_q, first, base):
    rows, cols = seg_k.shape[0], seg_q.shape[1]
    key_pos = first + lax.broadcasted_iota(jnp.int32, (rows, cols), 0)
    query_pos = base + lax.broadcasted_iota(jnp.int32, (rows, cols), 1)
    bias = jnp.where((seg_k == seg_q) & (key_pos <= query_pos), 0.0, -1e30).astype(f32)
    return jnp.concatenate([bias] * GROUP, axis=1)


def limits(base_ref, low_ref, half_rows, chunk):
    at = pl.program_id(0) * pl.num_programs(2) + pl.program_id(2)
    base = base_ref[pl.program_id(2)]
    return base, low_ref[at] // chunk, (base + half_rows - 1) // chunk


def forward_kernel(
    chunk, base_ref, low_ref, q_ref, k_ref, vt_ref, segq_ref, segk_ref, o_ref, lse_ref, s_ref
):
    half_rows = q_ref.shape[2]
    length = k_ref.shape[1]
    base, low, high = limits(base_ref, low_ref, half_rows, chunk)
    scale = HEAD_DIM**-0.5 * log2_e

    def run(seen):
        queries = stack_heads(q_ref[0, 0])
        seg_q = segq_ref[0, 0]
        top = None
        for c in seen:
            at = pl.ds(c * chunk, chunk)
            s = dot_nt(k_ref[0, at], queries) * scale
            s = s + bias_of(segk_ref[0, at], seg_q, c * chunk, base)
            s_ref[at] = s
            now = jnp.max(s, axis=0, keepdims=True)
            top = now if top is None else jnp.maximum(top, now)
        total = None
        mixed = None
        for c in seen:
            at = pl.ds(c * chunk, chunk)
            p = jnp.exp2(s_ref[at] - top)
            now = jnp.sum(p, axis=0, keepdims=True)
            total = now if total is None else total + now
            part = dot_nn(vt_ref[0, :, at], p.astype(bf16))
            mixed = part if mixed is None else mixed + part
        out = (mixed / total).T.astype(bf16)
        for g in range(GROUP):
            o_ref[0, 0, :, g * LANES : (g + 1) * LANES] = out[g * half_rows : (g + 1) * half_rows]
        lse_ref[0, 0, 0] = top + jnp.log2(total)

    for one in range(length // chunk):
        for two in range(one, length // chunk):
            seen = range(one, two + 1)
            pl.when((low == one) & (high == two))(functools.partial(run, seen))


def backward_kernel(
    chunk,
    base_ref,
    low_ref,
    q_ref,
    k_ref,
    kt_ref,
    v_ref,
    segq_ref,
    segk_ref,
    do_ref,
    lse_ref,
    cos_ref,
    sin_ref,
    dq_ref,
    dk_ref,
    dv_ref,
    p_ref,
    dp_ref,
):
    half_rows = q_ref.shape[2]
    length = k_ref.shape[1]
    base, low, high = limits(base_ref, low_ref, half_rows, chunk)
    scale = HEAD_DIM**-0.5

    @pl.when(pl.program_id(2) == 0)
    def _():
        dk_ref[...] = jnp.zeros_like(dk_ref)
        dv_ref[...] = jnp.zeros_like(dv_ref)

    def run(seen):
        queries = stack_heads(q_ref[0, 0])
        grads = stack_heads(do_ref[0, 0])
        seg_q = segq_ref[0, 0]
        log_total = lse_ref[0, 0, 0]
        inner = None
        for c in seen:
            at = pl.ds(c * chunk, chunk)
            s = dot_nt(k_ref[0, at], queries) * (scale * log2_e)
            s = s + bias_of(segk_ref[0, at], seg_q, c * chunk, base)
            p = jnp.exp2(s - log_total)
            dp = dot_nt(v_ref[0, at], grads)
            dv_ref[0, at] += dot_nn(p.astype(bf16), grads)
            now = jnp.sum(p * dp, axis=0, keepdims=True)
            inner = now if inner is None else inner + now
            p_ref[at] = p
            dp_ref[at] = dp
        dq = None
        for c in seen:
            at = pl.ds(c * chunk, chunk)
            ds = (p_ref[at] * (dp_ref[at] - inner)).astype(bf16)
            dk_ref[0, at] += dot_nn(ds, queries) * scale
            part = dot_nn(kt_ref[0, :, at], ds)
            dq = part if dq is None else dq + part
        dq = (dq * scale).T
        cosine, sine = cos_ref[0], sin_ref[0]
        for g in range(GROUP):
            one = dq[g * half_rows : (g + 1) * half_rows]
            turned = one * cosine - pltpu.roll(one, LANES // 2, 1) * sine
            dq_ref[0, 0, :, g * LANES : (g + 1) * LANES] = turned.astype(bf16)

    for one in range(length // chunk):
        for two in range(one, length // chunk):
            seen = range(one, two + 1)
            pl.when((low == one) & (high == two))(functools.partial(run, seen))


def attention_specs(half_rows, length):
    wide = GROUP * LANES
    query = pl.BlockSpec((1, 1, half_rows, wide), lambda s, e, j, *_: (s, j, 0, e))
    keys = pl.BlockSpec((1, length, LANES), lambda s, e, j, *_: (s, 0, 2 * e))
    values = pl.BlockSpec((1, length, LANES), lambda s, e, j, *_: (s, 0, 2 * e + 1))
    keys_t = pl.BlockSpec((1, LANES, length), lambda s, e, j, *_: (s, 2 * e, 0))
    values_t = pl.BlockSpec((1, LANES, length), lambda s, e, j, *_: (s, 2 * e + 1, 0))
    seg_q = pl.BlockSpec((1, 1, 1, half_rows), lambda s, e, j, *_: (s, j, 0, 0))
    seg_k = pl.BlockSpec((1, length, 1), lambda s, e, j, *_: (s, 0, 0))
    lse = pl.BlockSpec((1, 1, 1, 1, GROUP * half_rows), lambda s, e, j, *_: (s, j, e, 0, 0))
    table = pl.BlockSpec((1, half_rows, LANES), lambda s, e, j, *_: (j, 0, 0))
    summed = pl.BlockSpec((1, length, LANES), lambda s, e, j, *_: (s, 0, e))
    return query, keys, values, keys_t, values_t, seg_q, seg_k, lse, table, summed


def attend(bases, lows, queries, kv, kv_t, seg_q, seg_k):
    seqs, subs, half_rows, wide = queries.shape
    length = kv.shape[1]
    chunk = 256
    query, keys, _, _, values_t, sq, sk, lse, _, _ = attention_specs(half_rows, length)
    return pl.pallas_call(
        functools.partial(forward_kernel, chunk),
        grid_spec=pltpu.PrefetchScalarGridSpec(
            num_scalar_prefetch=2,
            grid=(seqs, 2, subs),
            in_specs=[query, keys, values_t, sq, sk],
            out_specs=[query, lse],
            scratch_shapes=[pltpu.VMEM((length, GROUP * half_rows), f32)],
        ),
        out_shape=[
            jax.ShapeDtypeStruct(queries.shape, bf16),
            jax.ShapeDtypeStruct((seqs, subs, 2, 1, GROUP * half_rows), f32),
        ],
        compiler_params=pltpu.CompilerParams(vmem_limit_bytes=48 << 20),
        cost_estimate=lasting(16),
    )(bases, lows, queries, kv, kv_t, seg_q, seg_k)


def attend_back(bases, lows, queries, kv, kv_t, seg_q, seg_k, grads, lse_in, cosine, sine):
    seqs, subs, half_rows, wide = queries.shape
    length = kv.shape[1]
    chunk = 256
    query, keys, values, keys_t, _, sq, sk, lse, table, summed = attention_specs(half_rows, length)
    return pl.pallas_call(
        functools.partial(backward_kernel, chunk),
        grid_spec=pltpu.PrefetchScalarGridSpec(
            num_scalar_prefetch=2,
            grid=(seqs, 2, subs),
            in_specs=[query, keys, keys_t, values, sq, sk, query, lse, table, table],
            out_specs=[query, summed, summed],
            scratch_shapes=[pltpu.VMEM((length, GROUP * half_rows), f32)] * 2,
        ),
        out_shape=[
            jax.ShapeDtypeStruct(queries.shape, bf16),
            jax.ShapeDtypeStruct((seqs, length, 2 * LANES), f32),
            jax.ShapeDtypeStruct((seqs, length, 2 * LANES), f32),
        ],
        compiler_params=pltpu.CompilerParams(vmem_limit_bytes=48 << 20),
        cost_estimate=lasting(24),
    )(bases, lows, queries, kv, kv_t, kv, seg_q, seg_k, grads, lse_in, cosine, sine)


def project_kernel(order_ref, *refs):
    blocks, (w_own, w_other, gain_ref, cos_ref, sin_ref, norm_ref, q_ref, kv_ref) = refs[:4], refs[4:]

    def run(x_ref):
        values = x_ref[...].astype(f32)
        normed = (values * rms_scale(values) * gain_ref[...]).astype(bf16)
        norm_ref[...] = normed
        cosine, sine = cos_ref[0], sin_ref[0]
        for e, w_ref in enumerate((w_own, w_other)):
            product = dot_nn(normed, w_ref[...])
            for g in range(GROUP + 1):
                one = product[:, g * LANES : (g + 1) * LANES]
                turned = (one * cosine + pltpu.roll(one, LANES // 2, 1) * sine).astype(bf16)
                if g < GROUP:
                    at = e * GROUP + g
                    q_ref[:, at * LANES : (at + 1) * LANES] = turned
                else:
                    kv_ref[:, 2 * e * LANES : (2 * e + 1) * LANES] = turned
            one = product[:, (GROUP + 1) * LANES :]
            kv_ref[:, (2 * e + 1) * LANES : (2 * e + 2) * LANES] = one.astype(bf16)

    for i, ref in enumerate(blocks):
        pl.when(pl.program_id(0) == i)(functools.partial(run, ref))


def project(order, blocks, weights, gain, cosine, sine):
    rows, width = blocks[0].shape
    table = pl.BlockSpec((1, rows, LANES), lambda i, order: (order[i] % 2, 0, 0))
    columns = (width, 2 * GROUP * LANES, 4 * LANES)
    return pl.pallas_call(
        project_kernel,
        grid_spec=pltpu.PrefetchScalarGridSpec(
            num_scalar_prefetch=1,
            grid=(4,),
            in_specs=[whole(a) for a in (*blocks, *weights, gain)] + [table, table],
            out_specs=[
                pl.BlockSpec((rows, cols), lambda i, order: (order[i], 0)) for cols in columns
            ],
        ),
        out_shape=[jax.ShapeDtypeStruct((4 * rows, cols), bf16) for cols in columns],
        compiler_params=pltpu.CompilerParams(vmem_limit_bytes=56 << 20),
        cost_estimate=lasting(18),
    )(order, *blocks, *weights, gain, cosine, sine)


def weight_kernel(count, packed, added, order_ref, *refs):
    xs, ds, rest = refs[: count[0]], refs[count[0] : sum(count)], list(refs[sum(count) : -1])
    total = None
    each = count[0] // count[1]
    for i, x_ref in enumerate(xs):
        rows = x_ref.shape[0]
        at = pl.ds(pl.multiple_of(order_ref[i % each] * rows, rows), rows)
        part = dot_tn(x_ref[...], ds[i // each][at])
        total = part if total is None else total + part
    if packed:
        total = dot_nt(total.astype(bf16), rest.pop(0)[...])
    if added:
        total = total + rest.pop(0)[...].astype(f32)
    refs[-1][...] = total.astype(bf16)


def weight_grad(order, xs, ds, half, place=None, more=None, tile=256):
    count = (len(xs), len(ds))
    width, cols = xs[0].shape[1], ds[0].shape[1] // 2
    places = [] if place is None else [place]
    out_cols = cols if place is None else place.shape[0]
    block = pl.BlockSpec((tile, out_cols), lambda i, _: (i, 0))
    adds = [] if more is None else [more]
    return pl.pallas_call(
        functools.partial(weight_kernel, count, bool(places), bool(adds)),
        grid_spec=pltpu.PrefetchScalarGridSpec(
            num_scalar_prefetch=1,
            grid=(width // tile,),
            in_specs=[pl.BlockSpec((x.shape[0], tile), lambda i, _: (0, i)) for x in xs]
            + [pl.BlockSpec((d.shape[0], cols), lambda i, _: (0, half)) for d in ds]
            + [whole(p) for p in places]
            + [block] * len(adds),
            out_specs=block,
        ),
        out_shape=jax.ShapeDtypeStruct((width, out_cols), bf16),
        compiler_params=pltpu.CompilerParams(vmem_limit_bytes=60 << 20),
        cost_estimate=dense(sum(d.shape[0] for d in ds), width, cols),
    )(order, *xs, *ds, *places, *adds)


PARAMS = pltpu.CompilerParams(vmem_limit_bytes=56 << 20)


def whole(a):
    return pl.BlockSpec(a.shape, lambda *_: (0,) * a.ndim)


def expand_kernel(*refs):
    blocks, (w_own, w_other, both_ref, act_ref) = refs[:4], refs[4:]
    half = pl.num_programs(0) // 2

    def run(w_ref):
        w = w_ref[...]
        for i, x_ref in enumerate(blocks):
            rows = x_ref.shape[0]
            at = slice(i * rows, (i + 1) * rows)
            both = dot_nn(x_ref[...], w)
            gate, up = both[:, :LANES], both[:, LANES:]
            both_ref[at] = both
            act_ref[at] = (gate * jax.nn.sigmoid(gate) * up).astype(bf16)

    pl.when(pl.program_id(0) < half)(lambda: run(w_own))
    pl.when(pl.program_id(0) >= half)(lambda: run(w_other))


def halves_spec(shape, axis, tiles):
    def place(at):
        return (0, at) if axis else (at, 0)

    return [
        pl.BlockSpec(shape, lambda j, *_: place(jnp.minimum(j, tiles - 1))),
        pl.BlockSpec(shape, lambda j, *_: place(jnp.maximum(j - tiles, 0))),
    ]


def expand(blocks, weights):
    rows, width = blocks[0].shape
    cols = 2 * weights[0].shape[1]
    tiles = cols // (4 * LANES)
    return pl.pallas_call(
        expand_kernel,
        grid=(2 * tiles,),
        in_specs=[whole(b) for b in blocks] + halves_spec((width, 2 * LANES), 1, tiles),
        out_specs=[
            pl.BlockSpec((4 * rows, 2 * LANES), lambda j: (0, j)),
            pl.BlockSpec((4 * rows, LANES), lambda j: (0, j)),
        ],
        out_shape=[
            jax.ShapeDtypeStruct((4 * rows, cols), f32),
            jax.ShapeDtypeStruct((4 * rows, cols // 2), bf16),
        ],
        compiler_params=PARAMS,
        cost_estimate=dense(4 * rows, width, cols),
    )(*blocks, *weights)


def expand_back_kernel(*refs):
    blocks, (both_ref, w_own, w_other, out_ref) = refs[:4], refs[4:]

    def run(g_ref):
        g = g_ref[...]
        for e, w_ref in enumerate((w_own, w_other)):
            d_act = dot_nn(g, w_ref[...])
            tiles = d_act.shape[1] // LANES
            for j in range(tiles):
                first = 2 * (e * tiles + j) * LANES
                gate = both_ref[:, first : first + LANES]
                up = both_ref[:, first + LANES : first + 2 * LANES]
                d = d_act[:, j * LANES : (j + 1) * LANES]
                sigma = jax.nn.sigmoid(gate)
                d_sigma = d * sigma
                d_gate = d_sigma * up * (1.0 + gate * (1.0 - sigma))
                out_ref[:, first : first + LANES] = d_gate.astype(bf16)
                out_ref[:, first + LANES : first + 2 * LANES] = (d_sigma * gate).astype(bf16)

    for i, ref in enumerate(blocks):
        pl.when(pl.program_id(0) == i)(functools.partial(run, ref))


def expand_back(blocks, both, weights):
    rows, width = blocks[0].shape
    cols = both.shape[1]
    return pl.pallas_call(
        expand_back_kernel,
        grid=(4,),
        in_specs=[whole(b) for b in blocks]
        + [pl.BlockSpec((rows, cols), lambda i: (i, 0))]
        + [whole(w) for w in weights],
        out_specs=pl.BlockSpec((rows, cols), lambda i: (i, 0)),
        out_shape=jax.ShapeDtypeStruct((4 * rows, cols), bf16),
        compiler_params=PARAMS,
        cost_estimate=dense(4 * rows, width, cols // 2),
    )(*blocks, both, *weights)


def shrink_kernel(order_ref, a_ref, own_ref, other_ref, *outs):
    depth = own_ref.shape[1]
    rows = outs[0].shape[0]
    own, other = own_ref[...], other_ref[...]
    for i, ref in enumerate(outs):
        at = pl.ds(pl.multiple_of(order_ref[i] * rows, rows), rows)
        out = dot_nt(a_ref[at, :depth], own) + dot_nt(a_ref[at, depth:], other)
        ref[...] = out.astype(bf16)


def shrink(order, a, weights, tile=256):
    rows, depth = a.shape
    cols = weights[0].shape[0]
    block = pl.BlockSpec((rows // 4, tile), lambda j, _: (0, j))
    return pl.pallas_call(
        shrink_kernel,
        grid_spec=pltpu.PrefetchScalarGridSpec(
            num_scalar_prefetch=1,
            grid=(cols // tile,),
            in_specs=[whole(a)] + [pl.BlockSpec((tile, depth // 2), lambda j, _: (j, 0))] * 2,
            out_specs=[block] * 4,
        ),
        out_shape=[jax.ShapeDtypeStruct((rows // 4, cols), bf16)] * 4,
        compiler_params=PARAMS,
        cost_estimate=dense(rows, depth, cols),
    )(order, a, *weights)


def grow_kernel(order_ref, *refs):
    blocks, (w_own, w_other, out_ref) = refs[:4], refs[4:]
    half = pl.num_programs(0) // 2

    def run(w_ref):
        w = w_ref[...]
        for i, x_ref in enumerate(blocks):
            rows = x_ref.shape[0]
            at = pl.ds(pl.multiple_of(order_ref[i] * rows, rows), rows)
            out_ref[at] = dot_nn(x_ref[...], w).astype(bf16)

    pl.when(pl.program_id(0) < half)(lambda: run(w_own))
    pl.when(pl.program_id(0) >= half)(lambda: run(w_other))


def grow(order, blocks, weights, tile=256):
    rows, depth = blocks[0].shape
    cols = 2 * weights[0].shape[1]
    tiles = cols // (2 * tile)
    return pl.pallas_call(
        grow_kernel,
        grid_spec=pltpu.PrefetchScalarGridSpec(
            num_scalar_prefetch=1,
            grid=(2 * tiles,),
            in_specs=[whole(b) for b in blocks] + halves_spec((depth, tile), 1, tiles),
            out_specs=pl.BlockSpec((4 * rows, tile), lambda j, _: (0, j)),
        ),
        out_shape=jax.ShapeDtypeStruct((4 * rows, cols), bf16),
        compiler_params=PARAMS,
        cost_estimate=dense(4 * rows, depth, cols),
    )(order, *blocks, *weights)


def by_rows(kernel, ins, outs, vectors=()):
    rows, width = outs[0].shape
    tile = rows // 2 if rows % 32 == 0 else rows
    specs, arrays = [whole(v) for v in vectors], list(vectors)
    for one in ins:
        if not isinstance(one, tuple) and one.ndim == 3:
            one = (one, 0)
        if isinstance(one, tuple):
            one, at = one
            specs.append(pl.BlockSpec((None, tile, width), lambda i, at=at: (at, i, 0)))
        else:
            specs.append(pl.BlockSpec((tile, width), lambda i: (i, 0)))
        arrays.append(one)
    return pl.pallas_call(
        kernel,
        grid=(rows // tile,),
        in_specs=specs,
        out_specs=[pl.BlockSpec((tile, width), lambda i: (i, 0))] * len(outs),
        out_shape=outs,
        compiler_params=PARAMS,
        cost_estimate=lasting(5.5),
    )(*arrays)


def wide_sum(refs):
    total = refs[0][...].astype(f32)
    for ref in refs[1:]:
        total = total + ref[...].astype(f32)
    return total


def norm_kernel(gain_ref, *refs):
    residual = wide_sum(refs[:-2])
    refs[-2][...] = residual
    refs[-1][...] = (residual * rms_scale(residual) * gain_ref[...]).astype(bf16)


def norm_back_kernel(count, gain_ref, g_ref, residual_ref, *refs):
    residual = residual_ref[...].astype(f32)
    scale = rms_scale(residual)
    hat = residual * scale
    d_hat = wide_sum(refs[:count]) * gain_ref[...]
    inner = jnp.mean(d_hat * hat, axis=-1, keepdims=True)
    out = g_ref[...].astype(f32) + scale * (d_hat - hat * inner)
    for ref in refs[count:]:
        ref[...] = out.astype(ref.dtype)


def sum_kernel(*refs):
    refs[-1][...] = wide_sum(refs[:-1]).astype(refs[-1].dtype)


def shaped(a, kind):
    return jax.ShapeDtypeStruct(a.shape, kind)


def finish_mlp_kernel(hidden, rep_ref, mine_ref, other_ref, wg_ref, wu_ref, *outs):
    gate_ref, up_ref, down_ref, sum_ref = outs
    t = pl.program_id(0)
    wide = gate_ref.shape[1]
    own = jnp.broadcast_to((t // INNER == rep_ref[0]).astype(f32), (1, LANES))
    total = None
    for j in range(wide // LANES):
        cut = slice(j * LANES, (j + 1) * LANES)
        keep = t * wide + j * LANES < hidden

        def taken(column):
            at = slice(column * LANES, (column + 1) * LANES)
            mine, other = mine_ref[0, :, at].astype(f32), other_ref[0, :, at].astype(f32)
            return jnp.where(own > 0.5, mine, other)

        gate, up = taken(2 * j), taken(2 * j + 1)
        gate_ref[:, cut] = gate
        up_ref[:, cut] = up
        down_ref[:, cut] = taken(2 * (wide // LANES) + j)
        part = wg_ref[:, cut].astype(f32) * gate + wu_ref[:, cut].astype(f32) * up
        part = jnp.where(jnp.broadcast_to(keep, part.shape), part, 0.0)
        total = part if total is None else total + part

    @pl.when(t == 0)
    def _():
        sum_ref[...] = jnp.zeros_like(sum_ref)

    sum_ref[...] += total


def finish_mlp(rep, mine, other, w_gate, w_up):
    _, rows, cols = mine.shape
    wide = cols // 3
    hidden = w_gate.shape[1]
    share = pl.BlockSpec((1, rows, cols), lambda t, *_: (t % INNER, 0, 0))
    block = pl.BlockSpec((rows, wide), lambda t, *_: (0, t))
    return pl.pallas_call(
        functools.partial(finish_mlp_kernel, hidden),
        grid_spec=pltpu.PrefetchScalarGridSpec(
            num_scalar_prefetch=1,
            grid=(SHARE,),
            in_specs=[share, share, block, block],
            out_specs=[block, block, block, pl.BlockSpec((rows, LANES), lambda t, *_: (0, 0))],
        ),
        out_shape=[jax.ShapeDtypeStruct((rows, hidden), f32)] * 3
        + [jax.ShapeDtypeStruct((rows, LANES), f32)],
        compiler_params=PARAMS,
        cost_estimate=lasting(13),
    )(rep, mine, other, w_gate, w_up)


def after(a, *others):
    return lax.optimization_barrier((a, *others))[0]


ORDER = (
    "Wa", "ca", "na", "xd0", "Wm", "cm", "xr0", "xz0", "tb", "wq", "P0", "xd1", "gd0", "wo", "nm",
    "xr1", "T0", "O0", "xz1", "P1", "Oa0", "gr0", "T1", "N0", "nd0", "gz0", "O1", "nr0", "gd1",
    "wg", "Oa1", "nz0", "E0", "N1", "wd", "B0", "nd1", "gr1", "X0", "nr1", "nz1", "E1", "gz1",
    "S0", "B1", "Xa0", "X1", "M0", "Wdo", "Xa1", "Wgo", "bd0", "M1", "bd1", "Wd", "Wg", "br1",
    "br0", "S1", "bz0", "A0", "Q0", "J0", "bz1", "Y0", "A1", "Sa1", "Woo", "Sa0", "out1", "Q1",
    "out0", "J1", "Ya0", "Y1", "F0", "Wo", "Wqo", "Ya1", "gpm", "gcm", "Wq", "F1", "gpo", "glm",
    "gco", "gpa", "gca", "glo", "gla", "jm", "jo", "ja",
)


class Place:
    def __init__(self):
        self.parts = lax.axis_size("dp")
        self.ctx = lax.axis_size("ctx")
        self.outer = self.ctx // INNER
        self.rep = lax.axis_index("rep")
        self.part = lax.axis_index("dp")
        self.at_ctx = lax.axis_index("ctx")
        self.inner = self.at_ctx % INNER
        self.hi = self.at_ctx // INNER
        self.core = self.inner % 2
        self.mid = self.inner // 2
        self.last = None
        self.order = jnp.where(self.core == 0, jnp.array([0, 2, 1, 3]), jnp.arange(4)).astype(jnp.int32)

    def run(self, work, *inputs, waits=()):
        held = () if self.last is None else (self.last,)
        inputs, _, _ = lax.optimization_barrier((inputs, held, tuple(waits)))
        out = work(*inputs)
        self.last = jax.tree.leaves(out)[-1]
        return out

    def gate(self, a):
        return a if self.last is None else after(a, self.last)

    def flip(self, a, bits):
        return lax.ppermute(a, "ctx", [(i, i ^ bits) for i in range(self.ctx)])

    def swap_rep(self, a):
        return lax.ppermute(a, "rep", [(0, 1), (1, 0)])

    def shift_hi(self, a, by):
        pairs = [(i, (i + INNER * by) % self.ctx) for i in range(self.ctx)]
        return lax.ppermute(a, "ctx", pairs)


    def gather_rows(self, piece):
        whole = lax.all_gather(piece, "dp", axis=0, tiled=True)
        if self.outer > 1:
            whole = jnp.concatenate(
                [whole] + [self.shift_hi(whole, j) for j in range(1, self.outer)], axis=0
            )
        return whole

    def reduce_rows(self, whole):
        whole = whole.reshape((self.outer, -1) + whole.shape[1:])
        mine = whole[0]
        for j in range(1, self.outer):
            mine = mine + self.shift_hi(whole[j], -j)
        return lax.psum_scatter(mine, "dp", scatter_dimension=0, tiled=True)

    def by_core(self, keep, got):
        return jnp.where(self.core == 0, jnp.stack([keep, got]), jnp.stack([got, keep]))

    def by_mid(self, keep, got):
        return jnp.where(self.mid == 0, jnp.stack([keep, got]), jnp.stack([got, keep]))

    def pick(self, a, index, axis):
        return lax.dynamic_index_in_dim(a, index, axis, keepdims=False)

    def spread_core(self, parts):
        return self.flip(self.gate(self.pick(parts, 1 - self.core, 1)), 1)

    def spread_mid(self, parts, got):
        both = self.run(
            lambda parts, got: self.by_core(self.pick(parts, self.core, 1), got), parts, got
        )
        return both, self.flip(self.gate(self.pick(both, 1 - self.mid, 1)), 2)

    def spread_close(self, both, got):
        return self.by_mid(self.pick(both, self.mid, 1), got)

    def join_shares(self, mine, other):
        low = jnp.where(self.rep == 0, mine, other)
        high = jnp.where(self.rep == 0, other, mine)
        return jnp.concatenate([low, high], axis=0)


    def to_own_order(self, a):
        if self.outer == 1:
            return a
        n, outer = self.parts, self.outer
        width = a.shape[-1] // (n * outer)
        cut = []
        for j in range(outer):
            for part in range(n):
                block = part * outer + (self.hi - j) % outer
                cut.append(lax.dynamic_slice_in_dim(a, block * width, width, a.ndim - 1))
        return jnp.concatenate(cut, axis=-1)

    def to_natural_order(self, a):
        if self.outer == 1:
            return a
        n, outer = self.parts, self.outer
        width = a.shape[-1] // (n * outer)
        cut = []
        for part in range(n):
            for hi in range(outer):
                block = ((self.hi - hi) % outer) * n + part
                cut.append(lax.dynamic_slice_in_dim(a, block * width, width, a.ndim - 1))
        return jnp.concatenate(cut, axis=-1)


    def by_core_pairs(self, rep_core):
        pairs = []
        for r in range(2):
            for i in range(self.ctx):
                to = (1 - r) * self.ctx + i if i % 2 == rep_core else r * self.ctx + (i ^ 2)
                pairs.append((r * self.ctx + i, to))
        return pairs

    def send_first(self, a):
        return lax.ppermute(a, ("rep", "ctx"), self.by_core_pairs(0))

    def send_second(self, a):
        return lax.ppermute(a, ("rep", "ctx"), self.by_core_pairs(1))

    def gather_start(self, a):
        a = self.gate(a)
        return self.send_first(a), self.send_second(a)

    def gather_relay(self, a, first, second):
        first, second = self.run(lambda *both: both, first, second)
        return a, first, second, self.send_second(first)

    def gather_close(self, *blocks):
        return self.run(lambda *blocks: blocks, *blocks)


    def reduce_start(self, here, to_first, to_second, far):
        return here, to_first, self.send_second(self.gate(far)), self.send_second(self.gate(to_second))

    def reduce_send(self, here, to_first, got, from_second):
        from_second, to_first = self.run(
            lambda second, *parts: (second, by_rows(sum_kernel, parts, [shaped(got, bf16)])[0]),
            from_second,
            to_first,
            got,
        )
        return here, from_second, self.send_first(to_first)

    def natural_rows(self, a):
        a = jnp.where(self.core == 0, a, jnp.flip(a, 0))
        a = jnp.where(self.mid == 0, a, jnp.flip(a, 2))
        return jnp.moveaxis(a, 0, 2)

    def relative_rows(self, a):
        a = jnp.moveaxis(a, 2, 0)
        a = jnp.where(self.core == 0, a, jnp.flip(a, 0))
        return jnp.where(self.mid == 0, a, jnp.flip(a, 2))


    def gather_outer(self, a, axis):
        if self.outer == 1:
            return a
        shape = a.shape[:axis] + (self.outer,) + a.shape[axis:]
        got = jnp.zeros(shape, a.dtype)
        for j in range(self.outer):
            one = self.shift_hi(a, j) if j else a
            got = lax.dynamic_update_index_in_dim(got, one, (self.hi - j) % self.outer, axis)
        return got.reshape(a.shape[:axis] + (-1,) + a.shape[axis + 1 :])

    def reduce_outer(self, a, axis):
        if self.outer == 1:
            return a
        a = a.reshape(a.shape[:axis] + (self.outer, -1) + a.shape[axis + 1 :]).astype(bf16)
        total = None
        for j in range(self.outer):
            one = lax.dynamic_index_in_dim(a, (self.hi + j) % self.outer, axis, keepdims=False)
            one = self.shift_hi(one, j) if j else one
            total = one.astype(f32) if total is None else total + one.astype(f32)
        return total


def place_matrix(shape, pairs):
    row = lax.broadcasted_iota(jnp.int32, shape, 0)
    col = lax.broadcasted_iota(jnp.int32, shape, 1)
    hit = jnp.zeros(shape, jnp.bool_)
    for at_row, at_col, width in pairs:
        hit |= (row - at_row == col - at_col) & (row >= at_row) & (row < at_row + width)
    return hit.astype(bf16)


def head_halves(row, col):
    return [(row + i * HALF, col + i * (LANES // 2), HALF) for i in range(2)]


def half_of(w, rep):
    cols = w.shape[1] // 2
    return lax.dynamic_slice_in_dim(w, rep * cols, cols, 1)


def join_columns(by_share):
    return jnp.concatenate(list(by_share), axis=1)


def half_even(w, rep, wide):
    w = jnp.pad(w, ((0, 0), (0, SHARE * wide - w.shape[1])))
    return lax.dynamic_slice_in_dim(w, rep * INNER * wide, INNER * wide, 1)


def alternate(gate, up):
    tiles = gate.shape[1] // LANES
    cut = [one[:, j * LANES : (j + 1) * LANES] for j in range(tiles) for one in (gate, up)]
    return jnp.concatenate(cut, axis=1)


def by_position(a, axis, half_rows):
    lead = a.shape[:axis]
    a = a.reshape(lead + (-1, 2, half_rows) + a.shape[axis + 1 :])
    early = lax.index_in_dim(a, 0, axis + 1, keepdims=False)
    late = jnp.flip(lax.index_in_dim(a, 1, axis + 1, keepdims=False), axis)
    both = jnp.concatenate([early, late], axis=axis)
    return both.reshape(lead + (-1,) + both.shape[axis + 2 :])


def by_storage(a, axis, half_rows):
    lead = a.shape[:axis]
    a = a.reshape(lead + (2, -1, half_rows) + a.shape[axis + 1 :])
    early = lax.index_in_dim(a, 0, axis, keepdims=False)
    late = jnp.flip(lax.index_in_dim(a, 1, axis, keepdims=False), axis)
    both = jnp.stack([early, late], axis=axis + 1)
    return both.reshape(lead + (-1,) + both.shape[axis + 3 :])


def body(
    tokens,
    cotangent,
    segments,
    attn_gain,
    w_query,
    w_key,
    w_value,
    w_out,
    mlp_gain,
    w_gate,
    w_up,
    w_down,
):
    at = Place()
    micro_count, local_batch, rows, model_width = tokens.shape
    streams = micro_count * local_batch
    seq_length = rows * at.ctx
    half_rows = rows // 2
    own_rows = w_query.shape[0]
    hidden = w_gate.shape[1]
    wide = round_up(-(-hidden // SHARE), LANES)
    heads_wide = GROUP * LANES

    x_own = [at.to_own_order(one) for one in tokens.reshape(streams, rows, model_width)]
    g_own = [at.to_own_order(one) for one in cotangent.reshape(streams, rows, model_width)]
    every = range(streams)
    qkv_wide = heads_wide + 2 * LANES
    q_cols, k_cols = GROUP * HEAD_DIM, HEAD_DIM
    qkv_cols = round_up(q_cols + 2 * k_cols + 2, LANES)
    o_cols = round_up(q_cols, LANES)
    qkv_place = place_matrix(
        (qkv_cols, qkv_wide),
        [
            pair
            for g in range(GROUP + 1)
            for pair in head_halves(g * HEAD_DIM, g * LANES)
        ]
        + [(q_cols + k_cols, heads_wide + LANES, HEAD_DIM)],
    )
    o_place = place_matrix(
        (o_cols, heads_wide), [(g * HEAD_DIM, g * LANES, HEAD_DIM) for g in range(GROUP)]
    )
    gain_place = place_matrix((8, qkv_cols), [(0, q_cols + 2 * k_cols, 2)])

    def attn_shares(w_query, w_key, w_value, w_out, attn_gain, mlp_gain):
        both = jnp.stack([attn_gain, mlp_gain], axis=1)
        gap = jnp.zeros((own_rows, qkv_cols - q_cols - 2 * k_cols - 2), bf16)
        gap_o = jnp.zeros((own_rows, o_cols - q_cols), bf16)
        w_query, w_key, w_value, w_out = (
            half_of(w, at.rep) for w in (w_query, w_key, w_value, w_out)
        )
        shares = [
            jnp.concatenate(
                [
                    w_query[:, i * q_cols : (i + 1) * q_cols],
                    w_key[:, i * k_cols : (i + 1) * k_cols],
                    w_value[:, i * k_cols : (i + 1) * k_cols],
                    both,
                    gap,
                    w_out[:, i * q_cols : (i + 1) * q_cols],
                    gap_o,
                ],
                axis=1,
            )
            for i in range(INNER)
        ]
        return jnp.stack(shares).reshape(2, 2, own_rows, -1)

    def mlp_shares(*ws):
        gate, up, down = (half_even(w, at.rep, wide) for w in ws)
        shares = []
        for i in range(INNER):
            cut = slice(i * wide, (i + 1) * wide)
            shares.append(
                jnp.concatenate([alternate(gate[:, cut], up[:, cut]), down[:, cut]], axis=1)
            )
        return jnp.stack(shares).reshape(2, 2, own_rows, -1)

    positions = true_positions(seq_length, at.ctx)
    rel_pos = jnp.stack(
        [
            lax.dynamic_slice_in_dim(positions, (at.at_ctx ^ (2 * m)) * rows, rows)
            for m in range(2)
        ]
    )
    bases = rel_pos.reshape(-1, half_rows)[:, 0]
    frequency = rope_base ** (-2.0 * jnp.arange(HALF, dtype=f32) / HEAD_DIM)
    angles = rel_pos.reshape(2, rows, 1).astype(f32) * frequency
    gap = jnp.zeros((2, rows, LANES // 2 - HALF), f32)
    cos_half, sin_half = jnp.cos(angles), jnp.sin(angles)
    cosine = jnp.concatenate([cos_half, gap, cos_half, gap], axis=2)
    sine = jnp.concatenate([-sin_half, gap, sin_half, gap], axis=2)
    own_segments = segments.reshape(streams, seq_length)
    all_segments = jnp.stack([own_segments, at.swap_rep(own_segments)], axis=1)
    seg_k = by_position(all_segments, 2, half_rows)[..., None]
    seg_q = jnp.stack(
        [
            lax.dynamic_slice_in_dim(all_segments, (at.at_ctx ^ (2 * m)) * rows, rows, 2)
            for m in range(2)
        ],
        axis=2,
    ).reshape(streams, 2, -1, 1, half_rows)

    cosine_sub = cosine.reshape(-1, half_rows, LANES)
    sine_sub = sine.reshape(-1, half_rows, LANES)
    lowest = jnp.min(seg_q, axis=(3, 4))
    lows = jnp.sum(seg_k[:, :, None, :, 0] < lowest[..., None], axis=3, dtype=jnp.int32)
    lows = lows.reshape(streams, -1)
    tables = (bases, cosine, sine, cosine_sub, sine_sub, seg_q, seg_k, lows)

    def swap_shares(kv):
        half = kv.shape[-1] // 2
        return jnp.concatenate([kv[..., half:], kv[..., :half]], axis=-1)

    def attention_part(queries, kv, kv_got, bases, lows, seg_q, seg_k):
        queries = queries.reshape(2, 4, half_rows, -1)
        kv = jnp.stack([kv, swap_shares(kv_got)]).reshape(2, 2, 2, rows, -1)
        kv = at.gather_outer(at.natural_rows(kv).reshape(2, INNER * rows, -1), 1)
        kv = by_position(kv, 1, half_rows)
        kv_t = kv.transpose(0, 2, 1)
        attended, lse = attend(bases, lows, queries, kv, kv_t, seg_q, seg_k)
        return queries, kv, kv_t, lse, attended.reshape(4 * rows, -1)

    def attention_back(
        d_attended, queries, kv, kv_t, lse, bases, lows, cos_sub, sin_sub, seg_q, seg_k
    ):
        dq, dk, dv = attend_back(
            bases,
            lows,
            queries,
            kv,
            kv_t,
            seg_q,
            seg_k,
            d_attended.reshape(queries.shape),
            lse,
            cos_sub,
            sin_sub,
        )
        parts = [d[..., e * LANES : (e + 1) * LANES] for e in range(2) for d in (dk, dv)]
        d_kv = jnp.concatenate(parts, axis=2)
        d_kv = at.reduce_outer(by_storage(d_kv, 1, half_rows), 1)
        d_kv = at.relative_rows(d_kv.reshape(2, 2, 2, rows, -1)).reshape(2, 4 * rows, -1)
        return dq.reshape(4 * rows, -1), d_kv[0], swap_shares(d_kv[1]).astype(bf16)

    def attention_join(dq, d_kv, got, cosine, sine):
        d_kv = d_kv + got.astype(f32)
        cosine, sine = (t.reshape(1, 2 * rows, LANES) for t in (cosine, sine))
        parts = []
        for e in range(2):
            dk = d_kv[:, 2 * e * LANES : (2 * e + 1) * LANES].reshape(2, 2 * rows, LANES)
            dk = dk * cosine - jnp.roll(dk, LANES // 2, axis=2) * sine
            parts.append(dq[:, e * heads_wide : (e + 1) * heads_wide])
            parts.append(dk.reshape(4 * rows, LANES).astype(bf16))
            parts.append(d_kv[:, (2 * e + 1) * LANES : (2 * e + 2) * LANES].astype(bf16))
        return jnp.concatenate(parts, axis=1)

    def second_norm(x, gain, *parts):
        return by_rows(norm_kernel, [x, *parts], [shaped(x, f32), shaped(x, bf16)], [gain])

    def second_norm_back(g, residual, gain, *parts):
        return by_rows(
            functools.partial(norm_back_kernel, len(parts)),
            [g, residual, *parts],
            [shaped(g, f32), shaped(g, bf16)],
            [gain],
        )

    def first_norm_back(x, d_residual, gain, *parts):
        return by_rows(
            functools.partial(norm_back_kernel, len(parts)),
            [d_residual, x, *parts],
            [shaped(x, f32)],
            [gain],
        )[0]

    def add_up(*parts):
        return by_rows(sum_kernel, parts, [shaped(parts[0], bf16)])[0]

    def expand_weights(w, gain_place, qkv_place):
        return dot_nt(gain_place, w), dot_nn(w, qkv_place, bf16)

    def grad_parts(*parts):
        return jnp.concatenate(parts, axis=1).reshape(2, 2, own_rows, -1)

    def close_rows(*cuts):
        def work(both, got):
            whole_rows = at.spread_close(both, got).reshape(INNER * own_rows, -1)
            return [whole_rows[:, a:b] for a, b in cuts]

        return work

    def close_shares(both, got):
        return at.spread_close(both, got).reshape(INNER, own_rows, -1)

    v = {}
    task = {}

    def put(name, work):
        task[name] = lambda: v.__setitem__(name, work())

    def gather_tasks(p, i, source):
        put(p + "d" + i, lambda: at.gather_start(source()))
        put(p + "r" + i, lambda: at.gather_relay(source(), *v[p + "d" + i]))
        put(p + "z" + i, lambda: at.gather_close(*v[p + "r" + i]))

    def reduce_tasks(p, i, order, left, right):
        put(p + i, lambda: at.reduce_start(*at.run(shrink, order, left(), right())))
        put(p + "a" + i, lambda: at.reduce_send(*v[p + i]))

    def grad_tasks(name, order, lefts, rights, place=None):
        def grad(half, *more):
            xs, ds = lefts(), rights()
            count = len(xs) + len(ds)
            return at.run(
                lambda order, *parts: weight_grad(
                    order, parts[: len(xs)], parts[len(xs) : count], half, place, *parts[count:]
                ),
                order,
                *xs,
                *ds,
                *more,
            )

        put(name + "o", lambda: at.flip(grad(1), 1))
        put(name, lambda: at.reduce_rows(grad(0, v[name + "o"])))

    def start_exchange(work, *parts):
        whole_parts = at.run(work, *parts)
        return whole_parts, at.spread_core(whole_parts)

    def project_task(i):
        normed, queries, kv = at.run(project, at.order, v[f"xz{i}"], v["wq"], v["gain"][0], *v["tb"][1:3])
        return normed, queries, kv, at.flip(kv, 1)

    def back_task(i):
        dq, d_kv, sent = at.run(
            attention_back,
            v[f"A{i}"],
            *v[f"T{i}"][:4],
            v["tb"][0],
            v["tb"][7][i],
            *v["tb"][3:5],
            v["tb"][5][i],
            v["tb"][6][i],
        )
        return dq, d_kv, at.flip(sent, 1)

    as_is = jnp.arange(4, dtype=jnp.int32)
    every = range(streams)
    for i in every:
        one = str(i)
        gather_tasks("x", one, lambda i=i: x_own[i])
        gather_tasks("g", one, lambda i=i: g_own[i])
        gather_tasks("n", one, lambda i=i: v[f"N{i}"][1])
        gather_tasks("b", one, lambda i=i: v[f"M{i}"][1])
        put(f"P{i}", lambda i=i: project_task(i))
        put(
            f"T{i}",
            lambda i=i: at.run(
                attention_part, *v[f"P{i}"][1:], v["tb"][0], v["tb"][7][i], v["tb"][5][i], v["tb"][6][i]
            ),
        )
        reduce_tasks("O", one, at.order, lambda i=i: v[f"T{i}"][4], lambda: v["wo"])
        put(f"N{i}", lambda i=i: at.run(second_norm, x_own[i], v["gain"][1], *v[f"Oa{i}"]))
        put(f"E{i}", lambda i=i: at.run(expand, v[f"nz{i}"], v["wg"]))
        reduce_tasks("S", one, as_is, lambda i=i: v[f"E{i}"][1], lambda: v["wd"])
        put(f"out{i}", lambda i=i: at.run(add_up, v[f"N{i}"][0], *v[f"Sa{i}"]))
        put(f"B{i}", lambda i=i: at.run(expand_back, v[f"gz{i}"], v[f"E{i}"][0], v["wd"]))
        reduce_tasks("X", one, as_is, lambda i=i: v[f"B{i}"], lambda: v["wg"])
        put(
            f"M{i}",
            lambda i=i: at.run(
                second_norm_back, g_own[i], v[f"N{i}"][0], v["gain"][1], *v[f"Xa{i}"]
            ),
        )
        put(f"A{i}", lambda i=i: at.run(grow, at.order, v[f"bz{i}"], v["wo"]))
        put(f"Q{i}", lambda i=i: back_task(i))
        put(f"J{i}", lambda i=i: at.run(attention_join, *v[f"Q{i}"], *v["tb"][1:3]))
        reduce_tasks("Y", one, at.order, lambda i=i: v[f"J{i}"], lambda: v["wq"])
        put(
            f"F{i}",
            lambda i=i: at.run(
                first_norm_back, x_own[i], v[f"M{i}"][0], v["gain"][0], *v[f"Ya{i}"]
            ),
        )
    put("tb", lambda: at.run(lambda *parts: parts, *tables))
    put(
        "Wa",
        lambda: start_exchange(
            attn_shares, w_query, w_key, w_value, w_out, attn_gain, mlp_gain
        ),
    )
    put("ca", lambda: at.spread_mid(*v["Wa"]))
    put(
        "na",
        lambda: [
            at.gather_rows(one)
            for one in at.run(
                close_rows((0, qkv_cols), (qkv_cols, qkv_cols + o_cols)), *v["ca"]
            )
        ],
    )
    put("Wm", lambda: start_exchange(mlp_shares, w_gate, w_up, w_down))
    put("cm", lambda: at.spread_mid(*v["Wm"]))
    put(
        "nm",
        lambda: [
            at.gather_rows(one)
            for one in at.run(close_rows((0, 2 * wide), (2 * wide, 3 * wide)), *v["cm"])
        ],
    )

    def expanded_weights():
        gains, w = at.run(expand_weights, v["na"][0], gain_place, qkv_place)
        v["gain"] = (gains[0:1], gains[1:2])
        return w, at.flip(w, 1)

    def expanded_out():
        w = at.run(lambda w, place: dot_nn(w, place, bf16), v["na"][1], o_place)
        return w, at.flip(w, 1)

    put("wq", expanded_weights)
    put("wo", expanded_out)
    put("wg", lambda: (v["nm"][0], at.flip(at.gate(v["nm"][0]), 1)))
    put("wd", lambda: (v["nm"][1], at.flip(at.gate(v["nm"][1]), 1)))

    def over_blocks(p):
        return lambda: [one for i in every for one in v[f"{p}z{i}"]]

    grad_tasks("Wd", as_is, over_blocks("g"), lambda: [v[f"E{i}"][1] for i in every])
    grad_tasks("Wg", as_is, over_blocks("n"), lambda: [v[f"B{i}"] for i in every])
    grad_tasks(
        "Wo", at.order, over_blocks("b"), lambda: [v[f"T{i}"][4] for i in every], o_place
    )
    grad_tasks(
        "Wq",
        as_is,
        lambda: [v[f"P{i}"][0] for i in every],
        lambda: [v[f"J{i}"] for i in every],
        qkv_place,
    )
    put("gpm", lambda: start_exchange(grad_parts, v["Wg"], v["Wd"]))
    put("gcm", lambda: at.spread_mid(*v["gpm"]))

    def swapped(both, got):
        mine = at.run(close_shares, both, got)
        return mine, at.swap_rep(mine)

    put("glm", lambda: swapped(*v["gcm"]))
    put("gpa", lambda: start_exchange(grad_parts, v["Wq"]))
    put("gca", lambda: at.spread_mid(*v["gpa"]))
    put("gla", lambda: swapped(*v["gca"]))
    put("gpo", lambda: start_exchange(grad_parts, v["Wo"]))
    put("gco", lambda: at.spread_mid(*v["gpo"]))
    put("glo", lambda: swapped(*v["gco"]))
    rep_number = at.rep.astype(jnp.int32).reshape(1)
    put("jm", lambda: at.run(finish_mlp, rep_number, *v["glm"], w_gate, w_up))

    def grad_columns(*cuts):
        def work(mine, other):
            shares = at.join_shares(mine, other)
            return [join_columns(shares[..., a:b]).astype(f32) for a, b in zip(cuts, cuts[1:])]

        return work

    ends = (0, q_cols, q_cols + k_cols, q_cols + 2 * k_cols)
    put("ja", lambda: at.run(grad_columns(*ends), *v["gla"]))
    put("jo", lambda: at.run(grad_columns(0, q_cols), *v["glo"]))
    for name in ORDER:
        task[name]()
    outputs = [at.to_natural_order(v[f"out{i}"]) for i in every]
    input_grads = [at.to_natural_order(v[f"F{i}"]) for i in every]
    gate_grad, up_grad, down_grad, mlp_sums = v["jm"]
    query_grad, key_grad, value_grad = v["ja"]
    (out_grad,) = v["jo"]

    def along(w, grad):
        return jnp.sum(w.astype(f32) * grad, axis=1)

    attn_gain_grad = (
        along(w_query, query_grad) + along(w_key, key_grad) + along(w_value, value_grad)
    ) / attn_gain.astype(f32)
    mlp_gain_grad = jnp.sum(mlp_sums, axis=1) / mlp_gain.astype(f32)

    return (
        jnp.stack(outputs).reshape(tokens.shape),
        jnp.stack(input_grads).reshape(tokens.shape),
        attn_gain_grad,
        query_grad,
        key_grad,
        value_grad,
        out_grad,
        mlp_gain_grad,
        gate_grad,
        up_grad,
        down_grad,
    )


def solution(mesh):
    sequence = P(None, ("rep", "dp"), "ctx", None)
    rows = P(("dp", "ctx"), None)
    vector = P(("dp", "ctx"))
    return jax.shard_map(
        body,
        mesh=mesh,
        in_specs=(
            sequence,
            sequence,
            P(None, ("rep", "dp"), None),
            vector,
            rows,
            rows,
            rows,
            rows,
            vector,
            rows,
            rows,
            rows,
        ),
        out_specs=(sequence, sequence, vector, rows, rows, rows, rows, vector, rows, rows, rows),
        check_vma=False,
    )
```
